128 devices in a mesh: segment: 4 (over z), dp: 32 (over x, y, core).
Axes of the slice: x: 4, y: 4, z: 4, core: 2. Of those that a mesh axis runs over, the one named last changes fastest.
Arguments:
- teacher_in: bfloat16 [64, 256, 1792], P('dp'), may hold values from -8 to 8
- teacher_qkv: bfloat16 [4, 1792, 2688], P('segment', 'dp'), may hold values from -2.5 to 2.5
- teacher_out: bfloat16 [4, 896, 1792], P('segment', 'dp'), may hold values from -0.1875 to 0.1875
- teacher_gain: float32 [4, 1792], P('segment'), may hold values from 0.25 to 1.75
- final_gain: float32 [1792], replicated, may hold values from 0.25 to 1.75
- projection: bfloat16 [1792, 1024], P('dp'), may hold values from -0.125 to 0.125
- bucket: int32 [64], replicated, may hold values from 0 to 2, as said below
- slot_image: int32 [64], replicated, may hold values from 0 to 63, as said below
- mask_list: int32 [64, 102], replicated, may hold values from 0 to 255, as said below
- student_in: bfloat16 [64, 256, 1024], P('dp'), may hold values from -6 to 6
- student_gain: float32 [1024], replicated, may hold values from 0.25 to 1.75
- w_gate: bfloat16 [1024, 1408], replicated, may hold values from -0.1875 to 0.1875
- w_up: bfloat16 [1024, 1408], replicated, may hold values from -0.1875 to 0.1875
- w_down: bfloat16 [1408, 1024], replicated, may hold values from -0.15625 to 0.15625
Outputs:
- grad_gate: float32 [1024, 1408], P(('segment', 'dp'))
- grad_up: float32 [1024, 1408], P(('segment', 'dp'))
- grad_down: float32 [1408, 1024], P(('segment', 'dp'))
The draws below stay inside these ranges and needn't reach their ends.
Inputs may be any that keep to these rules, and one draw needn't show every extreme that they name: An image of bucket b holds data in its first (16 - 2 b) * (16 - 2 b) patch slots; every bucket occurs. A permutation: student slot k holds teacher image slot_image[k]. `mask_list`: for slot k with v the valid patches of image slot_image[k], the first (2 v) // 5 entries are distinct patches below v.
All inputs are finite; a program needn't handle non-finite values.
Results may differ from the reference program's by a relative error of at most 0.019.
Values may be sent and summed in bfloat16 or wider, within the bound.
No kernel may reach another device: no remote copies, remote signals or barrier semaphores. Data moves between devices by JAX's collectives and lax.ppermute only.
A program may use at most 128 MiB of HBM per device.

```python
import math
import jax
import jax.numpy as jnp
from jax import lax

TD = 1792
HD = 112
TQ = 896
SD = 1024
SF = 1408
SIDE = 16
P_SIZE = 256
BUCKETS = 3
MASKN = 102
TLAYERS = 4
IMAGES = 64


def shared_layout(key):
    bucket_draw = jax.random.permutation(jax.random.fold_in(key, 101), IMAGES) % BUCKETS
    slot_draw = jax.random.permutation(jax.random.fold_in(key, 102), IMAGES)
    return (bucket_draw.astype(jnp.int32), slot_draw.astype(jnp.int32))


def draw_bucket(key, part):
    bucket_draw, slot_draw = shared_layout(key)
    return bucket_draw


def draw_slot_image(key, part):
    bucket_draw, slot_draw = shared_layout(key)
    return slot_draw


def draw_mask_list(key, part):
    bucket_draw, slot_draw = shared_layout(key)
    key = jax.random.fold_in(key, 3)
    side_len = SIDE - 2 * bucket_draw[slot_draw]
    valid_count = side_len * side_len
    positions = jnp.arange(P_SIZE, dtype=jnp.int32)
    ranking = jax.random.randint(key, (IMAGES, P_SIZE), 0, P_SIZE, dtype=jnp.int32) * P_SIZE + positions[None, :]
    ranking = jnp.where(positions[None, :] < valid_count[:, None], ranking, P_SIZE * P_SIZE + positions[None, :])
    ordered = jnp.argsort(ranking, axis=1, stable=True)
    return ordered[:, :MASKN].astype(jnp.int32)


def draw_teacher_qkv(key, part):
    key = jax.random.fold_in(key, 7)
    base_draw = jax.random.normal(jax.random.fold_in(key, 1), (TLAYERS, TD, 3 * TQ), jnp.float32)
    base_draw = jnp.clip(base_draw, -4.0, 4.0) / math.sqrt(TD)
    return base_draw.astype(jnp.bfloat16)


def draw_teacher_in(key, part):
    key = jax.random.fold_in(key, 5)
    drawn = jax.random.normal(jax.random.fold_in(key, 1), (IMAGES, P_SIZE, TD), jnp.float32)
    return jnp.clip(drawn, -5.0, 5.0).astype(jnp.bfloat16)


def spiked(values, key, source, target, shards_of, factor):
    owner, partner = [(jnp.arange(values.shape[position]) // (values.shape[position] // shards_of)).reshape([-1 if axis == position else 1 for axis in range(values.ndim)]) for position in (source, target)]
    chosen = jax.random.permutation(key, shards_of)[partner]
    strong = (owner == chosen) | (owner == (partner + shards_of // 2) % shards_of)
    return jnp.where(strong, factor * values, values)


def block_levels(key, shape, split, least, top_value):
    factor_of = 1.0
    for dim, blocks in split:
        heights = jax.random.uniform(jax.random.fold_in(jax.random.fold_in(key, 6), dim), (blocks,), jnp.float32, least / len(split), top_value / len(split))
        factor_of = factor_of * jnp.repeat(jnp.exp(heights), shape[dim] // blocks).reshape((-1,) + (1,) * (len(shape) - 1 - dim))
    return factor_of


def noise(stream_key, dims, deviation, limit, shards=(), kind=jnp.bfloat16):
    level = block_levels(stream_key, dims, shards, -0.22, 0.18) if shards else 1.0
    drawn = jax.random.normal(stream_key, dims, jnp.float32) * deviation * level
    return jnp.minimum(jnp.maximum(drawn, -limit), limit).astype(kind)


def bell_draw_with(stream_key, shape, spread, reach, cuts, heavy, kind=jnp.bfloat16):
    drawn = spread * jax.random.normal(stream_key, shape, jnp.float32)
    if cuts:
        drawn = drawn * block_levels(stream_key, shape, cuts, -0.22, 0.18)
    return jnp.clip(spiked(drawn, jax.random.fold_in(stream_key, 3), *heavy), -reach, reach).astype(kind)


def setup_inputs(seed: int = 0) -> dict:
    keys = jax.random.split(jax.random.key(seed), 15)
    teacher_in = draw_teacher_in(jax.random.fold_in(keys[14], 71), 0)
    teacher_qkv = draw_teacher_qkv(jax.random.fold_in(keys[14], 71), 0)
    teacher_out = noise(keys[2], (TLAYERS, TQ, TD), TQ ** -0.5, 0.1875, ((0, 4), (1, 32)))
    teacher_gain = jnp.clip(1.0 + 0.15 * jax.random.normal(keys[3], (TLAYERS, TD), jnp.float32), 0.25, 1.75)
    final_gain = jnp.clip(1.0 + 0.15 * jax.random.normal(keys[4], (TD,), jnp.float32), 0.25, 1.75)
    projection = noise(keys[5], (TD, SD), TD ** -0.5, 0.125, ((0, 32),))
    bucket = draw_bucket(jax.random.fold_in(keys[14], 71), 0)
    slot_image = draw_slot_image(jax.random.fold_in(keys[14], 71), 0)
    mask_list = draw_mask_list(jax.random.fold_in(keys[14], 71), 0)
    student_in = bell_draw_with(keys[9], (IMAGES, P_SIZE, SD), 1.0, 6.0, ((0, 32),), (0, 2, 32, 2.75))
    student_gain = jnp.clip(1.0 + 0.15 * jax.random.normal(keys[10], (SD,), jnp.float32), 0.25, 1.75)
    w_gate = noise(keys[11], (SD, SF), SD ** -0.5, 0.1875)
    w_up = noise(keys[12], (SD, SF), SD ** -0.5, 0.1875)
    w_down = noise(keys[13], (SF, SD), SF ** -0.5, 0.15625)
    return dict(teacher_in=teacher_in, teacher_qkv=teacher_qkv, teacher_out=teacher_out, teacher_gain=teacher_gain, final_gain=final_gain, projection=projection, bucket=bucket, slot_image=slot_image, mask_list=mask_list, student_in=student_in, student_gain=student_gain, w_gate=w_gate, w_up=w_up, w_down=w_down)


EPS = 1e-06
LOSS_SCALE = 4096.0

def normalize(values_in, gain):
    centred = values_in - lax.optimization_barrier(jnp.mean(values_in, axis=-1, keepdims=True))
    return centred * lax.rsqrt(lax.optimization_barrier(jnp.mean(centred * centred, axis=-1, keepdims=True)) + EPS) * gain

def valid_counts(bucket_ids):
    side_len = SIDE - 2 * bucket_ids
    return side_len * side_len

def teacher_layer(activation, valid_count, qkv_weight, out_weight, layer_gain):
    patches = activation.shape[0]
    features = out_weight.shape[0]
    head_count = features // HD
    hidden = normalize(activation.astype(jnp.float32), layer_gain).astype(jnp.bfloat16)
    qkv_rows = jnp.dot(hidden, qkv_weight, preferred_element_type=jnp.float32).astype(jnp.bfloat16)
    queries = qkv_rows[:, :features].reshape(patches, head_count, HD).astype(jnp.float32)
    key_rows = qkv_rows[:, features:2 * features].reshape(patches, head_count, HD).astype(jnp.float32)
    values = qkv_rows[:, 2 * features:].reshape(patches, head_count, HD).astype(jnp.float32)
    scores = jnp.einsum('qhd,khd->hqk', queries, key_rows) * HD ** (-0.5)
    live_keys = jnp.arange(patches, dtype=jnp.int32) < valid_count
    scores = jnp.where(live_keys[None, None, :], scores, -jnp.inf)
    row_max = lax.optimization_barrier(jnp.max(scores, axis=-1, keepdims=True))
    exp_scores = jnp.exp(scores - row_max)
    attn_probs = (exp_scores / lax.optimization_barrier(jnp.sum(exp_scores, axis=-1, keepdims=True))).astype(jnp.bfloat16)
    attended = jnp.einsum('hqk,khd->qhd', attn_probs.astype(jnp.float32), values)
    attended = attended.astype(jnp.bfloat16).reshape(patches, features)
    update = jnp.dot(attended, out_weight, preferred_element_type=jnp.float32)
    return (activation.astype(jnp.float32) + update).astype(jnp.bfloat16)

def row_weights(slot_bucket, mask_list, positions):
    mask_count = 2 * valid_counts(slot_bucket) // 5
    listed = jnp.arange(mask_list.shape[1], dtype=jnp.int32)[None, :] < mask_count[:, None]
    mask_hit = (mask_list[:, None, :] == positions[None, :, None]) & listed[:, None, :]
    inverse = 1.0 / mask_count.astype(jnp.float32)
    return jnp.where(jnp.any(mask_hit, axis=-1), inverse[:, None], jnp.zeros((), jnp.float32)).astype(jnp.float32)

def student_terms(own_rows, goal_in, weights, student_gain, w_gate, w_up, w_down):
    features = own_rows.shape[-1]
    flat_rows = own_rows.reshape(-1, features)
    normed = normalize(flat_rows.astype(jnp.float32), student_gain).astype(jnp.bfloat16)
    gate_act = jnp.dot(normed, w_gate, preferred_element_type=jnp.float32)
    up_act = jnp.dot(normed, w_up, preferred_element_type=jnp.float32)
    gate_sig = jax.nn.sigmoid(gate_act)
    hidden = (gate_act * gate_sig * up_act).astype(jnp.bfloat16)
    output = flat_rows.astype(jnp.float32) + jnp.dot(hidden, w_down, preferred_element_type=jnp.float32)
    goal_rows = goal_in.reshape(-1, features).astype(jnp.float32)
    out_scale = lax.rsqrt(lax.optimization_barrier(jnp.mean(output * output, axis=-1)) + EPS)
    goal_scale = lax.rsqrt(lax.optimization_barrier(jnp.mean(goal_rows * goal_rows, axis=-1)) + EPS)
    inner_prod = lax.optimization_barrier(jnp.sum(output * goal_rows, axis=-1))
    factor = -LOSS_SCALE * weights.reshape(-1) * goal_scale / features
    cubed = out_scale * out_scale * out_scale
    upstream = factor[:, None] * (out_scale[:, None] * goal_rows - (inner_prod * cubed / features)[:, None] * output)
    upstream = upstream.astype(jnp.bfloat16)
    grad_down = jnp.dot(hidden.T, upstream, preferred_element_type=jnp.float32)
    back_hidden = jnp.dot(upstream, w_down.T, preferred_element_type=jnp.float32)
    gate_grad = (back_hidden * up_act * gate_sig * (1.0 + gate_act * (1.0 - gate_sig))).astype(jnp.bfloat16)
    up_grad = (back_hidden * gate_act * gate_sig).astype(jnp.bfloat16)
    grad_gate = jnp.dot(normed.T, gate_grad, preferred_element_type=jnp.float32)
    grad_up = jnp.dot(normed.T, up_grad, preferred_element_type=jnp.float32)
    return (grad_gate, grad_up, grad_down)

def reference(teacher_in, teacher_qkv, teacher_out, teacher_gain, final_gain, projection, bucket, slot_image, mask_list, student_in, student_gain, w_gate, w_up, w_down):
    valid_all = valid_counts(bucket)

    def run_image(packed):
        activation, valid_count = packed
        for layer_idx in range(teacher_qkv.shape[0]):
            activation = teacher_layer(activation, valid_count, teacher_qkv[layer_idx], teacher_out[layer_idx], teacher_gain[layer_idx])
        features = normalize(activation.astype(jnp.float32), final_gain).astype(jnp.bfloat16)
        return jnp.dot(features, projection, preferred_element_type=jnp.float32).astype(jnp.bfloat16)
    targets = lax.map(run_image, (teacher_in, valid_all))
    slot_targets = targets[slot_image]
    slot_bucket = bucket[slot_image]
    positions = jnp.arange(P_SIZE, dtype=jnp.int32)
    weights = row_weights(slot_bucket, mask_list, positions)
    grad_gate, grad_up, grad_down = student_terms(student_in, slot_targets, weights, student_gain, w_gate, w_up, w_down)
    return (grad_gate, grad_up, grad_down)
```

```python
import functools

import jax
import jax.numpy as jnp
import numpy as np
from jax import lax
from jax.experimental import pallas as pl
from jax.experimental.pallas import tpu as pltpu
from jax.sharding import PartitionSpec as P

HD = 112
SIDE = 16
EPS = 1e-06
LOSS_SCALE = 4096.0

ROWS = 128
QCHUNK = 384
QSTEPS = 7
STEPS = 9
QUARTER = 28
BF = jnp.bfloat16
F32 = jnp.float32


def normalize(values_in, gain):
    centred = values_in - jnp.mean(values_in, axis=-1, keepdims=True)
    return centred * lax.rsqrt(jnp.mean(centred * centred, axis=-1, keepdims=True) + EPS) * gain


def valid_counts(bucket_ids):
    side_len = SIDE - 2 * bucket_ids
    return side_len * side_len


def spread_matrices():
    left = np.zeros((HD, 2 * HD), np.float32)
    right = np.zeros((HD, 2 * HD), np.float32)
    for feature in range(HD):
        owner, offset = divmod(feature, QUARTER)
        left[feature, 2 * QUARTER * owner + offset] = 1.0
        right[feature, 2 * QUARTER * owner + QUARTER + offset] = 1.0
    return jnp.asarray(left, BF), jnp.asarray(right, BF)


def dot(a, b):
    return jnp.dot(a, b, preferred_element_type=F32)


def sublayers_kernel(
    masked_last, valid_ref, x_ref, gain_ref, pick_ref, left_ref, right_ref, wq_ref, wo_ref,
    out_ref, x_scr, h_scr, qkv_scr, acc_scr,
):
    step = pl.program_id(0)
    layer = step // STEPS
    part = step % STEPS
    features = wo_ref.shape[-1]
    group_heads = features // HD // 2

    @pl.when(step == 0)
    def _():
        x_scr[...] = x_ref[...]

    @pl.when(part == 0)
    def _():
        gain = gain_ref[pl.ds(layer, 1), :]
        h_scr[...] = normalize(x_scr[...].astype(F32), gain).astype(BF)

    @pl.when(part < QSTEPS)
    def _():
        start = pl.multiple_of(part * QCHUNK, 128)
        qkv_scr[:, pl.ds(start, QCHUNK)] = dot(h_scr[...], wq_ref[0]).astype(BF)

    def attend(group, picked):
        rows = ROWS if picked else x_scr.shape[0]
        lefts, rights = [], []
        live = lax.broadcasted_iota(jnp.int32, (rows, x_scr.shape[0]), 1) < valid_ref[0]
        for head in range(group * group_heads, (group + 1) * group_heads):
            q = qkv_scr[:, head * HD : (head + 1) * HD]
            k = qkv_scr[:, features + head * HD : features + (head + 1) * HD]
            v = qkv_scr[:, 2 * features + head * HD : 2 * features + (head + 1) * HD]
            if picked:
                q = dot(pick_ref[...], q).astype(BF)
            scores = lax.dot_general(q, k, (((1,), (1,)), ((), ())), preferred_element_type=F32)
            scores = jnp.where(live, scores * HD ** (-0.5), -jnp.inf)
            weights = jnp.exp(scores - jnp.max(scores, axis=-1, keepdims=True))
            probs = (weights * (1.0 / jnp.sum(weights, axis=-1, keepdims=True))).astype(BF)
            lefts.append(dot(probs, dot(v, left_ref[...]).astype(BF)).astype(BF))
            rights.append(dot(probs, dot(v, right_ref[...]).astype(BF)).astype(BF))
        left = dot(jnp.concatenate(lefts, axis=1), wo_ref[0])
        right = dot(jnp.concatenate(rights, axis=1), wo_ref[0])
        return left, right

    def first_group(picked):
        left, right = attend(0, picked)
        rows = left.shape[0]
        acc_scr[:rows, :features] = left
        acc_scr[:rows, features:] = right

    def second_group(picked):
        left, right = attend(1, picked)
        rows = left.shape[0]
        before = dot(pick_ref[...], x_scr[...]) if picked else x_scr[...].astype(F32)
        left = (before[:, :features] + (acc_scr[:rows, :features] + left)).astype(BF)
        right = (before[:, features:] + (acc_scr[:rows, features:] + right)).astype(BF)
        if picked:
            out_ref[:, :features] = left
            out_ref[:, features:] = right
        else:
            x_scr[:, :features] = left
            x_scr[:, features:] = right
            if not masked_last:
                out_ref[:, :features] = left
                out_ref[:, features:] = right

    if masked_last:
        pl.when((part == QSTEPS) & (layer == 0))(functools.partial(first_group, False))
        pl.when((part == QSTEPS + 1) & (layer == 0))(functools.partial(second_group, False))
        pl.when((part == QSTEPS) & (layer == 1))(functools.partial(first_group, True))
        pl.when((part == QSTEPS + 1) & (layer == 1))(functools.partial(second_group, True))
    else:
        pl.when(part == QSTEPS)(functools.partial(first_group, False))
        pl.when(part == QSTEPS + 1)(functools.partial(second_group, False))


def sublayers(masked_last, valid, x, gains, pick, packed):
    patches, width = x.shape
    features = width // 2
    left, right = spread_matrices()
    out_rows = ROWS if masked_last else patches

    def qkv_block(step):
        layer, part = step // STEPS, step % STEPS
        ahead = part >= QSTEPS
        wrap = ahead & (layer == 0)
        return (
            jnp.where(wrap, 1, layer),
            0,
            jnp.where(wrap, 0, jnp.where(ahead, QSTEPS - 1, part)),
        )

    def out_block(step):
        layer, part = step // STEPS, step % STEPS
        return layer, jnp.where(part > QSTEPS, 1, 0), 3

    def whole(*shape):
        return pl.BlockSpec(shape, lambda step: (0,) * len(shape))

    return pl.pallas_call(
        functools.partial(sublayers_kernel, masked_last),
        grid=(2 * STEPS,),
        in_specs=[
            pl.BlockSpec(memory_space=pltpu.SMEM),
            whole(patches, width),
            whole(2, width),
            whole(ROWS, patches),
            whole(HD, 2 * HD),
            whole(HD, 2 * HD),
            pl.BlockSpec((1, width, QCHUNK), qkv_block),
            pl.BlockSpec((1, features, features), out_block),
        ],
        out_specs=whole(out_rows, width),
        out_shape=jax.ShapeDtypeStruct((out_rows, width), BF),
        scratch_shapes=[
            pltpu.VMEM((patches, width), BF),
            pltpu.VMEM((patches, width), BF),
            pltpu.VMEM((patches, 3 * features), BF),
            pltpu.VMEM((patches, width), F32),
        ],
        compiler_params=pltpu.CompilerParams(vmem_limit_bytes=40 * 1024 * 1024),
        cost_estimate=pl.CostEstimate(
            flops=14 * 10**9, bytes_accessed=27 * 10**6, transcendentals=10**6
        ),
        name="sublayers",
    )(valid, x, gains, pick, left, right, packed, packed)


def shards(
    teacher_in,
    teacher_qkv,
    teacher_out,
    teacher_gain,
    final_gain,
    projection,
    bucket,
    slot_image,
    mask_list,
    student_in,
    student_gain,
    w_gate,
    w_up,
    w_down,
):
    section = lax.axis_index("segment")
    column = lax.axis_index("dp")
    members = lax.axis_size("dp")
    images = bucket.shape[0]
    patches = teacher_in.shape[1]
    features = teacher_out.shape[2] // 2
    width = student_in.shape[-1]
    hidden_width = w_gate.shape[1]
    half = hidden_width // 4

    packed_own = jnp.concatenate(
        [
            teacher_qkv[0],
            jnp.concatenate([teacher_out[0, :, :features], teacher_out[0, :, features:]], axis=0),
        ],
        axis=1,
    )
    pair_groups = [list(range(0, 2 * members)), list(range(2 * members, 4 * members))]
    packed = lax.all_gather(
        packed_own, ("segment", "dp"), axis=0, tiled=True, axis_index_groups=pair_groups
    )
    packed = packed.reshape(2, members * packed_own.shape[0], packed_own.shape[1])
    other_gain = lax.ppermute(teacher_gain, "segment", [(0, 1), (1, 0), (2, 3), (3, 2)])
    upper = section % 2
    gains = jnp.where(
        upper == 0,
        jnp.concatenate([teacher_gain, other_gain], axis=0),
        jnp.concatenate([other_gain, teacher_gain], axis=0),
    )

    image_ids = jnp.arange(images, dtype=jnp.int32)
    positions = jnp.arange(patches, dtype=jnp.int32)
    slot_of = jnp.sum(
        jnp.where(slot_image[None, :] == image_ids[:, None], image_ids[None, :], 0), axis=1
    )
    listed = jnp.pad(mask_list, ((0, 0), (0, ROWS - mask_list.shape[1])))
    own_slots = lax.dynamic_slice_in_dim(listed, 2 * column, 2)
    own_pick = (own_slots[:, :, None] == positions[None, None, :]).astype(BF)
    chosen = jnp.einsum("srp,spf->srf", own_pick, student_in, preferred_element_type=F32).astype(BF)
    chosen = lax.all_to_all(chosen, "dp", split_axis=1, concat_axis=0, tiled=True)
    chosen = jnp.take(chosen, slot_of, axis=0)
    chosen = lax.all_to_all(chosen, "dp", split_axis=0, concat_axis=1, tiled=True)
    my_slots = lax.dynamic_slice_in_dim(slot_of, 2 * column, 2)
    my_lists = jnp.take(listed, my_slots, axis=0)
    my_valid = valid_counts(lax.dynamic_slice_in_dim(bucket, 2 * column, 2))
    my_count = 2 * my_valid // 5
    weights = jnp.where(
        jnp.arange(ROWS, dtype=jnp.int32)[None, :] < my_count[:, None],
        1.0 / my_count.astype(F32)[:, None],
        0.0,
    ).reshape(-1)

    flat_rows = chosen.reshape(-1, width)
    normed = normalize(flat_rows.astype(F32), student_gain).astype(BF)
    gate_act = dot(normed, w_gate)
    up_act = dot(normed, w_up)
    gate_sig = jax.nn.sigmoid(gate_act)
    hidden = (gate_act * gate_sig * up_act).astype(BF)
    output = flat_rows.astype(F32) + dot(hidden, w_down)
    out_scale = lax.rsqrt(jnp.mean(output * output, axis=-1) + EPS)
    gate_factor = up_act * gate_sig * (1.0 + gate_act * (1.0 - gate_sig))
    up_factor = gate_act * gate_sig
    normed_rows = lax.dynamic_slice_in_dim(normed, section * (width // 4), width // 4, 1).T
    down_rows = lax.dynamic_slice_in_dim(hidden, section * half, half, 1).T
    down_rows = down_rows.reshape(members, half // members, -1)
    down_top = down_rows[:, :8].reshape(8 * members, -1)
    down_rest = jnp.pad(down_rows[:, 8:], ((0, 0), (0, 16 - half // members), (0, 0)))
    down_rest = down_rest.reshape(8 * members, -1)

    which = jnp.where((section == 0) | (section == 3), 0, 1)
    image = lax.dynamic_index_in_dim(teacher_in, which, 0, keepdims=False)
    valid = lax.dynamic_slice_in_dim(my_valid, which, 1)
    my_list = lax.dynamic_index_in_dim(my_lists, which, 0, keepdims=False)
    pick = (my_list[:, None] == positions[None, :]).astype(BF)
    middle = sublayers(False, valid, image, gains, pick, packed)
    middle = lax.ppermute(middle, "segment", [(0, 3), (1, 2)])
    packed, projection = lax.optimization_barrier((packed, projection))
    proj_full = lax.all_gather(projection, "dp", axis=0, tiled=True)
    last = sublayers(True, valid, middle, gains, pick, packed)
    normed_last = normalize(last.astype(F32), final_gain).astype(BF)
    target = dot(normed_last, proj_full).astype(BF)

    swapped = lax.ppermute(target, "segment", [(2, 3), (3, 2)])
    near = lax.ppermute(target, "segment", [(3, 0), (2, 1)])
    far = lax.ppermute(target, "segment", [(3, 1), (2, 0)])
    upper_half = section >= 2
    one = jnp.where(upper_half, target, near)
    two = jnp.where(upper_half, swapped, far)
    goal = jnp.where(which == 0, jnp.stack([one, two]), jnp.stack([two, one]))

    goal_rows = goal.reshape(-1, width).astype(F32)
    goal_scale = lax.rsqrt(jnp.mean(goal_rows * goal_rows, axis=-1) + EPS)
    inner_prod = jnp.sum(output * goal_rows, axis=-1)
    factor = -LOSS_SCALE * weights * goal_scale / width
    cubed = out_scale * out_scale * out_scale
    upstream = factor[:, None] * (
        out_scale[:, None] * goal_rows - (inner_prod * cubed / width)[:, None] * output
    )
    upstream = upstream.astype(BF)
    back_hidden = lax.dot_general(
        upstream, w_down, (((1,), (1,)), ((), ())), preferred_element_type=F32
    )
    gate_grad = (back_hidden * gate_factor).astype(BF)
    up_grad = (back_hidden * up_factor).astype(BF)
    terms = jnp.concatenate(
        [
            dot(normed_rows, gate_grad).astype(BF),
            dot(normed_rows, up_grad).astype(BF),
            dot(down_top, upstream).astype(BF),
            dot(down_rest, upstream).astype(BF),
        ],
        axis=1,
    ).reshape(members, 8, -1)
    terms = lax.all_to_all(terms, "dp", split_axis=0, concat_axis=0, tiled=True)
    summed = jnp.sum(terms.astype(F32), axis=0)
    cut = 2 * hidden_width
    grad_down = jnp.concatenate(
        [summed[:, cut : cut + width], summed[: half // members - 8, cut + width :]], axis=0
    )
    return summed[:, :hidden_width], summed[:, hidden_width:cut], grad_down


def solution(mesh):
    in_specs = (
        P("dp", None, None),
        P("segment", "dp", None),
        P("segment", "dp", None),
        P("segment", None),
        P(),
        P("dp", None),
        P(),
        P(),
        P(),
        P("dp", None, None),
        P(),
        P(),
        P(),
        P(),
    )
    out_specs = (P(("segment", "dp"), None), P(("segment", "dp"), None), P(("segment", "dp"), None))
    return jax.shard_map(shards, mesh=mesh, in_specs=in_specs, out_specs=out_specs, check_vma=False)
```

```python
import functools

import jax
import jax.numpy as jnp
import numpy as np
from jax import lax
from jax.experimental import pallas as pl
from jax.experimental.pallas import tpu as pltpu
from jax.sharding import PartitionSpec as P

HD = 112
SIDE = 16
EPS = 1e-06
LOSS_SCALE = 4096.0

ROWS = 128
QCHUNK = 384
QSTEPS = 7
STEPS = 9
QUARTER = 28
BF = jnp.bfloat16
F32 = jnp.float32


def normalize(values_in, gain):
    centred = values_in - jnp.mean(values_in, axis=-1, keepdims=True)
    return centred * lax.rsqrt(jnp.mean(centred * centred, axis=-1, keepdims=True) + EPS) * gain


def valid_counts(bucket_ids):
    side_len = SIDE - 2 * bucket_ids
    return side_len * side_len


def spread_matrices():
    left = np.zeros((HD, 2 * HD), np.float32)
    right = np.zeros((HD, 2 * HD), np.float32)
    for feature in range(HD):
        owner, offset = divmod(feature, QUARTER)
        left[feature, 2 * QUARTER * owner + offset] = 1.0
        right[feature, 2 * QUARTER * owner + QUARTER + offset] = 1.0
    return jnp.asarray(left, BF), jnp.asarray(right, BF)


def dot(a, b):
    return jnp.dot(a, b, preferred_element_type=F32)


def sublayers_kernel(
    masked_last, valid_ref, x_ref, gain_ref, pick_ref, left_ref, right_ref, wq_ref, wo_ref,
    out_ref, x_scr, h_scr, qkv_scr, acc_scr,
):
    step = pl.program_id(0)
    layer = step // STEPS
    part = step % STEPS
    features = wo_ref.shape[-1]
    group_heads = features // HD // 2

    @pl.when(step == 0)
    def _():
        x_scr[...] = x_ref[...]

    @pl.when(part == 0)
    def _():
        gain = gain_ref[pl.ds(layer, 1), :]
        h_scr[...] = normalize(x_scr[...].astype(F32), gain).astype(BF)

    @pl.when(part < QSTEPS)
    def _():
        start = pl.multiple_of(part * QCHUNK, 128)
        qkv_scr[:, pl.ds(start, QCHUNK)] = dot(h_scr[...], wq_ref[...]).astype(BF)

    def attend(group, picked):
        rows = ROWS if picked else x_scr.shape[0]
        lefts, rights = [], []
        live = lax.broadcasted_iota(jnp.int32, (rows, x_scr.shape[0]), 1) < valid_ref[0]
        for head in range(group * group_heads, (group + 1) * group_heads):
            q = qkv_scr[:, head * HD : (head + 1) * HD]
            k = qkv_scr[:, features + head * HD : features + (head + 1) * HD]
            v = qkv_scr[:, 2 * features + head * HD : 2 * features + (head + 1) * HD]
            if picked:
                q = dot(pick_ref[...], q).astype(BF)
            scores = lax.dot_general(q, k, (((1,), (1,)), ((), ())), preferred_element_type=F32)
            scores = jnp.where(live, scores * HD ** (-0.5), -jnp.inf)
            weights = jnp.exp(scores - jnp.max(scores, axis=-1, keepdims=True))
            probs = (weights * (1.0 / jnp.sum(weights, axis=-1, keepdims=True))).astype(BF)
            lefts.append(dot(probs, dot(v, left_ref[...]).astype(BF)).astype(BF))
            rights.append(dot(probs, dot(v, right_ref[...]).astype(BF)).astype(BF))
        left = dot(jnp.concatenate(lefts, axis=1), wo_ref[...])
        right = dot(jnp.concatenate(rights, axis=1), wo_ref[...])
        return left, right

    def first_group(picked):
        left, right = attend(0, picked)
        rows = left.shape[0]
        acc_scr[:rows, :features] = left
        acc_scr[:rows, features:] = right

    def second_group(picked):
        left, right = attend(1, picked)
        rows = left.shape[0]
        before = dot(pick_ref[...], x_scr[...]) if picked else x_scr[...].astype(F32)
        left = (before[:, :features] + (acc_scr[:rows, :features] + left)).astype(BF)
        right = (before[:, features:] + (acc_scr[:rows, features:] + right)).astype(BF)
        if picked:
            out_ref[:, :features] = left
            out_ref[:, features:] = right
        else:
            x_scr[:, :features] = left
            x_scr[:, features:] = right
            if not masked_last:
                out_ref[:, :features] = left
                out_ref[:, features:] = right

    if masked_last:
        pl.when((part == QSTEPS) & (layer == 0))(functools.partial(first_group, False))
        pl.when((part == QSTEPS + 1) & (layer == 0))(functools.partial(second_group, False))
        pl.when((part == QSTEPS) & (layer == 1))(functools.partial(first_group, True))
        pl.when((part == QSTEPS + 1) & (layer == 1))(functools.partial(second_group, True))
    else:
        pl.when(part == QSTEPS)(functools.partial(first_group, False))
        pl.when(part == QSTEPS + 1)(functools.partial(second_group, False))


def sublayers(masked_last, valid, x, gains, pick, packed):
    patches, width = x.shape
    features = width // 2
    left, right = spread_matrices()
    out_rows = ROWS if masked_last else patches

    def qkv_block(step):
        layer, part = step // STEPS, step % STEPS
        ahead = (part >= QSTEPS) & (layer == 0)
        return 0, jnp.where(ahead, QSTEPS, QSTEPS * layer + jnp.minimum(part, QSTEPS - 1))

    def out_block(step):
        layer, part = step // STEPS, step % STEPS
        return jnp.where(part > QSTEPS, 1, 0), 6 + layer

    def whole(*shape):
        return pl.BlockSpec(shape, lambda step: (0,) * len(shape))

    return pl.pallas_call(
        functools.partial(sublayers_kernel, masked_last),
        grid=(2 * STEPS,),
        in_specs=[
            pl.BlockSpec(memory_space=pltpu.SMEM),
            whole(patches, width),
            whole(2, width),
            whole(ROWS, patches),
            whole(HD, 2 * HD),
            whole(HD, 2 * HD),
            pl.BlockSpec((width, QCHUNK), qkv_block),
            pl.BlockSpec((features, features), out_block),
        ],
        out_specs=whole(out_rows, width),
        out_shape=jax.ShapeDtypeStruct((out_rows, width), BF),
        scratch_shapes=[
            pltpu.VMEM((patches, width), BF),
            pltpu.VMEM((patches, width), BF),
            pltpu.VMEM((patches, 3 * features), BF),
            pltpu.VMEM((patches, width), F32),
        ],
        compiler_params=pltpu.CompilerParams(vmem_limit_bytes=40 * 1024 * 1024),
        cost_estimate=pl.CostEstimate(
            flops=14 * 10**9, bytes_accessed=27 * 10**6, transcendentals=10**6
        ),
        name="sublayers",
    )(valid, x, gains, pick, left, right, packed, packed)


def shards(
    teacher_in,
    teacher_qkv,
    teacher_out,
    teacher_gain,
    final_gain,
    projection,
    bucket,
    slot_image,
    mask_list,
    student_in,
    student_gain,
    w_gate,
    w_up,
    w_down,
):
    section = lax.axis_index("segment")
    column = lax.axis_index("dp")
    members = lax.axis_size("dp")
    images = bucket.shape[0]
    patches = teacher_in.shape[1]
    features = teacher_out.shape[2] // 2
    width = student_in.shape[-1]
    hidden_width = w_gate.shape[1]
    half = hidden_width // 4

    swap = [(0, 1), (1, 0), (2, 3), (3, 2)]
    upper = section % 2
    packed_own = jnp.concatenate(
        [
            teacher_qkv[0],
            jnp.concatenate([teacher_out[0, :, :features], teacher_out[0, :, features:]], axis=0),
        ],
        axis=1,
    )
    packed_other = lax.ppermute(packed_own, "segment", swap)
    lower_rows = jnp.where(upper == 0, packed_own, packed_other)
    upper_rows = jnp.where(upper == 0, packed_other, packed_own)
    cut = 3 * features
    packed = jnp.concatenate(
        [lower_rows[:, :cut], upper_rows[:, :cut], lower_rows[:, cut:], upper_rows[:, cut:]], axis=1
    )
    packed = lax.all_gather(packed, "dp", axis=0, tiled=True)
    other_gain = lax.ppermute(teacher_gain, "segment", swap)
    gains = jnp.where(
        upper == 0,
        jnp.concatenate([teacher_gain, other_gain], axis=0),
        jnp.concatenate([other_gain, teacher_gain], axis=0),
    )

    image_ids = jnp.arange(images, dtype=jnp.int32)
    positions = jnp.arange(patches, dtype=jnp.int32)
    slot_of = jnp.sum(
        jnp.where(slot_image[None, :] == image_ids[:, None], image_ids[None, :], 0), axis=1
    )
    listed = jnp.pad(mask_list, ((0, 0), (0, ROWS - mask_list.shape[1])))
    own_slots = lax.dynamic_slice_in_dim(listed, 2 * column, 2)
    own_pick = (own_slots[:, :, None] == positions[None, None, :]).astype(BF)
    chosen = jnp.einsum("srp,spf->srf", own_pick, student_in, preferred_element_type=F32).astype(BF)
    chosen = lax.all_to_all(chosen, "dp", split_axis=1, concat_axis=0, tiled=True)
    chosen = jnp.take(chosen, slot_of, axis=0)
    chosen = lax.all_to_all(chosen, "dp", split_axis=0, concat_axis=1, tiled=True)
    my_slots = lax.dynamic_slice_in_dim(slot_of, 2 * column, 2)
    my_lists = jnp.take(listed, my_slots, axis=0)
    my_valid = valid_counts(lax.dynamic_slice_in_dim(bucket, 2 * column, 2))
    my_count = 2 * my_valid // 5
    weights = jnp.where(
        jnp.arange(ROWS, dtype=jnp.int32)[None, :] < my_count[:, None],
        1.0 / my_count.astype(F32)[:, None],
        0.0,
    ).reshape(-1)

    flat_rows = chosen.reshape(-1, width)
    normed = normalize(flat_rows.astype(F32), student_gain).astype(BF)
    gate_act = dot(normed, w_gate)
    up_act = dot(normed, w_up)
    gate_sig = jax.nn.sigmoid(gate_act)
    hidden = (gate_act * gate_sig * up_act).astype(BF)
    output = flat_rows.astype(F32) + dot(hidden, w_down)
    out_scale = lax.rsqrt(jnp.mean(output * output, axis=-1) + EPS)
    gate_factor = up_act * gate_sig * (1.0 + gate_act * (1.0 - gate_sig))
    up_factor = gate_act * gate_sig
    normed_rows = lax.dynamic_slice_in_dim(normed, section * (width // 4), width // 4, 1).T
    down_rows = lax.dynamic_slice_in_dim(hidden, section * half, half, 1).T
    down_rows = down_rows.reshape(members, half // members, -1)
    down_top = down_rows[:, :8].reshape(8 * members, -1)
    down_rest = jnp.pad(down_rows[:, 8:], ((0, 0), (0, 16 - half // members), (0, 0)))
    down_rest = down_rest.reshape(8 * members, -1)

    packed, output, out_scale, gate_factor, up_factor, normed_rows, down_top, down_rest = (
        lax.optimization_barrier(
            (packed, output, out_scale, gate_factor, up_factor, normed_rows, down_top, down_rest)
        )
    )

    which = jnp.where((section == 0) | (section == 3), 0, 1)
    image = lax.dynamic_index_in_dim(teacher_in, which, 0, keepdims=False)
    valid = lax.dynamic_slice_in_dim(my_valid, which, 1)
    my_list = lax.dynamic_index_in_dim(my_lists, which, 0, keepdims=False)
    pick = (my_list[:, None] == positions[None, :]).astype(BF)
    middle = sublayers(False, valid, image, gains, pick, packed)
    middle = lax.ppermute(middle, "segment", [(0, 3), (1, 2)])
    packed, projection = lax.optimization_barrier((packed, projection))
    proj_full = lax.all_gather(projection, "dp", axis=0, tiled=True)
    last = sublayers(True, valid, middle, gains, pick, packed)
    normed_last = normalize(last.astype(F32), final_gain).astype(BF)
    target = dot(normed_last, proj_full).astype(BF)

    swapped = lax.ppermute(target, "segment", [(2, 3), (3, 2)])
    near = lax.ppermute(target, "segment", [(3, 0), (2, 1)])
    far = lax.ppermute(target, "segment", [(3, 1), (2, 0)])
    upper_half = section >= 2
    one = jnp.where(upper_half, target, near)
    two = jnp.where(upper_half, swapped, far)
    goal = jnp.where(which == 0, jnp.stack([one, two]), jnp.stack([two, one]))

    goal_rows = goal.reshape(-1, width).astype(F32)
    goal_scale = lax.rsqrt(jnp.mean(goal_rows * goal_rows, axis=-1) + EPS)
    inner_prod = jnp.sum(output * goal_rows, axis=-1)
    factor = -LOSS_SCALE * weights * goal_scale / width
    cubed = out_scale * out_scale * out_scale
    upstream = factor[:, None] * (
        out_scale[:, None] * goal_rows - (inner_prod * cubed / width)[:, None] * output
    )
    upstream = upstream.astype(BF)
    back_hidden = lax.dot_general(
        upstream, w_down, (((1,), (1,)), ((), ())), preferred_element_type=F32
    )
    gate_grad = (back_hidden * gate_factor).astype(BF)
    up_grad = (back_hidden * up_factor).astype(BF)
    terms = jnp.concatenate(
        [
            dot(normed_rows, gate_grad).astype(BF),
            dot(normed_rows, up_grad).astype(BF),
            dot(down_top, upstream).astype(BF),
            dot(down_rest, upstream).astype(BF),
        ],
        axis=1,
    ).reshape(members, 8, -1)
    terms = lax.all_to_all(terms, "dp", split_axis=0, concat_axis=0, tiled=True)
    summed = jnp.sum(terms.astype(F32), axis=0)
    cut = 2 * hidden_width
    grad_down = jnp.concatenate(
        [summed[:, cut : cut + width], summed[: half // members - 8, cut + width :]], axis=0
    )
    return summed[:, :hidden_width], summed[:, hidden_width:cut], grad_down


def solution(mesh):
    in_specs = (
        P("dp", None, None),
        P("segment", "dp", None),
        P("segment", "dp", None),
        P("segment", None),
        P(),
        P("dp", None),
        P(),
        P(),
        P(),
        P("dp", None, None),
        P(),
        P(),
        P(),
        P(),
    )
    out_specs = (P(("segment", "dp"), None), P(("segment", "dp"), None), P(("segment", "dp"), None))
    return jax.shard_map(shards, mesh=mesh, in_specs=in_specs, out_specs=out_specs, check_vma=False)
```

```python
import functools

import jax
import jax.numpy as jnp
import numpy as np
from jax import lax
from jax.experimental import pallas as pl
from jax.experimental.pallas import tpu as pltpu
from jax.sharding import PartitionSpec as P

HD = 112
SIDE = 16
EPS = 1e-06
LOSS_SCALE = 4096.0

ROWS = 112
SENT_ROWS = 128
BLOCK = 512
BLOCKS = 7
WINDOW = 256
QUARTER = 28
GROUP = 4
BF = jnp.bfloat16
F32 = jnp.float32


def normalize(values_in, gain):
    centred = values_in - jnp.mean(values_in, axis=-1, keepdims=True)
    return centred * lax.rsqrt(jnp.mean(centred * centred, axis=-1, keepdims=True) + EPS) * gain


def valid_counts(bucket_ids):
    side_len = SIDE - 2 * bucket_ids
    return side_len * side_len


def head_window(head):
    first = head * HD // 128 * 128
    first = min(first, 8 * HD - WINDOW)
    return first, head * HD - first


def spread_window(head):
    start = 2 * HD * (head % GROUP)
    first = start // 128 * 128
    return first, start - first, -(-(start + 2 * HD - first) // 128) * 128


def spread_matrices():
    feature = jnp.arange(WINDOW, dtype=jnp.int32)[:, None]
    lane = jnp.arange(384, dtype=jnp.int32)[None, :]
    sides = []
    for head in range(8):
        _, offset = head_window(head)
        _, lane_offset, _ = spread_window(head)
        place = feature - offset
        owner = sum((place >= QUARTER * i).astype(jnp.int32) for i in range(1, GROUP))
        target = lane_offset + place + QUARTER * owner
        inside = (place >= 0) & (place < HD)
        for side in range(2):
            sides.append((inside & (lane == target + QUARTER * side)).astype(BF))
    return jnp.stack(sides)


def dot(a, b):
    return jnp.dot(a, b, preferred_element_type=F32)


def sublayers_kernel(
    masked_last, valid_ref, x_ref, gain_ref, pick_ref, spread_ref, w_hbm,
    out_ref, x_scr, qkv_scr, att_scr, w_scr, sems,
):
    patches, width = x_ref.shape
    features = width // 2
    heads = features // HD
    copies = [
        pltpu.make_async_copy(
            w_hbm.at[:, pl.ds(BLOCK * i, BLOCK)], w_scr.at[i], sems.at[i]
        )
        for i in range(2 * BLOCKS)
    ]
    for copy in copies:
        copy.start()

    def attend(picked):
        rows = ROWS if picked else patches
        lane = lax.broadcasted_iota(jnp.int32, (1, WINDOW), 1)
        live = lax.broadcasted_iota(jnp.int32, (1, patches), 1) < valid_ref[0]
        for group in range(heads // GROUP):
            members = range(group * GROUP, (group + 1) * GROUP)
            scores = []
            for head in members:
                first, offset = head_window(head)
                q = qkv_scr[:, first : first + WINDOW]
                k = qkv_scr[:, features + first : features + first + WINDOW]
                if picked:
                    q = dot(pick_ref[...], q).astype(BF)
                q = jnp.where((lane >= offset) & (lane < offset + HD), q, jnp.zeros_like(q))
                scores.append(
                    lax.dot_general(q, k, (((1,), (1,)), ((), ())), preferred_element_type=F32)
                )
            attended = []
            for head, score in zip(members, scores):
                first, _ = head_window(head)
                v = qkv_scr[:, 2 * features + first : 2 * features + first + WINDOW]
                score = jnp.where(live, score * HD ** (-0.5), -jnp.inf)
                weights = jnp.exp(score - jnp.max(score, axis=-1, keepdims=True))
                probs = (weights * (1.0 / jnp.sum(weights, axis=-1, keepdims=True))).astype(BF)
                attended.append(dot(probs, v).astype(BF))
            for side in range(2):
                tiles = [[] for _ in range(GROUP * 2 * HD // 128)]
                for head, att in zip(members, attended):
                    first, _, wide = spread_window(head)
                    spread = dot(att, spread_ref[2 * head + side, :, :wide])
                    for tile in range(wide // 128):
                        tiles[first // 128 + tile].append(spread[:, tile * 128 : tile * 128 + 128])
                for tile, parts in enumerate(tiles):
                    start = GROUP * 2 * HD * group + 128 * tile
                    att_scr[rows * side : rows * (side + 1), start : start + 128] = sum(
                        parts[1:], parts[0]
                    ).astype(BF)

    for layer in range(2):
        base = layer * BLOCKS
        picked = masked_last and layer == 1
        rows = ROWS if picked else patches
        source = x_ref if layer == 0 else x_scr
        h = normalize(source[...].astype(F32), gain_ref[layer : layer + 1, :]).astype(BF)
        for block in range(BLOCKS - 2):
            copies[base + block].wait()
            qkv_scr[:, block * BLOCK : (block + 1) * BLOCK] = dot(h, w_scr[base + block]).astype(BF)
        rest = 3 * features - (BLOCKS - 2) * BLOCK
        copies[base + BLOCKS - 2].wait()
        qkv_scr[:, 3 * features - rest :] = dot(h, w_scr[base + BLOCKS - 2, :, :rest]).astype(BF)
        attend(picked)
        target = out_ref if picked or (layer == 1 and not masked_last) else x_scr

        def finish(start, columns, weights):
            update = dot(att_scr[: 2 * rows, :], weights)
            for side in range(2):
                place = slice(side * features + start, side * features + start + columns)
                before = source[:, place]
                before = dot(pick_ref[...], before) if picked else before.astype(F32)
                target[:, place] = (before + update[rows * side : rows * (side + 1)]).astype(BF)

        finish(0, BLOCK - rest, w_scr[base + BLOCKS - 2, :, rest:])
        copies[base + BLOCKS - 1].wait()
        finish(BLOCK - rest, BLOCK, w_scr[base + BLOCKS - 1])


def sublayers(masked_last, valid, x, gains, pick, spread, packed):
    patches, width = x.shape
    features = width // 2
    out_rows = ROWS if masked_last else patches
    vmem = pl.BlockSpec(memory_space=pltpu.VMEM)
    return pl.pallas_call(
        functools.partial(sublayers_kernel, masked_last),
        in_specs=[
            pl.BlockSpec(memory_space=pltpu.SMEM),
            vmem,
            vmem,
            vmem,
            vmem,
            pl.BlockSpec(memory_space=pl.ANY),
        ],
        out_specs=vmem,
        out_shape=jax.ShapeDtypeStruct((out_rows, width), BF),
        scratch_shapes=[
            pltpu.VMEM((patches, width), BF),
            pltpu.VMEM((patches, 3 * features), BF),
            pltpu.VMEM((2 * patches, width), BF),
            pltpu.VMEM((2 * BLOCKS, width, BLOCK), BF),
            pltpu.SemaphoreType.DMA((2 * BLOCKS,)),
        ],
        compiler_params=pltpu.CompilerParams(vmem_limit_bytes=48 * 1024 * 1024),
        cost_estimate=pl.CostEstimate(
            flops=14 * 10**9, bytes_accessed=27 * 10**6, transcendentals=10**6
        ),
        name="sublayers",
    )(valid, x, gains, pick, spread, packed)


def shards(
    teacher_in,
    teacher_qkv,
    teacher_out,
    teacher_gain,
    final_gain,
    projection,
    bucket,
    slot_image,
    mask_list,
    student_in,
    student_gain,
    w_gate,
    w_up,
    w_down,
):
    section = lax.axis_index("segment")
    column = lax.axis_index("dp")
    members = lax.axis_size("dp")
    images = bucket.shape[0]
    patches = teacher_in.shape[1]
    features = teacher_out.shape[2] // 2
    width = student_in.shape[-1]
    hidden_width = w_gate.shape[1]

    swap = [(0, 1), (1, 0), (2, 3), (3, 2)]
    upper = section % 2
    packed_own = jnp.concatenate(
        [
            teacher_qkv[0],
            jnp.concatenate([teacher_out[0, :, :features], teacher_out[0, :, features:]], axis=0),
        ],
        axis=1,
    )
    packed_other = lax.ppermute(packed_own, "segment", swap)
    lower_rows = jnp.where(upper == 0, packed_own, packed_other)
    upper_rows = jnp.where(upper == 0, packed_other, packed_own)
    packed = jnp.concatenate([lower_rows, upper_rows], axis=1)
    packed = lax.all_gather(packed, "dp", axis=0, tiled=True)
    other_gain = lax.ppermute(teacher_gain, "segment", swap)
    gains = jnp.where(
        upper == 0,
        jnp.concatenate([teacher_gain, other_gain], axis=0),
        jnp.concatenate([other_gain, teacher_gain], axis=0),
    )

    core = column % 2
    other_core = [(device, device ^ 1) for device in range(members)]

    def of_chip(own):
        other = lax.ppermute(own, "dp", other_core)
        first = jnp.where(core == 0, own, other)
        second = jnp.where(core == 0, other, own)
        return jnp.concatenate([first, second], axis=0)

    image_ids = jnp.arange(images, dtype=jnp.int32)
    positions = jnp.arange(patches, dtype=jnp.int32)
    slot_of = jnp.sum(
        jnp.where(slot_image[None, :] == image_ids[:, None], image_ids[None, :], 0), axis=1
    )
    listed = jnp.pad(mask_list, ((0, 0), (0, SENT_ROWS - mask_list.shape[1])))
    own_slots = lax.dynamic_slice_in_dim(listed, 2 * column, 2)
    own_pick = (own_slots[:, :, None] == positions[None, None, :]).astype(BF)
    chosen = jnp.einsum("srp,spf->srf", own_pick, student_in, preferred_element_type=F32).astype(BF)
    chosen = lax.all_to_all(chosen, "dp", split_axis=1, concat_axis=0, tiled=True)
    chosen = jnp.take(chosen, slot_of, axis=0)
    chosen = lax.all_to_all(chosen, "dp", split_axis=0, concat_axis=1, tiled=True)
    chosen = of_chip(chosen[:, :ROWS])
    my_slots = lax.dynamic_slice_in_dim(slot_of, 2 * column, 2)
    my_lists = jnp.take(listed[:, :ROWS], my_slots, axis=0)
    my_valid = valid_counts(lax.dynamic_slice_in_dim(bucket, 2 * column, 2))
    chip_count = 2 * valid_counts(lax.dynamic_slice_in_dim(bucket, 4 * (column // 2), 4)) // 5
    weights = jnp.where(
        jnp.arange(ROWS, dtype=jnp.int32)[None, :] < chip_count[:, None],
        1.0 / chip_count.astype(F32)[:, None],
        0.0,
    ).reshape(-1)

    flat_rows = chosen.reshape(-1, width)
    normed = normalize(flat_rows.astype(F32), student_gain).astype(BF)
    gate_act = dot(normed, w_gate)
    up_act = dot(normed, w_up)
    gate_sig = jax.nn.sigmoid(gate_act)
    hidden = (gate_act * gate_sig * up_act).astype(BF)
    output = flat_rows.astype(F32) + dot(hidden, w_down)
    out_scale = lax.rsqrt(jnp.mean(output * output, axis=-1) + EPS)
    gate_factor = up_act * gate_sig * (1.0 + gate_act * (1.0 - gate_sig))
    up_factor = gate_act * gate_sig

    chips = members // 2

    def own_rows(columns, count):
        rows = lax.dynamic_slice_in_dim(columns, section * count, count, 1).T
        rows = rows.reshape(chips, 2, count // members, -1)
        return lax.dynamic_index_in_dim(rows, core, 1, keepdims=False)

    normed_rows = own_rows(normed, width // 4).reshape(8 * chips, -1)
    down_rows = own_rows(hidden, hidden_width // 4)
    down_each = hidden_width // 4 // members
    down_top = down_rows[:, :8].reshape(8 * chips, -1)
    down_rest = jnp.pad(down_rows[:, 8:], ((0, 0), (0, 16 - down_each), (0, 0)))
    down_rest = down_rest.reshape(8 * chips, -1)
    spread = spread_matrices()

    packed, spread, output, out_scale, gate_factor, up_factor, normed_rows, down_top, down_rest = (
        lax.optimization_barrier(
            (packed, spread, output, out_scale, gate_factor, up_factor, normed_rows, down_top, down_rest)
        )
    )

    which = jnp.where((section == 0) | (section == 3), 0, 1)
    image = lax.dynamic_index_in_dim(teacher_in, which, 0, keepdims=False)
    valid = lax.dynamic_slice_in_dim(my_valid, which, 1)
    my_list = lax.dynamic_index_in_dim(my_lists, which, 0, keepdims=False)
    pick = (my_list[:, None] == positions[None, :]).astype(BF)
    middle = sublayers(False, valid, image, gains, pick, spread, packed)
    middle = lax.ppermute(middle, "segment", [(0, 3), (1, 2)])
    packed, projection = lax.optimization_barrier((packed, projection))
    proj_full = lax.all_gather(projection, "dp", axis=0, tiled=True)
    last = sublayers(True, valid, middle, gains, pick, spread, packed)
    normed_last = normalize(last.astype(F32), final_gain).astype(BF)
    target = dot(normed_last, proj_full).astype(BF)

    swapped = lax.ppermute(target, "segment", [(2, 3), (3, 2)])
    near = lax.ppermute(target, "segment", [(3, 0), (2, 1)])
    far = lax.ppermute(target, "segment", [(3, 1), (2, 0)])
    upper_half = section >= 2
    one = jnp.where(upper_half, target, near)
    two = jnp.where(upper_half, swapped, far)
    goal = of_chip(jnp.where(which == 0, jnp.stack([one, two]), jnp.stack([two, one])))

    goal_rows = goal.reshape(-1, width).astype(F32)
    goal_scale = lax.rsqrt(jnp.mean(goal_rows * goal_rows, axis=-1) + EPS)
    inner_prod = jnp.sum(output * goal_rows, axis=-1)
    factor = -LOSS_SCALE * weights * goal_scale / width
    cubed = out_scale * out_scale * out_scale
    upstream = factor[:, None] * (
        out_scale[:, None] * goal_rows - (inner_prod * cubed / width)[:, None] * output
    )
    upstream = upstream.astype(BF)
    back_hidden = lax.dot_general(
        upstream, w_down, (((1,), (1,)), ((), ())), preferred_element_type=F32
    )
    gate_grad = (back_hidden * gate_factor).astype(BF)
    up_grad = (back_hidden * up_factor).astype(BF)
    terms = jnp.concatenate(
        [
            dot(normed_rows, gate_grad).astype(BF),
            dot(normed_rows, up_grad).astype(BF),
            dot(down_top, upstream).astype(BF),
            dot(down_rest, upstream).astype(BF),
        ],
        axis=1,
    ).reshape(chips, 8, -1)
    same_core = [list(range(0, members, 2)), list(range(1, members, 2))]
    terms = lax.all_to_all(
        terms, "dp", split_axis=0, concat_axis=0, tiled=True, axis_index_groups=same_core
    )
    summed = jnp.sum(terms.astype(F32), axis=0)
    cut = 2 * hidden_width
    grad_down = jnp.concatenate(
        [summed[:, cut : cut + width], summed[: down_each - 8, cut + width :]], axis=0
    )
    return summed[:, :hidden_width], summed[:, hidden_width:cut], grad_down


def solution(mesh):
    in_specs = (
        P("dp", None, None),
        P("segment", "dp", None),
        P("segment", "dp", None),
        P("segment", None),
        P(),
        P("dp", None),
        P(),
        P(),
        P(),
        P("dp", None, None),
        P(),
        P(),
        P(),
        P(),
    )
    out_specs = (P(("segment", "dp"), None), P(("segment", "dp"), None), P(("segment", "dp"), None))
    return jax.shard_map(shards, mesh=mesh, in_specs=in_specs, out_specs=out_specs, check_vma=False)
```

```python
import functools

import jax
import jax.numpy as jnp
import numpy as np
from jax import lax
from jax.experimental import pallas as pl
from jax.experimental.pallas import tpu as pltpu
from jax.sharding import PartitionSpec as P

HD = 112
SIDE = 16
EPS = 1e-06
LOSS_SCALE = 4096.0

ROWS = 112
SENT_ROWS = 128
BLOCK = 512
BLOCKS = 7
WINDOW = 256
QUARTER = 28
GROUP = 4
BF = jnp.bfloat16
F32 = jnp.float32


def normalize(values_in, gain):
    centred = values_in - jnp.mean(values_in, axis=-1, keepdims=True)
    return centred * lax.rsqrt(jnp.mean(centred * centred, axis=-1, keepdims=True) + EPS) * gain


def valid_counts(bucket_ids):
    side_len = SIDE - 2 * bucket_ids
    return side_len * side_len


def head_window(head):
    first = head * HD // 128 * 128
    first = min(first, 8 * HD - WINDOW)
    return first, head * HD - first


def spread_window(head):
    start = 2 * HD * (head % GROUP)
    first = start // 128 * 128
    return first, start - first, -(-(start + 2 * HD - first) // 128) * 128


def spread_matrices():
    feature = jnp.arange(WINDOW, dtype=jnp.int32)[:, None]
    lane = jnp.arange(384, dtype=jnp.int32)[None, :]
    sides = []
    for head in range(8):
        _, offset = head_window(head)
        _, lane_offset, _ = spread_window(head)
        place = feature - offset
        owner = sum((place >= QUARTER * i).astype(jnp.int32) for i in range(1, GROUP))
        target = lane_offset + place + QUARTER * owner
        inside = (place >= 0) & (place < HD)
        for side in range(2):
            sides.append((inside & (lane == target + QUARTER * side)).astype(BF))
    return jnp.stack(sides)


def dot(a, b):
    return jnp.dot(a, b, preferred_element_type=F32)


def sublayers_kernel(
    masked_last, valid_ref, place_ref, x_ref, gain_ref, pick_ref, spread_ref, own_hbm, *refs
):
    pieces_hbm, (out_ref, x_scr, qkv_scr, att_scr, w_scr, own_sems, sems) = refs[:10], refs[10:]
    patches, width = x_ref.shape
    features = width // 2
    heads = features // HD
    own_slot = place_ref[32]
    core = place_ref[33]
    copies = [
        pltpu.make_async_copy(
            own_hbm.at[:, pl.ds(BLOCK * i, BLOCK)],
            w_scr.at[own_slot, :, pl.ds(BLOCK * i, BLOCK)],
            own_sems.at[i],
        )
        for i in range(BLOCKS)
    ]

    def half_copies(mine):
        arrays = pieces_hbm[:5] if mine else pieces_hbm[5:]
        half = core if mine else 1 - core
        base = 0 if mine else 16
        found = []
        for array, behind, left, wide in zip(
            arrays, (0, 1, 3, 2, 2), (0, 0, 0, 0, features), (width, width, width, features, features)
        ):
            for along in range(4):
                row = pl.multiple_of(place_ref[base + 4 * behind + along], 16)
                column = pl.multiple_of(half * width + left, 128)
                found.append(
                    pltpu.make_async_copy(
                        array.at[along],
                        w_scr.at[1 - own_slot, pl.ds(row, array.shape[1]), pl.ds(column, wide)],
                        sems.at[0 if mine else 1, len(found)],
                    )
                )
        return found

    def each_half(half, act):
        for mine in (True, False):

            @pl.when((core == half) if mine else (core != half))
            def _():
                for copy in half_copies(mine):
                    act(copy)

    def start_own():
        for copy in copies:
            copy.start()

    def start_other():
        for half in range(2):
            each_half(half, lambda copy: copy.start())

    @pl.when(own_slot == 0)
    def _():
        start_own()
        start_other()

    @pl.when(own_slot == 1)
    def _():
        start_other()
        start_own()

    def arrive(layer, block):
        @pl.when(own_slot == layer)
        def _():
            copies[block].wait()

        if block in (0, 3):

            @pl.when(own_slot != layer)
            def _():
                each_half(block // 3, lambda copy: copy.wait())

    def attend(picked):
        rows = ROWS if picked else patches
        lane = lax.broadcasted_iota(jnp.int32, (1, WINDOW), 1)
        live = lax.broadcasted_iota(jnp.int32, (1, patches), 1) < valid_ref[0]
        for group in range(heads // GROUP):
            members = range(group * GROUP, (group + 1) * GROUP)
            scores = []
            for head in members:
                first, offset = head_window(head)
                q = qkv_scr[:, first : first + WINDOW]
                k = qkv_scr[:, features + first : features + first + WINDOW]
                if picked:
                    q = dot(pick_ref[...], q).astype(BF)
                q = jnp.where((lane >= offset) & (lane < offset + HD), q, jnp.zeros_like(q))
                scores.append(
                    lax.dot_general(q, k, (((1,), (1,)), ((), ())), preferred_element_type=F32)
                )
            attended = []
            for head, score in zip(members, scores):
                first, _ = head_window(head)
                v = qkv_scr[:, 2 * features + first : 2 * features + first + WINDOW]
                score = jnp.where(live, score * HD ** (-0.5), -jnp.inf)
                weights = jnp.exp(score - jnp.max(score, axis=-1, keepdims=True))
                probs = (weights * (1.0 / jnp.sum(weights, axis=-1, keepdims=True))).astype(BF)
                attended.append(dot(probs, v).astype(BF))
            for side in range(2):
                tiles = [[] for _ in range(GROUP * 2 * HD // 128)]
                for head, att in zip(members, attended):
                    first, _, wide = spread_window(head)
                    spread = dot(att, spread_ref[2 * head + side, :, :wide])
                    for tile in range(wide // 128):
                        tiles[first // 128 + tile].append(spread[:, tile * 128 : tile * 128 + 128])
                for tile, parts in enumerate(tiles):
                    start = GROUP * 2 * HD * group + 128 * tile
                    att_scr[rows * side : rows * (side + 1), start : start + 128] = sum(
                        parts[1:], parts[0]
                    ).astype(BF)

    for layer in range(2):
        picked = masked_last and layer == 1
        rows = ROWS if picked else patches
        source = x_ref if layer == 0 else x_scr
        h = normalize(source[...].astype(F32), gain_ref[layer : layer + 1, :]).astype(BF)
        for block in range(BLOCKS - 2):
            arrive(layer, block)
            here = slice(block * BLOCK, (block + 1) * BLOCK)
            qkv_scr[:, here] = dot(h, w_scr[layer, :, here]).astype(BF)
        rest = 3 * features - (BLOCKS - 2) * BLOCK
        arrive(layer, BLOCKS - 2)
        here = slice(3 * features - rest, 3 * features)
        qkv_scr[:, here] = dot(h, w_scr[layer, :, here]).astype(BF)
        attend(picked)
        target = out_ref if picked or (layer == 1 and not masked_last) else x_scr

        def finish(start, columns, weights):
            update = dot(att_scr[: 2 * rows, :], weights)
            for side in range(2):
                place = slice(side * features + start, side * features + start + columns)
                before = source[:, place]
                before = dot(pick_ref[...], before) if picked else before.astype(F32)
                target[:, place] = (before + update[rows * side : rows * (side + 1)]).astype(BF)

        last = (BLOCKS - 1) * BLOCK
        finish(0, BLOCK - rest, w_scr[layer, :, 3 * features : last])
        arrive(layer, BLOCKS - 1)
        finish(BLOCK - rest, BLOCK, w_scr[layer, :, last:])


def sublayers(masked_last, valid, place, x, gains, pick, spread, own, pieces):
    patches, width = x.shape
    features = width // 2
    out_rows = ROWS if masked_last else patches
    vmem = pl.BlockSpec(memory_space=pltpu.VMEM)
    smem = pl.BlockSpec(memory_space=pltpu.SMEM)
    return pl.pallas_call(
        functools.partial(sublayers_kernel, masked_last),
        in_specs=[smem, smem, vmem, vmem, vmem, vmem] + [pl.BlockSpec(memory_space=pl.ANY)] * 11,
        out_specs=vmem,
        out_shape=jax.ShapeDtypeStruct((out_rows, width), BF),
        scratch_shapes=[
            pltpu.VMEM((patches, width), BF),
            pltpu.VMEM((patches, 3 * features), BF),
            pltpu.VMEM((2 * patches, width), BF),
            pltpu.VMEM((2, width, 2 * width), BF),
            pltpu.SemaphoreType.DMA((BLOCKS,)),
            pltpu.SemaphoreType.DMA((2, 20)),
        ],
        compiler_params=pltpu.CompilerParams(vmem_limit_bytes=48 * 1024 * 1024),
        cost_estimate=pl.CostEstimate(
            flops=14 * 10**9, bytes_accessed=27 * 10**6, transcendentals=10**6
        ),
        name="sublayers",
    )(valid, place, x, gains, pick, spread, own, *pieces)


def gather_other(own, swap):
    column = lax.axis_index("dp")
    members = lax.axis_size("dp")
    core = column % 2
    half = own.shape[1] // 2
    cut = half // 2

    def pairs(first, second):
        found = []
        for device in range(members):
            x, y, c = device // 8, device // 2 % 4, device % 2
            ahead = (first, second) if c == 0 else (second, first)
            found.append((device, ((x + ahead[0]) % 4 * 4 + (y + ahead[1]) % 4) * 2 + c))
        return found

    def moved(value, first, second):
        return lax.ppermute(value, "dp", pairs(first, second))

    other_core = [(device, device ^ 1) for device in range(members)]
    keep = jnp.where(core == 0, own[:, :half], own[:, half:])
    give = jnp.where(core == 0, own[:, half:], own[:, :half])
    got = lax.ppermute(give, "dp", other_core)
    rows = jnp.concatenate(
        [jnp.where(core == 0, keep, got), jnp.where(core == 0, got, keep)], axis=0
    )
    rows = lax.ppermute(rows, "segment", swap)
    behind = moved(rows, 1, 0)
    ahead = moved(rows, -1, 0)
    across = jnp.concatenate(
        [moved(behind[:, :cut], 1, 0), moved(ahead[:, cut:], -1, 0)], axis=1
    )
    line = jnp.stack([rows, ahead, across, behind])
    line_behind = moved(line, 0, 1)
    line_ahead = moved(line, 0, -1)
    across_left = moved(line_behind[:, :, :cut], 0, 1)
    across_right = moved(line_ahead[:, :, cut:], 0, -1)
    mine = [line, line_ahead, line_behind, across_left, across_right]
    theirs = [lax.ppermute(piece, "dp", other_core) for piece in mine]

    x, y = column // 8, column // 2 % 4
    steps = jnp.arange(4, dtype=jnp.int32)
    x_first = 4 * ((x + steps[None, :]) % 4) + (y + steps[:, None]) % 4
    y_first = 4 * ((x + steps[:, None]) % 4) + (y + steps[None, :]) % 4
    chips = jnp.stack([jnp.where(core == 0, x_first, y_first), jnp.where(core == 0, y_first, x_first)])
    return mine + theirs, chips.reshape(-1) * rows.shape[0], core


def shards(
    teacher_in,
    teacher_qkv,
    teacher_out,
    teacher_gain,
    final_gain,
    projection,
    bucket,
    slot_image,
    mask_list,
    student_in,
    student_gain,
    w_gate,
    w_up,
    w_down,
):
    section = lax.axis_index("segment")
    column = lax.axis_index("dp")
    members = lax.axis_size("dp")
    images = bucket.shape[0]
    patches = teacher_in.shape[1]
    features = teacher_out.shape[2] // 2
    width = student_in.shape[-1]
    hidden_width = w_gate.shape[1]

    swap = [(0, 1), (1, 0), (2, 3), (3, 2)]
    upper = section % 2
    packed_own = jnp.concatenate(
        [
            teacher_qkv[0],
            jnp.concatenate([teacher_out[0, :, :features], teacher_out[0, :, features:]], axis=0),
        ],
        axis=1,
    )
    pieces, place, core = gather_other(packed_own, swap)
    place = jnp.concatenate([place, upper[None], core[None]]).astype(jnp.int32)
    packed = lax.all_gather(packed_own, "dp", axis=0, tiled=True)
    other_gain = lax.ppermute(teacher_gain, "segment", swap)
    gains = jnp.where(
        upper == 0,
        jnp.concatenate([teacher_gain, other_gain], axis=0),
        jnp.concatenate([other_gain, teacher_gain], axis=0),
    )

    other_core = [(device, device ^ 1) for device in range(members)]

    def of_chip(own):
        other = lax.ppermute(own, "dp", other_core)
        first = jnp.where(core == 0, own, other)
        second = jnp.where(core == 0, other, own)
        return jnp.concatenate([first, second], axis=0)

    student_in, first_piece = lax.optimization_barrier((student_in, pieces[0]))
    pieces = [first_piece] + pieces[1:]
    image_ids = jnp.arange(images, dtype=jnp.int32)
    positions = jnp.arange(patches, dtype=jnp.int32)
    slot_of = jnp.sum(
        jnp.where(slot_image[None, :] == image_ids[:, None], image_ids[None, :], 0), axis=1
    )
    listed = jnp.pad(mask_list, ((0, 0), (0, SENT_ROWS - mask_list.shape[1])))
    own_slots = lax.dynamic_slice_in_dim(listed, 2 * column, 2)
    own_pick = (own_slots[:, :, None] == positions[None, None, :]).astype(BF)
    chosen = jnp.einsum("srp,spf->srf", own_pick, student_in, preferred_element_type=F32).astype(BF)
    chosen = lax.all_to_all(chosen, "dp", split_axis=1, concat_axis=0, tiled=True)
    chosen = jnp.take(chosen, slot_of, axis=0)
    chosen = lax.all_to_all(chosen, "dp", split_axis=0, concat_axis=1, tiled=True)
    chosen = of_chip(chosen[:, :ROWS])
    spread = spread_matrices()
    packed, pieces, chosen, spread = lax.optimization_barrier((packed, pieces, chosen, spread))
    my_slots = lax.dynamic_slice_in_dim(slot_of, 2 * column, 2)
    my_lists = jnp.take(listed[:, :ROWS], my_slots, axis=0)
    my_valid = valid_counts(lax.dynamic_slice_in_dim(bucket, 2 * column, 2))
    chip_count = 2 * valid_counts(lax.dynamic_slice_in_dim(bucket, 4 * (column // 2), 4)) // 5
    weights = jnp.where(
        jnp.arange(ROWS, dtype=jnp.int32)[None, :] < chip_count[:, None],
        1.0 / chip_count.astype(F32)[:, None],
        0.0,
    ).reshape(-1)

    flat_rows = chosen.reshape(-1, width)
    normed = normalize(flat_rows.astype(F32), student_gain).astype(BF)
    gate_act = dot(normed, w_gate)
    up_act = dot(normed, w_up)
    gate_sig = jax.nn.sigmoid(gate_act)
    hidden = (gate_act * gate_sig * up_act).astype(BF)
    output = flat_rows.astype(F32) + dot(hidden, w_down)
    out_scale = lax.rsqrt(jnp.mean(output * output, axis=-1) + EPS)
    gate_factor = up_act * gate_sig * (1.0 + gate_act * (1.0 - gate_sig))
    up_factor = gate_act * gate_sig

    chips = members // 2

    def own_rows(columns, count):
        rows = lax.dynamic_slice_in_dim(columns, section * count, count, 1).T
        rows = rows.reshape(chips, 2, count // members, -1)
        return lax.dynamic_index_in_dim(rows, core, 1, keepdims=False)

    normed_rows = own_rows(normed, width // 4).reshape(8 * chips, -1)
    down_rows = own_rows(hidden, hidden_width // 4)
    down_each = hidden_width // 4 // members
    down_top = down_rows[:, :8].reshape(8 * chips, -1)
    down_rest = jnp.pad(down_rows[:, 8:], ((0, 0), (0, 16 - down_each), (0, 0)))
    down_rest = down_rest.reshape(8 * chips, -1)

    which = jnp.where((section == 0) | (section == 3), 0, 1)
    image = lax.dynamic_index_in_dim(teacher_in, which, 0, keepdims=False)
    valid = lax.dynamic_slice_in_dim(my_valid, which, 1)
    my_list = lax.dynamic_index_in_dim(my_lists, which, 0, keepdims=False)
    pick = (my_list[:, None] == positions[None, :]).astype(BF)
    middle = sublayers(False, valid, place, image, gains, pick, spread, packed, pieces)
    middle = lax.ppermute(middle, "segment", [(0, 3), (1, 2)])
    packed, projection = lax.optimization_barrier((packed, projection))
    proj_full = lax.all_gather(projection, "dp", axis=0, tiled=True)
    middle, output, out_scale, gate_factor, up_factor, normed_rows, down_top, down_rest = (
        lax.optimization_barrier(
            (middle, output, out_scale, gate_factor, up_factor, normed_rows, down_top, down_rest)
        )
    )
    last = sublayers(True, valid, place, middle, gains, pick, spread, packed, pieces)
    normed_last = normalize(last.astype(F32), final_gain).astype(BF)
    target = dot(normed_last, proj_full).astype(BF)

    swapped = lax.ppermute(target, "segment", [(2, 3), (3, 2)])
    near = lax.ppermute(target, "segment", [(3, 0), (2, 1)])
    far = lax.ppermute(target, "segment", [(3, 1), (2, 0)])
    upper_half = section >= 2
    one = jnp.where(upper_half, target, near)
    two = jnp.where(upper_half, swapped, far)
    goal = of_chip(jnp.where(which == 0, jnp.stack([one, two]), jnp.stack([two, one])))

    goal_rows = goal.reshape(-1, width).astype(F32)
    goal_scale = lax.rsqrt(jnp.mean(goal_rows * goal_rows, axis=-1) + EPS)
    inner_prod = jnp.sum(output * goal_rows, axis=-1)
    factor = -LOSS_SCALE * weights * goal_scale / width
    cubed = out_scale * out_scale * out_scale
    upstream = factor[:, None] * (
        out_scale[:, None] * goal_rows - (inner_prod * cubed / width)[:, None] * output
    )
    upstream = upstream.astype(BF)
    back_hidden = lax.dot_general(
        upstream, w_down, (((1,), (1,)), ((), ())), preferred_element_type=F32
    )
    gate_grad = (back_hidden * gate_factor).astype(BF)
    up_grad = (back_hidden * up_factor).astype(BF)
    terms = jnp.concatenate(
        [
            dot(normed_rows, gate_grad).astype(BF),
            dot(normed_rows, up_grad).astype(BF),
            dot(down_top, upstream).astype(BF),
            dot(down_rest, upstream).astype(BF),
        ],
        axis=1,
    ).reshape(chips, 8, -1)
    same_core = [list(range(0, members, 2)), list(range(1, members, 2))]
    terms = lax.all_to_all(
        terms, "dp", split_axis=0, concat_axis=0, tiled=True, axis_index_groups=same_core
    )
    summed = jnp.sum(terms.astype(F32), axis=0)
    cut = 2 * hidden_width
    grad_down = jnp.concatenate(
        [summed[:, cut : cut + width], summed[: down_each - 8, cut + width :]], axis=0
    )
    return summed[:, :hidden_width], summed[:, hidden_width:cut], grad_down


def solution(mesh):
    in_specs = (
        P("dp", None, None),
        P("segment", "dp", None),
        P("segment", "dp", None),
        P("segment", None),
        P(),
        P("dp", None),
        P(),
        P(),
        P(),
        P("dp", None, None),
        P(),
        P(),
        P(),
        P(),
    )
    out_specs = (P(("segment", "dp"), None), P(("segment", "dp"), None), P(("segment", "dp"), None))
    return jax.shard_map(shards, mesh=mesh, in_specs=in_specs, out_specs=out_specs, check_vma=False)
```

```python
import functools

import jax
import jax.numpy as jnp
import ml_dtypes
import numpy as np
from jax import lax
from jax.experimental import pallas as pl
from jax.experimental.pallas import tpu as pltpu
from jax.sharding import PartitionSpec as P

HD = 112
SIDE = 16
EPS = 1e-06
LOSS_SCALE = 4096.0

ROWS = 112
SENT_ROWS = 128
BLOCK = 512
BLOCKS = 7
WINDOW = 256
QUARTER = 28
GROUP = 4
BF = jnp.bfloat16
F32 = jnp.float32


def normalize(values_in, gain):
    centred = values_in - jnp.mean(values_in, axis=-1, keepdims=True)
    return centred * lax.rsqrt(jnp.mean(centred * centred, axis=-1, keepdims=True) + EPS) * gain


def valid_counts(bucket_ids):
    side_len = SIDE - 2 * bucket_ids
    return side_len * side_len


def head_window(head):
    first = head * HD // 128 * 128
    first = min(first, 8 * HD - WINDOW)
    return first, head * HD - first


def spread_window(head):
    start = 2 * HD * (head % GROUP)
    first = start // 128 * 128
    return first, start - first, -(-(start + 2 * HD - first) // 128) * 128


def spread_matrices():
    sides = np.zeros((16, WINDOW, 384), ml_dtypes.bfloat16)
    for head in range(8):
        _, offset = head_window(head)
        _, lane_offset, _ = spread_window(head)
        for place in range(HD):
            target = lane_offset + place + QUARTER * (place // QUARTER)
            for side in range(2):
                sides[2 * head + side, offset + place, target + QUARTER * side] = 1.0
    return jnp.asarray(sides)


def after(value, token):
    return lax.optimization_barrier((value, token))


def dot(a, b):
    return jnp.dot(a, b, preferred_element_type=F32)


def sublayers_kernel(
    masked_last, valid_ref, place_ref, x_ref, gain_ref, pick_ref, spread_ref, own_hbm, *refs
):
    pieces_hbm, (out_ref, x_scr, qkv_scr, att_scr, w_scr, own_sems, sems) = refs[:10], refs[10:]
    patches, width = x_ref.shape
    features = width // 2
    heads = features // HD
    own_slot = place_ref[32]
    core = place_ref[33]
    copies = [
        pltpu.make_async_copy(
            own_hbm.at[:, pl.ds(BLOCK * i, BLOCK)],
            w_scr.at[own_slot, :, pl.ds(BLOCK * i, BLOCK)],
            own_sems.at[i],
        )
        for i in range(BLOCKS)
    ]

    def half_copies(mine):
        arrays = pieces_hbm[:5] if mine else pieces_hbm[5:]
        half = core if mine else 1 - core
        base = 0 if mine else 16
        found = []
        for array, behind, left, wide in zip(
            arrays, (0, 1, 3, 2, 2), (0, 0, 0, 0, features), (width, width, width, features, features)
        ):
            for along in range(4):
                row = pl.multiple_of(place_ref[base + 4 * behind + along], 16)
                column = pl.multiple_of(half * width + left, 128)
                found.append(
                    pltpu.make_async_copy(
                        array.at[along],
                        w_scr.at[1 - own_slot, pl.ds(row, array.shape[1]), pl.ds(column, wide)],
                        sems.at[0 if mine else 1, len(found)],
                    )
                )
        return found

    def each_half(half, act):
        for mine in (True, False):

            @pl.when((core == half) if mine else (core != half))
            def _():
                for copy in half_copies(mine):
                    act(copy)

    def start_own():
        for copy in copies:
            copy.start()

    def start_other():
        for half in range(2):
            each_half(half, lambda copy: copy.start())

    @pl.when(own_slot == 0)
    def _():
        start_own()
        start_other()

    @pl.when(own_slot == 1)
    def _():
        start_other()
        start_own()

    def arrive(layer, block):
        @pl.when(own_slot == layer)
        def _():
            copies[block].wait()

        if block in (0, 3):

            @pl.when(own_slot != layer)
            def _():
                each_half(block // 3, lambda copy: copy.wait())

    def attend(picked):
        rows = ROWS if picked else patches
        lane = lax.broadcasted_iota(jnp.int32, (1, WINDOW), 1)
        live = lax.broadcasted_iota(jnp.int32, (1, patches), 1) < valid_ref[0]
        for group in range(heads // GROUP):
            members = range(group * GROUP, (group + 1) * GROUP)
            scores = []
            for head in members:
                first, offset = head_window(head)
                q = qkv_scr[:, first : first + WINDOW]
                k = qkv_scr[:, features + first : features + first + WINDOW]
                if picked:
                    q = dot(pick_ref[...], q).astype(BF)
                q = jnp.where((lane >= offset) & (lane < offset + HD), q, jnp.zeros_like(q))
                scores.append(
                    lax.dot_general(q, k, (((1,), (1,)), ((), ())), preferred_element_type=F32)
                )
            attended = []
            for head, score in zip(members, scores):
                first, _ = head_window(head)
                v = qkv_scr[:, 2 * features + first : 2 * features + first + WINDOW]
                score = jnp.where(live, score * HD ** (-0.5), -jnp.inf)
                weights = jnp.exp(score - jnp.max(score, axis=-1, keepdims=True))
                probs = (weights * (1.0 / jnp.sum(weights, axis=-1, keepdims=True))).astype(BF)
                attended.append(dot(probs, v).astype(BF))
            for side in range(2):
                tiles = [[] for _ in range(GROUP * 2 * HD // 128)]
                for head, att in zip(members, attended):
                    first, _, wide = spread_window(head)
                    spread = dot(att, spread_ref[2 * head + side, :, :wide])
                    for tile in range(wide // 128):
                        tiles[first // 128 + tile].append(spread[:, tile * 128 : tile * 128 + 128])
                for tile, parts in enumerate(tiles):
                    start = GROUP * 2 * HD * group + 128 * tile
                    att_scr[rows * side : rows * (side + 1), start : start + 128] = sum(
                        parts[1:], parts[0]
                    ).astype(BF)

    for layer in range(2):
        picked = masked_last and layer == 1
        rows = ROWS if picked else patches
        source = x_ref if layer == 0 else x_scr
        h = normalize(source[...].astype(F32), gain_ref[layer : layer + 1, :]).astype(BF)
        for block in range(BLOCKS - 2):
            arrive(layer, block)
            here = slice(block * BLOCK, (block + 1) * BLOCK)
            qkv_scr[:, here] = dot(h, w_scr[layer, :, here]).astype(BF)
        rest = 3 * features - (BLOCKS - 2) * BLOCK
        arrive(layer, BLOCKS - 2)
        here = slice(3 * features - rest, 3 * features)
        qkv_scr[:, here] = dot(h, w_scr[layer, :, here]).astype(BF)
        attend(picked)
        target = out_ref if picked or (layer == 1 and not masked_last) else x_scr

        def finish(start, columns, weights):
            update = dot(att_scr[: 2 * rows, :], weights)
            for side in range(2):
                place = slice(side * features + start, side * features + start + columns)
                before = source[:, place]
                before = dot(pick_ref[...], before) if picked else before.astype(F32)
                target[:, place] = (before + update[rows * side : rows * (side + 1)]).astype(BF)

        last = (BLOCKS - 1) * BLOCK
        finish(0, BLOCK - rest, w_scr[layer, :, 3 * features : last])
        arrive(layer, BLOCKS - 1)
        finish(BLOCK - rest, BLOCK, w_scr[layer, :, last:])


def sublayers(masked_last, valid, place, x, gains, pick, spread, own, pieces):
    patches, width = x.shape
    features = width // 2
    out_rows = ROWS if masked_last else patches
    vmem = pl.BlockSpec(memory_space=pltpu.VMEM)
    smem = pl.BlockSpec(memory_space=pltpu.SMEM)
    return pl.pallas_call(
        functools.partial(sublayers_kernel, masked_last),
        in_specs=[smem, smem, vmem, vmem, vmem, vmem] + [pl.BlockSpec(memory_space=pl.ANY)] * 11,
        out_specs=vmem,
        out_shape=jax.ShapeDtypeStruct((out_rows, width), BF),
        scratch_shapes=[
            pltpu.VMEM((patches, width), BF),
            pltpu.VMEM((patches, 3 * features), BF),
            pltpu.VMEM((2 * patches, width), BF),
            pltpu.VMEM((2, width, 2 * width), BF),
            pltpu.SemaphoreType.DMA((BLOCKS,)),
            pltpu.SemaphoreType.DMA((2, 20)),
        ],
        compiler_params=pltpu.CompilerParams(vmem_limit_bytes=48 * 1024 * 1024),
        cost_estimate=pl.CostEstimate(
            flops=14 * 10**9, bytes_accessed=27 * 10**6, transcendentals=10**6
        ),
        name="sublayers",
    )(valid, place, x, gains, pick, spread, own, *pieces)


def gather_other(own, swap, chosen):
    column = lax.axis_index("dp")
    members = lax.axis_size("dp")
    core = column % 2
    half = own.shape[1] // 2
    cut = half // 2

    def pairs(first, second):
        found = []
        for device in range(members):
            x, y, c = device // 8, device // 2 % 4, device % 2
            ahead = (first, second) if c == 0 else (second, first)
            found.append((device, ((x + ahead[0]) % 4 * 4 + (y + ahead[1]) % 4) * 2 + c))
        return found

    def moved(value, first, second):
        return lax.ppermute(value, "dp", pairs(first, second))

    other_core = [(device, device ^ 1) for device in range(members)]
    keep = jnp.where(core == 0, own[:, :half], own[:, half:])
    give = jnp.where(core == 0, own[:, half:], own[:, :half])
    got = lax.ppermute(give, "dp", other_core)
    rows = jnp.concatenate(
        [jnp.where(core == 0, keep, got), jnp.where(core == 0, got, keep)], axis=0
    )
    rows = lax.ppermute(rows, "segment", swap)
    behind = moved(rows, 1, 0)
    ahead = moved(rows, -1, 0)
    across = jnp.concatenate(
        [moved(behind[:, :cut], 1, 0), moved(ahead[:, cut:], -1, 0)], axis=1
    )
    line = jnp.stack([rows, ahead, across, behind])
    line_behind = moved(line, 0, 1)
    line_ahead = moved(line, 0, -1)
    line_theirs = lax.ppermute(line, "dp", other_core)
    chosen, line_theirs = lax.optimization_barrier((chosen, line_theirs))
    chosen = lax.all_to_all(chosen, "dp", split_axis=1, concat_axis=0, tiled=True)
    chosen, line_behind, line_ahead = lax.optimization_barrier((chosen, line_behind, line_ahead))
    across_left = moved(line_behind[:, :, :cut], 0, 1)
    across_right = moved(line_ahead[:, :, cut:], 0, -1)
    mine = [line, line_ahead, line_behind, across_left, across_right]
    theirs = [line_theirs] + [lax.ppermute(piece, "dp", other_core) for piece in mine[1:]]

    x, y = column // 8, column // 2 % 4
    steps = jnp.arange(4, dtype=jnp.int32)
    x_first = 4 * ((x + steps[None, :]) % 4) + (y + steps[:, None]) % 4
    y_first = 4 * ((x + steps[:, None]) % 4) + (y + steps[None, :]) % 4
    chips = jnp.stack([jnp.where(core == 0, x_first, y_first), jnp.where(core == 0, y_first, x_first)])
    return mine + theirs, chips.reshape(-1) * rows.shape[0], chosen


def shards(
    teacher_in,
    teacher_qkv,
    teacher_out,
    teacher_gain,
    final_gain,
    projection,
    bucket,
    slot_image,
    mask_list,
    student_in,
    student_gain,
    w_gate,
    w_up,
    w_down,
):
    section = lax.axis_index("segment")
    column = lax.axis_index("dp")
    members = lax.axis_size("dp")
    images = bucket.shape[0]
    patches = teacher_in.shape[1]
    features = teacher_out.shape[2] // 2
    width = student_in.shape[-1]
    hidden_width = w_gate.shape[1]

    core = column % 2
    other_core = [(device, device ^ 1) for device in range(members)]

    def of_chip(own):
        other = lax.ppermute(own, "dp", other_core)
        first = jnp.where(core == 0, own, other)
        second = jnp.where(core == 0, other, own)
        return jnp.concatenate([first, second], axis=0)

    image_ids = jnp.arange(images, dtype=jnp.int32)
    positions = jnp.arange(patches, dtype=jnp.int32)
    slot_of = jnp.sum(
        jnp.where(slot_image[None, :] == image_ids[:, None], image_ids[None, :], 0), axis=1
    )
    listed = jnp.pad(mask_list, ((0, 0), (0, SENT_ROWS - mask_list.shape[1])))
    own_slots = lax.dynamic_slice_in_dim(listed, 2 * column, 2)
    own_pick = (own_slots[:, :, None] == positions[None, None, :]).astype(BF)
    chosen = jnp.einsum("srp,spf->srf", own_pick, student_in, preferred_element_type=F32).astype(BF)

    swap = [(0, 1), (1, 0), (2, 3), (3, 2)]
    upper = section % 2
    packed_own = jnp.concatenate(
        [
            teacher_qkv[0],
            jnp.concatenate([teacher_out[0, :, :features], teacher_out[0, :, features:]], axis=0),
        ],
        axis=1,
    )
    pieces, place, chosen = gather_other(packed_own, swap, chosen)
    place = jnp.concatenate([place, upper[None], core[None]]).astype(jnp.int32)
    packed = lax.all_gather(packed_own, "dp", axis=0, tiled=True)
    other_gain = lax.ppermute(teacher_gain, "segment", swap)
    gains = jnp.where(
        upper == 0,
        jnp.concatenate([teacher_gain, other_gain], axis=0),
        jnp.concatenate([other_gain, teacher_gain], axis=0),
    )

    chosen = jnp.take(chosen, slot_of, axis=0)
    chosen, token = after(chosen, pieces[3][0, 0, :1])
    chosen = lax.all_to_all(chosen, "dp", split_axis=0, concat_axis=1, tiled=True)
    place = jnp.concatenate([place, token.astype(jnp.int32)])

    my_slots = lax.dynamic_slice_in_dim(slot_of, 2 * column, 2)
    my_lists = jnp.take(listed[:, :ROWS], my_slots, axis=0)
    my_valid = valid_counts(lax.dynamic_slice_in_dim(bucket, 2 * column, 2))
    chip_count = 2 * valid_counts(lax.dynamic_slice_in_dim(bucket, 4 * (column // 2), 4)) // 5
    weights = jnp.where(
        jnp.arange(ROWS, dtype=jnp.int32)[None, :] < chip_count[:, None],
        1.0 / chip_count.astype(F32)[:, None],
        0.0,
    ).reshape(-1)

    which = jnp.where((section == 0) | (section == 3), 0, 1)
    image = lax.dynamic_index_in_dim(teacher_in, which, 0, keepdims=False)
    valid = lax.dynamic_slice_in_dim(my_valid, which, 1)
    my_list = lax.dynamic_index_in_dim(my_lists, which, 0, keepdims=False)
    pick = (my_list[:, None] == positions[None, :]).astype(BF)
    spread = spread_matrices()
    middle = sublayers(False, valid, place, image, gains, pick, spread, packed, pieces)
    chosen, last_token = after(chosen, middle[0, :1])
    place_after = jnp.concatenate([place, last_token.astype(jnp.int32)])
    chosen = of_chip(chosen[:, :ROWS])


    flat_rows = chosen.reshape(-1, width)
    normed = normalize(flat_rows.astype(F32), student_gain).astype(BF)
    gate_act = dot(normed, w_gate)
    up_act = dot(normed, w_up)
    gate_sig = jax.nn.sigmoid(gate_act)
    hidden = (gate_act * gate_sig * up_act).astype(BF)
    output = flat_rows.astype(F32) + dot(hidden, w_down)
    out_scale = lax.rsqrt(jnp.mean(output * output, axis=-1) + EPS)
    gate_factor = up_act * gate_sig * (1.0 + gate_act * (1.0 - gate_sig))
    up_factor = gate_act * gate_sig

    chips = members // 2

    def own_rows(columns, count):
        rows = lax.dynamic_slice_in_dim(columns, section * count, count, 1).T
        rows = rows.reshape(chips, 2, count // members, -1)
        return lax.dynamic_index_in_dim(rows, core, 1, keepdims=False)

    normed_rows = own_rows(normed, width // 4).reshape(8 * chips, -1)
    down_rows = own_rows(hidden, hidden_width // 4)
    down_each = hidden_width // 4 // members
    down_top = down_rows[:, :8].reshape(8 * chips, -1)
    down_rest = jnp.pad(down_rows[:, 8:], ((0, 0), (0, 16 - down_each), (0, 0)))
    down_rest = down_rest.reshape(8 * chips, -1)

    middle = lax.ppermute(middle, "segment", [(0, 3), (1, 2)])
    packed, projection = lax.optimization_barrier((packed, projection))
    proj_full = lax.all_gather(projection, "dp", axis=0, tiled=True)
    middle, output, out_scale, gate_factor, up_factor = lax.optimization_barrier(
        (middle, output, out_scale, gate_factor, up_factor)
    )
    last = sublayers(True, valid, place_after, middle, gains, pick, spread, packed, pieces)
    normed_last = normalize(last.astype(F32), final_gain).astype(BF)
    target = dot(normed_last, proj_full).astype(BF)

    swapped = lax.ppermute(target, "segment", [(2, 3), (3, 2)])
    near = lax.ppermute(target, "segment", [(3, 0), (2, 1)])
    far = lax.ppermute(target, "segment", [(3, 1), (2, 0)])
    upper_half = section >= 2
    one = jnp.where(upper_half, target, near)
    two = jnp.where(upper_half, swapped, far)
    goal = of_chip(jnp.where(which == 0, jnp.stack([one, two]), jnp.stack([two, one])))

    goal_rows = goal.reshape(-1, width).astype(F32)
    goal_scale = lax.rsqrt(jnp.mean(goal_rows * goal_rows, axis=-1) + EPS)
    inner_prod = jnp.sum(output * goal_rows, axis=-1)
    factor = -LOSS_SCALE * weights * goal_scale / width
    cubed = out_scale * out_scale * out_scale
    upstream = factor[:, None] * (
        out_scale[:, None] * goal_rows - (inner_prod * cubed / width)[:, None] * output
    )
    upstream = upstream.astype(BF)
    back_hidden = lax.dot_general(
        upstream, w_down, (((1,), (1,)), ((), ())), preferred_element_type=F32
    )
    gate_grad = (back_hidden * gate_factor).astype(BF)
    up_grad = (back_hidden * up_factor).astype(BF)
    terms = jnp.concatenate(
        [
            dot(normed_rows, gate_grad).astype(BF),
            dot(normed_rows, up_grad).astype(BF),
            dot(down_top, upstream).astype(BF),
            dot(down_rest, upstream).astype(BF),
        ],
        axis=1,
    ).reshape(chips, 8, -1)
    same_core = [list(range(0, members, 2)), list(range(1, members, 2))]
    terms = lax.all_to_all(
        terms, "dp", split_axis=0, concat_axis=0, tiled=True, axis_index_groups=same_core
    )
    summed = jnp.sum(terms.astype(F32), axis=0)
    cut = 2 * hidden_width
    grad_down = jnp.concatenate(
        [summed[:, cut : cut + width], summed[: down_each - 8, cut + width :]], axis=0
    )
    return summed[:, :hidden_width], summed[:, hidden_width:cut], grad_down


def solution(mesh):
    in_specs = (
        P("dp", None, None),
        P("segment", "dp", None),
        P("segment", "dp", None),
        P("segment", None),
        P(),
        P("dp", None),
        P(),
        P(),
        P(),
        P("dp", None, None),
        P(),
        P(),
        P(),
        P(),
    )
    out_specs = (P(("segment", "dp"), None), P(("segment", "dp"), None), P(("segment", "dp"), None))
    return jax.shard_map(shards, mesh=mesh, in_specs=in_specs, out_specs=out_specs, check_vma=False)
```

```python
import functools

import jax
import jax.numpy as jnp
import ml_dtypes
import numpy as np
from jax import lax
from jax.experimental import pallas as pl
from jax.experimental.pallas import tpu as pltpu
from jax.sharding import PartitionSpec as P

HD = 112
SIDE = 16
EPS = 1e-06
LOSS_SCALE = 4096.0

ROWS = 112
SENT_ROWS = 128
BLOCK = 512
BLOCKS = 7
WINDOW = 256
QUARTER = 28
GROUP = 4
BF = jnp.bfloat16
F32 = jnp.float32


def normalize(values_in, gain):
    centred = values_in - jnp.mean(values_in, axis=-1, keepdims=True)
    return centred * lax.rsqrt(jnp.mean(centred * centred, axis=-1, keepdims=True) + EPS) * gain


def valid_counts(bucket_ids):
    side_len = SIDE - 2 * bucket_ids
    return side_len * side_len


def head_window(head):
    first = head * HD // 128 * 128
    first = min(first, 8 * HD - WINDOW)
    return first, head * HD - first


def spread_window(head):
    start = 2 * HD * (head % GROUP)
    first = start // 128 * 128
    return first, start - first, -(-(start + 2 * HD - first) // 128) * 128


def spread_matrices():
    sides = np.zeros((16, WINDOW, 384), ml_dtypes.bfloat16)
    for head in range(8):
        _, offset = head_window(head)
        _, lane_offset, _ = spread_window(head)
        for place in range(HD):
            target = lane_offset + place + QUARTER * (place // QUARTER)
            for side in range(2):
                sides[2 * head + side, offset + place, target + QUARTER * side] = 1.0
    return jnp.asarray(sides)


def dot(a, b):
    return jnp.dot(a, b, preferred_element_type=F32)


def teacher_kernel(
    valid_ref, x_ref, gain_ref, final_ref, pick_ref, spread_ref, w_hbm,
    out_ref, x_scr, qkv_scr, att_scr, last_scr, w_scr, proj_scr, sems, proj_sems,
):
    layers = gain_ref.shape[0]
    patches, width = x_ref.shape
    features = width // 2
    heads = features // HD
    copies = [
        pltpu.make_async_copy(
            w_hbm.at[pl.ds(layer * width, width), pl.ds(BLOCK * block, BLOCK)],
            w_scr.at[layer % 2 * BLOCKS + block],
            sems.at[layer * BLOCKS + block],
        )
        for layer in range(layers)
        for block in range(BLOCKS)
    ]
    share = proj_scr.shape[1] // layers
    proj_copies = [
        pltpu.make_async_copy(
            w_hbm.at[pl.ds(layer * width, width), pl.ds(BLOCK * BLOCKS, share)],
            proj_scr.at[:, pl.ds(layer * share, share)],
            proj_sems.at[layer],
        )
        for layer in range(layers)
    ]
    for copy in copies[: 2 * BLOCKS]:
        copy.start()

    def attend(picked):
        rows = ROWS if picked else patches
        lane = lax.broadcasted_iota(jnp.int32, (1, WINDOW), 1)
        live = lax.broadcasted_iota(jnp.int32, (1, patches), 1) < valid_ref[0]
        for group in range(heads // GROUP):
            members = range(group * GROUP, (group + 1) * GROUP)
            scores = []
            for head in members:
                first, offset = head_window(head)
                q = qkv_scr[:, first : first + WINDOW]
                k = qkv_scr[:, features + first : features + first + WINDOW]
                if picked:
                    q = dot(pick_ref[...], q).astype(BF)
                q = jnp.where((lane >= offset) & (lane < offset + HD), q, jnp.zeros_like(q))
                scores.append(
                    lax.dot_general(q, k, (((1,), (1,)), ((), ())), preferred_element_type=F32)
                )
            attended = []
            for head, score in zip(members, scores):
                first, _ = head_window(head)
                v = qkv_scr[:, 2 * features + first : 2 * features + first + WINDOW]
                score = jnp.where(live, score * HD ** (-0.5), -jnp.inf)
                weights = jnp.exp(score - jnp.max(score, axis=-1, keepdims=True))
                probs = (weights * (1.0 / jnp.sum(weights, axis=-1, keepdims=True))).astype(BF)
                attended.append(dot(probs, v).astype(BF))
            for side in range(2):
                tiles = [[] for _ in range(GROUP * 2 * HD // 128)]
                for head, att in zip(members, attended):
                    first, _, wide = spread_window(head)
                    spread = dot(att, spread_ref[2 * head + side, :, :wide])
                    for tile in range(wide // 128):
                        tiles[first // 128 + tile].append(spread[:, tile * 128 : tile * 128 + 128])
                for tile, parts in enumerate(tiles):
                    start = GROUP * 2 * HD * group + 128 * tile
                    att_scr[rows * side : rows * (side + 1), start : start + 128] = sum(
                        parts[1:], parts[0]
                    ).astype(BF)

    for layer in range(layers):
        base = layer * BLOCKS
        slot = layer % 2 * BLOCKS
        picked = layer == layers - 1
        rows = ROWS if picked else patches
        source = x_ref if layer == 0 else x_scr
        target = last_scr if picked else x_scr
        h = normalize(source[...].astype(F32), gain_ref[layer : layer + 1, :]).astype(BF)
        for block in range(BLOCKS - 2):
            copies[base + block].wait()
            qkv_scr[:, block * BLOCK : (block + 1) * BLOCK] = dot(h, w_scr[slot + block]).astype(BF)
        rest = 3 * features - (BLOCKS - 2) * BLOCK
        copies[base + BLOCKS - 2].wait()
        qkv_scr[:, 3 * features - rest :] = dot(h, w_scr[slot + BLOCKS - 2, :, :rest]).astype(BF)
        if layer + 2 < layers:
            for copy in copies[base + 2 * BLOCKS : base + 3 * BLOCKS - 2]:
                copy.start()
        attend(picked)

        def finish(start, columns, weights):
            update = dot(att_scr[: 2 * rows, :], weights)
            for side in range(2):
                place = slice(side * features + start, side * features + start + columns)
                before = source[:, place]
                before = dot(pick_ref[...], before) if picked else before.astype(F32)
                target[:, place] = (before + update[rows * side : rows * (side + 1)]).astype(BF)

        finish(0, BLOCK - rest, w_scr[slot + BLOCKS - 2, :, rest:])
        copies[base + BLOCKS - 1].wait()
        finish(BLOCK - rest, BLOCK, w_scr[slot + BLOCKS - 1])
        if layer + 2 < layers:
            for copy in copies[base + 3 * BLOCKS - 2 : base + 3 * BLOCKS]:
                copy.start()
        if layer == layers - 2:
            for copy in proj_copies:
                copy.start()

    feats = normalize(last_scr[...].astype(F32), final_ref[...]).astype(BF)
    for copy in proj_copies:
        copy.wait()
    out_ref[...] = dot(feats, proj_scr[...]).astype(BF)


def teacher(valid, x, gains, final_gain, pick, spread, packed):
    patches, width = x.shape
    layers = gains.shape[0]
    goal_width = (packed.shape[1] - BLOCK * BLOCKS) * layers
    vmem = pl.BlockSpec(memory_space=pltpu.VMEM)
    return pl.pallas_call(
        teacher_kernel,
        in_specs=[pl.BlockSpec(memory_space=pltpu.SMEM)]
        + [vmem] * 5
        + [pl.BlockSpec(memory_space=pl.ANY)],
        out_specs=vmem,
        out_shape=jax.ShapeDtypeStruct((ROWS, goal_width), BF),
        scratch_shapes=[
            pltpu.VMEM((patches, width), BF),
            pltpu.VMEM((patches, 3 * width // 2), BF),
            pltpu.VMEM((2 * patches, width), BF),
            pltpu.VMEM((ROWS, width), BF),
            pltpu.VMEM((2 * BLOCKS, width, BLOCK), BF),
            pltpu.VMEM((width, goal_width), BF),
            pltpu.SemaphoreType.DMA((layers * BLOCKS,)),
            pltpu.SemaphoreType.DMA((layers,)),
        ],
        compiler_params=pltpu.CompilerParams(vmem_limit_bytes=52 * 1024 * 1024),
        cost_estimate=pl.CostEstimate(
            flops=28 * 10**9, bytes_accessed=55 * 10**6, transcendentals=2 * 10**6
        ),
        name="teacher",
    )(valid, x, gains, final_gain, pick, spread, packed)


def shards(
    teacher_in,
    teacher_qkv,
    teacher_out,
    teacher_gain,
    final_gain,
    projection,
    bucket,
    slot_image,
    mask_list,
    student_in,
    student_gain,
    w_gate,
    w_up,
    w_down,
):
    section = lax.axis_index("segment")
    column = lax.axis_index("dp")
    members = lax.axis_size("dp")
    images = bucket.shape[0]
    patches = teacher_in.shape[1]
    features = teacher_out.shape[2] // 2
    width = student_in.shape[-1]
    hidden_width = w_gate.shape[1]

    sections = lax.axis_size("segment")
    share = projection.shape[1] // sections
    packed = jnp.concatenate(
        [
            teacher_qkv[0],
            jnp.concatenate([teacher_out[0, :, :features], teacher_out[0, :, features:]], axis=0),
            lax.dynamic_slice_in_dim(projection, section * share, share, 1),
        ],
        axis=1,
    )
    packed = lax.all_gather(packed, ("segment", "dp"), axis=0, tiled=True)

    def around(value, step):
        pairs = [((i + step) % sections, i) for i in range(sections)]
        return lax.ppermute(value, "segment", pairs)

    def by_plane(cycle):
        return jnp.select(
            [section == i for i in range(sections)],
            [jnp.roll(cycle, i, axis=0) for i in range(sections)],
        )

    gains = by_plane(
        jnp.concatenate([teacher_gain] + [around(teacher_gain, i) for i in range(1, sections)], axis=0)
    )

    core = column % 2
    other_core = [(device, device ^ 1) for device in range(members)]

    def of_chip(own):
        other = lax.ppermute(own, "dp", other_core)
        first = jnp.where(core == 0, own, other)
        second = jnp.where(core == 0, other, own)
        return jnp.concatenate([first, second], axis=0)

    image_ids = jnp.arange(images, dtype=jnp.int32)
    positions = jnp.arange(patches, dtype=jnp.int32)
    slot_of = jnp.sum(
        jnp.where(slot_image[None, :] == image_ids[:, None], image_ids[None, :], 0), axis=1
    )
    listed = jnp.pad(mask_list, ((0, 0), (0, SENT_ROWS - mask_list.shape[1])))
    own_slots = lax.dynamic_slice_in_dim(listed, 2 * column, 2)
    own_pick = (own_slots[:, :, None] == positions[None, None, :]).astype(BF)
    chosen = jnp.einsum("srp,spf->srf", own_pick, student_in, preferred_element_type=F32).astype(BF)
    chosen = lax.all_to_all(chosen, "dp", split_axis=1, concat_axis=0, tiled=True)
    chosen = jnp.take(chosen, slot_of, axis=0)
    chosen = lax.all_to_all(chosen, "dp", split_axis=0, concat_axis=1, tiled=True)
    chosen = of_chip(chosen[:, :ROWS])
    holder, which = section // 2, section % 2
    held = lax.dynamic_index_in_dim(teacher_in, which, 0, keepdims=False)
    image = jnp.where(core == holder, held, lax.ppermute(held, "dp", other_core))
    image_id = 4 * (column // 2) + section
    my_list = lax.dynamic_index_in_dim(
        listed[:, :ROWS], lax.dynamic_index_in_dim(slot_of, image_id, 0, keepdims=False), 0, False
    )
    valid = valid_counts(lax.dynamic_slice_in_dim(bucket, image_id, 1))
    pick = (my_list[:, None] == positions[None, :]).astype(BF)
    chip_count = 2 * valid_counts(lax.dynamic_slice_in_dim(bucket, 4 * (column // 2), 4)) // 5
    weights = jnp.where(
        jnp.arange(ROWS, dtype=jnp.int32)[None, :] < chip_count[:, None],
        1.0 / chip_count.astype(F32)[:, None],
        0.0,
    ).reshape(-1)

    flat_rows = chosen.reshape(-1, width)
    normed = normalize(flat_rows.astype(F32), student_gain).astype(BF)
    gate_act = dot(normed, w_gate)
    up_act = dot(normed, w_up)
    gate_sig = jax.nn.sigmoid(gate_act)
    hidden = (gate_act * gate_sig * up_act).astype(BF)
    output = flat_rows.astype(F32) + dot(hidden, w_down)
    out_scale = lax.rsqrt(jnp.mean(output * output, axis=-1) + EPS)
    gate_factor = up_act * gate_sig * (1.0 + gate_act * (1.0 - gate_sig))
    up_factor = gate_act * gate_sig

    chips = members // 2

    def own_rows(columns, count):
        rows = lax.dynamic_slice_in_dim(columns, section * count, count, 1).T
        rows = rows.reshape(chips, 2, count // members, -1)
        return lax.dynamic_index_in_dim(rows, core, 1, keepdims=False)

    normed_rows = own_rows(normed, width // 4).reshape(8 * chips, -1)
    down_rows = own_rows(hidden, hidden_width // 4)
    down_each = hidden_width // 4 // members
    down_top = down_rows[:, :8].reshape(8 * chips, -1)
    down_rest = jnp.pad(down_rows[:, 8:], ((0, 0), (0, 16 - down_each), (0, 0)))
    down_rest = down_rest.reshape(8 * chips, -1)
    spread = spread_matrices()

    (
        packed, gains, image, pick, spread,
        output, out_scale, gate_factor, up_factor, normed_rows, down_top, down_rest,
    ) = lax.optimization_barrier(
        (
            packed, gains, image, pick, spread,
            output, out_scale, gate_factor, up_factor, normed_rows, down_top, down_rest,
        )
    )
    target = teacher(valid, image, gains, final_gain[None, :], pick, spread, packed)

    kept = ROWS // 2
    half = lax.dynamic_slice_in_dim(target, core * kept, kept)

    halves = jnp.stack([around(half, i) for i in range(1, sections)])
    theirs = lax.ppermute(halves, "dp", other_core)
    others = jnp.where(
        core == 0,
        jnp.concatenate([halves, theirs], axis=1),
        jnp.concatenate([theirs, halves], axis=1),
    )
    goal = by_plane(jnp.concatenate([target[None], others], axis=0))

    goal_rows = goal.reshape(-1, width).astype(F32)
    goal_scale = lax.rsqrt(jnp.mean(goal_rows * goal_rows, axis=-1) + EPS)
    inner_prod = jnp.sum(output * goal_rows, axis=-1)
    factor = -LOSS_SCALE * weights * goal_scale / width
    cubed = out_scale * out_scale * out_scale
    upstream = factor[:, None] * (
        out_scale[:, None] * goal_rows - (inner_prod * cubed / width)[:, None] * output
    )
    upstream = upstream.astype(BF)
    back_hidden = lax.dot_general(
        upstream, w_down, (((1,), (1,)), ((), ())), preferred_element_type=F32
    )
    gate_grad = (back_hidden * gate_factor).astype(BF)
    up_grad = (back_hidden * up_factor).astype(BF)
    terms = jnp.concatenate(
        [
            dot(normed_rows, gate_grad).astype(BF),
            dot(normed_rows, up_grad).astype(BF),
            dot(down_top, upstream).astype(BF),
            dot(down_rest, upstream).astype(BF),
        ],
        axis=1,
    ).reshape(chips, 8, -1)
    same_core = [list(range(0, members, 2)), list(range(1, members, 2))]
    terms = lax.all_to_all(
        terms, "dp", split_axis=0, concat_axis=0, tiled=True, axis_index_groups=same_core
    )
    summed = jnp.sum(terms.astype(F32), axis=0)
    cut = 2 * hidden_width
    grad_down = jnp.concatenate(
        [summed[:, cut : cut + width], summed[: down_each - 8, cut + width :]], axis=0
    )
    return summed[:, :hidden_width], summed[:, hidden_width:cut], grad_down


def solution(mesh):
    in_specs = (
        P("dp", None, None),
        P("segment", "dp", None),
        P("segment", "dp", None),
        P("segment", None),
        P(),
        P("dp", None),
        P(),
        P(),
        P(),
        P("dp", None, None),
        P(),
        P(),
        P(),
        P(),
    )
    out_specs = (P(("segment", "dp"), None), P(("segment", "dp"), None), P(("segment", "dp"), None))
    return jax.shard_map(shards, mesh=mesh, in_specs=in_specs, out_specs=out_specs, check_vma=False)
```

```python
import functools

import jax
import jax.numpy as jnp
import ml_dtypes
import numpy as np
from jax import lax
from jax.experimental import pallas as pl
from jax.experimental.pallas import tpu as pltpu
from jax.sharding import PartitionSpec as P

HD = 112
SIDE = 16
EPS = 1e-06
LOSS_SCALE = 4096.0

ROWS = 112
SENT_ROWS = 128
BLOCK = 512
BLOCKS = 7
WINDOW = 256
QUARTER = 28
GROUP = 4
BF = jnp.bfloat16
F32 = jnp.float32


def normalize(values_in, gain):
    centred = values_in - jnp.mean(values_in, axis=-1, keepdims=True)
    return centred * lax.rsqrt(jnp.mean(centred * centred, axis=-1, keepdims=True) + EPS) * gain


def valid_counts(bucket_ids):
    side_len = SIDE - 2 * bucket_ids
    return side_len * side_len


def head_window(head):
    first = head * HD // 128 * 128
    first = min(first, 8 * HD - WINDOW)
    return first, head * HD - first


def spread_window(head):
    start = 2 * HD * (head % GROUP)
    first = start // 128 * 128
    return first, start - first, -(-(start + 2 * HD - first) // 128) * 128


def spread_matrices():
    sides = np.zeros((16, WINDOW, 384), ml_dtypes.bfloat16)
    for head in range(8):
        _, offset = head_window(head)
        _, lane_offset, _ = spread_window(head)
        for place in range(HD):
            target = lane_offset + place + QUARTER * (place // QUARTER)
            for side in range(2):
                sides[2 * head + side, offset + place, target + QUARTER * side] = 1.0
    return jnp.asarray(sides)


def dot(a, b):
    return jnp.dot(a, b, preferred_element_type=F32)


def sublayers_kernel(
    masked_last, valid_ref, x_ref, gain_ref, pick_ref, spread_ref, w_hbm,
    out_ref, x_scr, qkv_scr, att_scr, w_scr, sems,
):
    patches, width = x_ref.shape
    features = width // 2
    heads = features // HD
    copies = [
        pltpu.make_async_copy(
            w_hbm.at[:, pl.ds(BLOCK * i, BLOCK)], w_scr.at[i], sems.at[i]
        )
        for i in range(2 * BLOCKS)
    ]
    for copy in copies:
        copy.start()

    def attend(picked):
        rows = ROWS if picked else patches
        lane = lax.broadcasted_iota(jnp.int32, (1, WINDOW), 1)
        live = lax.broadcasted_iota(jnp.int32, (1, patches), 1) < valid_ref[0]
        for group in range(heads // GROUP):
            members = range(group * GROUP, (group + 1) * GROUP)
            scores = []
            for head in members:
                first, offset = head_window(head)
                q = qkv_scr[:, first : first + WINDOW]
                k = qkv_scr[:, features + first : features + first + WINDOW]
                if picked:
                    q = dot(pick_ref[...], q).astype(BF)
                q = jnp.where((lane >= offset) & (lane < offset + HD), q, jnp.zeros_like(q))
                scores.append(
                    lax.dot_general(q, k, (((1,), (1,)), ((), ())), preferred_element_type=F32)
                )
            attended = []
            for head, score in zip(members, scores):
                first, _ = head_window(head)
                v = qkv_scr[:, 2 * features + first : 2 * features + first + WINDOW]
                score = jnp.where(live, score * HD ** (-0.5), -jnp.inf)
                weights = jnp.exp(score - jnp.max(score, axis=-1, keepdims=True))
                probs = (weights * (1.0 / jnp.sum(weights, axis=-1, keepdims=True))).astype(BF)
                attended.append(dot(probs, v).astype(BF))
            for side in range(2):
                tiles = [[] for _ in range(GROUP * 2 * HD // 128)]
                for head, att in zip(members, attended):
                    first, _, wide = spread_window(head)
                    spread = dot(att, spread_ref[2 * head + side, :, :wide])
                    for tile in range(wide // 128):
                        tiles[first // 128 + tile].append(spread[:, tile * 128 : tile * 128 + 128])
                for tile, parts in enumerate(tiles):
                    start = GROUP * 2 * HD * group + 128 * tile
                    att_scr[rows * side : rows * (side + 1), start : start + 128] = sum(
                        parts[1:], parts[0]
                    ).astype(BF)

    for layer in range(2):
        base = layer * BLOCKS
        picked = masked_last and layer == 1
        rows = ROWS if picked else patches
        source = x_ref if layer == 0 else x_scr
        h = normalize(source[...].astype(F32), gain_ref[layer : layer + 1, :]).astype(BF)
        for block in range(BLOCKS - 2):
            copies[base + block].wait()
            qkv_scr[:, block * BLOCK : (block + 1) * BLOCK] = dot(h, w_scr[base + block]).astype(BF)
        rest = 3 * features - (BLOCKS - 2) * BLOCK
        copies[base + BLOCKS - 2].wait()
        qkv_scr[:, 3 * features - rest :] = dot(h, w_scr[base + BLOCKS - 2, :, :rest]).astype(BF)
        attend(picked)
        target = out_ref if picked or (layer == 1 and not masked_last) else x_scr

        def finish(start, columns, weights):
            update = dot(att_scr[: 2 * rows, :], weights)
            for side in range(2):
                place = slice(side * features + start, side * features + start + columns)
                before = source[:, place]
                before = dot(pick_ref[...], before) if picked else before.astype(F32)
                target[:, place] = (before + update[rows * side : rows * (side + 1)]).astype(BF)

        finish(0, BLOCK - rest, w_scr[base + BLOCKS - 2, :, rest:])
        copies[base + BLOCKS - 1].wait()
        finish(BLOCK - rest, BLOCK, w_scr[base + BLOCKS - 1])


def sublayers(masked_last, valid, x, gains, pick, spread, packed):
    patches, width = x.shape
    features = width // 2
    out_rows = ROWS if masked_last else patches
    vmem = pl.BlockSpec(memory_space=pltpu.VMEM)
    return pl.pallas_call(
        functools.partial(sublayers_kernel, masked_last),
        in_specs=[
            pl.BlockSpec(memory_space=pltpu.SMEM),
            vmem,
            vmem,
            vmem,
            vmem,
            pl.BlockSpec(memory_space=pl.ANY),
        ],
        out_specs=vmem,
        out_shape=jax.ShapeDtypeStruct((out_rows, width), BF),
        scratch_shapes=[
            pltpu.VMEM((patches, width), BF),
            pltpu.VMEM((patches, 3 * features), BF),
            pltpu.VMEM((2 * patches, width), BF),
            pltpu.VMEM((2 * BLOCKS, width, BLOCK), BF),
            pltpu.SemaphoreType.DMA((2 * BLOCKS,)),
        ],
        compiler_params=pltpu.CompilerParams(vmem_limit_bytes=48 * 1024 * 1024),
        cost_estimate=pl.CostEstimate(
            flops=14 * 10**9, bytes_accessed=27 * 10**6, transcendentals=10**6
        ),
        name="sublayers",
    )(valid, x, gains, pick, spread, packed)


def backward_kernel(
    goal_ref, output_ref, weight_ref, down_ref, gate_ref, up_ref, normed_ref, top_ref, rest_ref, out_ref
):
    width = output_ref.shape[1]
    hidden_width = gate_ref.shape[1]
    goal = goal_ref[...].astype(F32)
    output = output_ref[...]
    out_scale = lax.rsqrt(jnp.mean(output * output, axis=-1, keepdims=True) + EPS)
    goal_scale = lax.rsqrt(jnp.mean(goal * goal, axis=-1, keepdims=True) + EPS)
    inner_prod = jnp.sum(output * goal, axis=-1, keepdims=True)
    factor = -LOSS_SCALE * weight_ref[...] * goal_scale / width
    cubed = out_scale * out_scale * out_scale
    upstream = factor * (out_scale * goal - (inner_prod * cubed / width) * output)
    upstream = upstream.astype(BF)
    start = 2 * hidden_width
    out_ref[:, start : start + width] = dot(top_ref[...], upstream).astype(BF)
    out_ref[:, start + width :] = dot(rest_ref[...], upstream).astype(BF)
    for first in range(0, hidden_width, BLOCK):
        last = min(first + BLOCK, hidden_width)
        back_hidden = lax.dot_general(
            upstream,
            down_ref[first:last, :],
            (((1,), (1,)), ((), ())),
            preferred_element_type=F32,
        )
        gate_grad = (back_hidden * gate_ref[:, first:last]).astype(BF)
        up_grad = (back_hidden * up_ref[:, first:last]).astype(BF)
        out_ref[:, first:last] = dot(normed_ref[...], gate_grad).astype(BF)
        out_ref[:, hidden_width + first : hidden_width + last] = dot(
            normed_ref[...], up_grad
        ).astype(BF)


def backward(goal, output, weights, w_down, gate_factor, up_factor, normed_rows, top, rest):
    vmem = pl.BlockSpec(memory_space=pltpu.VMEM)
    columns = 2 * gate_factor.shape[1] + 2 * output.shape[1]
    return pl.pallas_call(
        backward_kernel,
        in_specs=[vmem] * 9,
        out_specs=vmem,
        out_shape=jax.ShapeDtypeStruct((normed_rows.shape[0], columns), BF),
        compiler_params=pltpu.CompilerParams(vmem_limit_bytes=40 * 1024 * 1024),
        cost_estimate=pl.CostEstimate(flops=3 * 10**9, bytes_accessed=12 * 10**6, transcendentals=1000),
        name="backward",
    )(goal, output, weights, w_down, gate_factor, up_factor, normed_rows, top, rest)


def shards(
    teacher_in,
    teacher_qkv,
    teacher_out,
    teacher_gain,
    final_gain,
    projection,
    bucket,
    slot_image,
    mask_list,
    student_in,
    student_gain,
    w_gate,
    w_up,
    w_down,
):
    section = lax.axis_index("segment")
    column = lax.axis_index("dp")
    members = lax.axis_size("dp")
    images = bucket.shape[0]
    patches = teacher_in.shape[1]
    features = teacher_out.shape[2] // 2
    width = student_in.shape[-1]
    hidden_width = w_gate.shape[1]

    def both_layers(own):
        near = lax.ppermute(own, "segment", [(1, 0), (2, 3)])
        next_to = lax.ppermute(own, "segment", [(1, 2), (2, 1)])
        across = lax.ppermute(own, "segment", [(0, 2), (3, 1)])
        planes = [section == plane for plane in range(3)]
        lower = jnp.select(planes, [own, next_to, across], near)
        upper = jnp.select(planes, [near, across, next_to], own)
        return lower, upper

    packed = jnp.concatenate(
        [
            teacher_qkv[0],
            jnp.concatenate([teacher_out[0, :, :features], teacher_out[0, :, features:]], axis=0),
        ],
        axis=1,
    )
    packed = jnp.concatenate(both_layers(packed), axis=1)
    packed = lax.all_gather(packed, "dp", axis=0, tiled=True)
    gains = jnp.concatenate(both_layers(teacher_gain), axis=0)

    core = column % 2
    other_core = [(device, device ^ 1) for device in range(members)]

    def of_chip(own):
        other = lax.ppermute(own, "dp", other_core)
        first = jnp.where(core == 0, own, other)
        second = jnp.where(core == 0, other, own)
        return jnp.concatenate([first, second], axis=0)

    image_ids = jnp.arange(images, dtype=jnp.int32)
    positions = jnp.arange(patches, dtype=jnp.int32)
    slot_of = jnp.sum(
        jnp.where(slot_image[None, :] == image_ids[:, None], image_ids[None, :], 0), axis=1
    )
    listed = jnp.pad(mask_list, ((0, 0), (0, SENT_ROWS - mask_list.shape[1])))
    own_slots = lax.dynamic_slice_in_dim(listed, 2 * column, 2)
    own_pick = (own_slots[:, :, None] == positions[None, None, :]).astype(BF)
    chosen = jnp.einsum("srp,spf->srf", own_pick, student_in, preferred_element_type=F32).astype(BF)
    chosen = lax.all_to_all(chosen, "dp", split_axis=1, concat_axis=0, tiled=True)
    chosen = jnp.take(chosen, slot_of, axis=0)
    chosen = lax.all_to_all(chosen, "dp", split_axis=0, concat_axis=1, tiled=True)
    chosen = of_chip(chosen[:, :ROWS])
    my_slots = lax.dynamic_slice_in_dim(slot_of, 2 * column, 2)
    my_lists = jnp.take(listed[:, :ROWS], my_slots, axis=0)
    my_valid = valid_counts(lax.dynamic_slice_in_dim(bucket, 2 * column, 2))
    chip_count = 2 * valid_counts(lax.dynamic_slice_in_dim(bucket, 4 * (column // 2), 4)) // 5
    weights = jnp.where(
        jnp.arange(ROWS, dtype=jnp.int32)[None, :] < chip_count[:, None],
        1.0 / chip_count.astype(F32)[:, None],
        0.0,
    ).reshape(-1)

    flat_rows = chosen.reshape(-1, width)
    normed = normalize(flat_rows.astype(F32), student_gain).astype(BF)
    gate_act = dot(normed, w_gate)
    up_act = dot(normed, w_up)
    gate_sig = jax.nn.sigmoid(gate_act)
    hidden = (gate_act * gate_sig * up_act).astype(BF)
    output = flat_rows.astype(F32) + dot(hidden, w_down)
    gate_factor = up_act * gate_sig * (1.0 + gate_act * (1.0 - gate_sig))
    up_factor = gate_act * gate_sig

    chips = members // 2

    def own_rows(columns, count):
        rows = lax.dynamic_slice_in_dim(columns, section * count, count, 1).T
        rows = rows.reshape(chips, 2, count // members, -1)
        return lax.dynamic_index_in_dim(rows, core, 1, keepdims=False)

    normed_rows = own_rows(normed, width // 4).reshape(8 * chips, -1)
    down_rows = own_rows(hidden, hidden_width // 4)
    down_each = hidden_width // 4 // members
    down_top = down_rows[:, :8].reshape(8 * chips, -1)
    down_rest = jnp.pad(down_rows[:, 8:], ((0, 0), (0, 16 - down_each), (0, 0)))
    down_rest = down_rest.reshape(8 * chips, -1)
    spread = spread_matrices()

    packed, spread, output, gate_factor, up_factor, normed_rows, down_top, down_rest = (
        lax.optimization_barrier(
            (packed, spread, output, gate_factor, up_factor, normed_rows, down_top, down_rest)
        )
    )

    which = jnp.select([section == 0, section == 1, section == 2], [0, core, 1], 1 - core)
    hop = []
    for device in range(members):
        same, other = device, 2 * members + device
        hop += [(same, (1 + 2 * (device % 2)) * members + device)]
        hop += [(other, (3 - 2 * (device % 2)) * members + device)]
    image = lax.dynamic_index_in_dim(teacher_in, which, 0, keepdims=False)
    valid = lax.dynamic_slice_in_dim(my_valid, which, 1)
    my_list = lax.dynamic_index_in_dim(my_lists, which, 0, keepdims=False)
    pick = (my_list[:, None] == positions[None, :]).astype(BF)
    middle = sublayers(False, valid, image, gains, pick, spread, packed)
    middle = lax.ppermute(middle, ("segment", "dp"), hop)
    packed, projection = lax.optimization_barrier((packed, projection))
    proj_full = lax.all_gather(projection, "dp", axis=0, tiled=True)
    last = sublayers(True, valid, middle, gains, pick, spread, packed)
    normed_last = normalize(last.astype(F32), final_gain).astype(BF)
    target = dot(normed_last, proj_full).astype(BF)

    first_way = lax.ppermute(target, "segment", [(1, 0), (3, 2)])
    second_way = lax.ppermute(target, "segment", [(3, 0), (1, 2)])
    swapped = lax.ppermute(target, "segment", [(1, 3), (3, 1)])
    planes = [section == plane for plane in range(3)]
    of_one = jnp.select(planes, [first_way, target, second_way], swapped)
    of_three = jnp.select(planes, [second_way, swapped, first_way], target)
    goal = jnp.where(core == 0, jnp.stack([of_one, of_three]), jnp.stack([of_three, of_one]))
    goal = of_chip(goal)

    terms = backward(
        goal.reshape(-1, width), output, weights[:, None], w_down,
        gate_factor, up_factor, normed_rows, down_top, down_rest,
    ).reshape(chips, 8, -1)
    same_core = [list(range(0, members, 2)), list(range(1, members, 2))]
    terms = lax.all_to_all(
        terms, "dp", split_axis=0, concat_axis=0, tiled=True, axis_index_groups=same_core
    )
    summed = jnp.sum(terms.astype(F32), axis=0)
    cut = 2 * hidden_width
    grad_down = jnp.concatenate(
        [summed[:, cut : cut + width], summed[: down_each - 8, cut + width :]], axis=0
    )
    return summed[:, :hidden_width], summed[:, hidden_width:cut], grad_down


def solution(mesh):
    in_specs = (
        P("dp", None, None),
        P("segment", "dp", None),
        P("segment", "dp", None),
        P("segment", None),
        P(),
        P("dp", None),
        P(),
        P(),
        P(),
        P("dp", None, None),
        P(),
        P(),
        P(),
        P(),
    )
    out_specs = (P(("segment", "dp"), None), P(("segment", "dp"), None), P(("segment", "dp"), None))
    return jax.shard_map(shards, mesh=mesh, in_specs=in_specs, out_specs=out_specs, check_vma=False)
```

```python
import functools

import jax
import jax.numpy as jnp
from jax import lax
from jax.experimental import pallas as pl
from jax.experimental.pallas import tpu as pltpu
from jax.sharding import PartitionSpec as P

HD = 112
SIDE = 16
EPS = 1e-06
LOSS_SCALE = 4096.0

ROWS = 112
SENT_ROWS = 128
BLOCK = 512
BLOCKS = 7
WINDOW = 256
QUARTER = 28
GROUP = 4
BF = jnp.bfloat16
F32 = jnp.float32


def normalize(values_in, gain):
    centred = values_in - jnp.mean(values_in, axis=-1, keepdims=True)
    return centred * lax.rsqrt(jnp.mean(centred * centred, axis=-1, keepdims=True) + EPS) * gain


def valid_counts(bucket_ids):
    side_len = SIDE - 2 * bucket_ids
    return side_len * side_len


def head_window(head):
    first = head * HD // 128 * 128
    first = min(first, 8 * HD - WINDOW)
    return first, head * HD - first


def spread_window(head):
    start = 2 * HD * (head % GROUP)
    first = start // 128 * 128
    return first, start - first, -(-(start + 2 * HD - first) // 128) * 128


def spread_matrices():
    feature = jnp.arange(WINDOW, dtype=jnp.int32)[:, None]
    lane = jnp.arange(384, dtype=jnp.int32)[None, :]
    sides = []
    for head in range(8):
        _, offset = head_window(head)
        _, lane_offset, _ = spread_window(head)
        place = feature - offset
        owner = sum((place >= QUARTER * i).astype(jnp.int32) for i in range(1, GROUP))
        target = lane_offset + place + QUARTER * owner
        inside = (place >= 0) & (place < HD)
        for side in range(2):
            sides.append((inside & (lane == target + QUARTER * side)).astype(BF))
    return jnp.stack(sides)


def dot(a, b):
    return jnp.dot(a, b, preferred_element_type=F32)


def sublayers_kernel(
    masked_last, valid_ref, x_ref, gain_ref, pick_ref, spread_ref, w_hbm,
    out_ref, x_scr, qkv_scr, att_scr, w_scr, sems,
):
    patches, width = x_ref.shape
    features = width // 2
    heads = features // HD
    copies = [
        pltpu.make_async_copy(
            w_hbm.at[:, pl.ds(BLOCK * i, BLOCK)], w_scr.at[i], sems.at[i]
        )
        for i in range(2 * BLOCKS)
    ]
    for copy in copies:
        copy.start()

    def attend(picked):
        rows = ROWS if picked else patches
        lane = lax.broadcasted_iota(jnp.int32, (1, WINDOW), 1)
        live = lax.broadcasted_iota(jnp.int32, (1, patches), 1) < valid_ref[0]
        for group in range(heads // GROUP):
            members = range(group * GROUP, (group + 1) * GROUP)
            scores = []
            for head in members:
                first, offset = head_window(head)
                q = qkv_scr[:, first : first + WINDOW]
                k = qkv_scr[:, features + first : features + first + WINDOW]
                if picked:
                    q = dot(pick_ref[...], q).astype(BF)
                q = jnp.where((lane >= offset) & (lane < offset + HD), q, jnp.zeros_like(q))
                scores.append(
                    lax.dot_general(q, k, (((1,), (1,)), ((), ())), preferred_element_type=F32)
                )
            attended = []
            for head, score in zip(members, scores):
                first, _ = head_window(head)
                v = qkv_scr[:, 2 * features + first : 2 * features + first + WINDOW]
                score = jnp.where(live, score * HD ** (-0.5), -jnp.inf)
                weights = jnp.exp(score - jnp.max(score, axis=-1, keepdims=True))
                probs = (weights * (1.0 / jnp.sum(weights, axis=-1, keepdims=True))).astype(BF)
                attended.append(dot(probs, v).astype(BF))
            for side in range(2):
                tiles = [[] for _ in range(GROUP * 2 * HD // 128)]
                for head, att in zip(members, attended):
                    first, _, wide = spread_window(head)
                    spread = dot(att, spread_ref[2 * head + side, :, :wide])
                    for tile in range(wide // 128):
                        tiles[first // 128 + tile].append(spread[:, tile * 128 : tile * 128 + 128])
                for tile, parts in enumerate(tiles):
                    start = GROUP * 2 * HD * group + 128 * tile
                    att_scr[rows * side : rows * (side + 1), start : start + 128] = sum(
                        parts[1:], parts[0]
                    ).astype(BF)

    for layer in range(2):
        base = layer * BLOCKS
        picked = masked_last and layer == 1
        rows = ROWS if picked else patches
        source = x_ref if layer == 0 else x_scr
        h = normalize(source[...].astype(F32), gain_ref[layer : layer + 1, :]).astype(BF)
        for block in range(BLOCKS - 2):
            copies[base + block].wait()
            qkv_scr[:, block * BLOCK : (block + 1) * BLOCK] = dot(h, w_scr[base + block]).astype(BF)
        rest = 3 * features - (BLOCKS - 2) * BLOCK
        copies[base + BLOCKS - 2].wait()
        qkv_scr[:, 3 * features - rest :] = dot(h, w_scr[base + BLOCKS - 2, :, :rest]).astype(BF)
        attend(picked)
        target = out_ref if picked or (layer == 1 and not masked_last) else x_scr

        def finish(start, columns, weights):
            update = dot(att_scr[: 2 * rows, :], weights)
            for side in range(2):
                place = slice(side * features + start, side * features + start + columns)
                before = source[:, place]
                before = dot(pick_ref[...], before) if picked else before.astype(F32)
                target[:, place] = (before + update[rows * side : rows * (side + 1)]).astype(BF)

        finish(0, BLOCK - rest, w_scr[base + BLOCKS - 2, :, rest:])
        copies[base + BLOCKS - 1].wait()
        finish(BLOCK - rest, BLOCK, w_scr[base + BLOCKS - 1])


def sublayers(masked_last, valid, x, gains, pick, spread, packed):
    patches, width = x.shape
    features = width // 2
    out_rows = ROWS if masked_last else patches
    vmem = pl.BlockSpec(memory_space=pltpu.VMEM)
    return pl.pallas_call(
        functools.partial(sublayers_kernel, masked_last),
        in_specs=[
            pl.BlockSpec(memory_space=pltpu.SMEM),
            vmem,
            vmem,
            vmem,
            vmem,
            pl.BlockSpec(memory_space=pl.ANY),
        ],
        out_specs=vmem,
        out_shape=jax.ShapeDtypeStruct((out_rows, width), BF),
        scratch_shapes=[
            pltpu.VMEM((patches, width), BF),
            pltpu.VMEM((patches, 3 * features), BF),
            pltpu.VMEM((2 * patches, width), BF),
            pltpu.VMEM((2 * BLOCKS, width, BLOCK), BF),
            pltpu.SemaphoreType.DMA((2 * BLOCKS,)),
        ],
        compiler_params=pltpu.CompilerParams(vmem_limit_bytes=36 * 1024 * 1024),
        cost_estimate=pl.CostEstimate(
            flops=14 * 10**9, bytes_accessed=27 * 10**6, transcendentals=10**6
        ),
        name="sublayers",
    )(valid, x, gains, pick, spread, packed)


def backward_kernel(
    goal_ref, output_ref, weight_ref, down_ref, gate_ref, up_ref, normed_ref, top_ref, rest_ref, out_ref
):
    width = output_ref.shape[1]
    hidden_width = gate_ref.shape[1]
    goal = goal_ref[...].astype(F32)
    output = output_ref[...]
    out_scale = lax.rsqrt(jnp.mean(output * output, axis=-1, keepdims=True) + EPS)
    goal_scale = lax.rsqrt(jnp.mean(goal * goal, axis=-1, keepdims=True) + EPS)
    inner_prod = jnp.sum(output * goal, axis=-1, keepdims=True)
    factor = -LOSS_SCALE * weight_ref[...] * goal_scale / width
    cubed = out_scale * out_scale * out_scale
    upstream = factor * (out_scale * goal - (inner_prod * cubed / width) * output)
    upstream = upstream.astype(BF)
    start = 2 * hidden_width
    out_ref[:, start : start + width] = dot(top_ref[...], upstream).astype(BF)
    out_ref[:, start + width :] = dot(rest_ref[...], upstream).astype(BF)
    for first in range(0, hidden_width, BLOCK):
        last = min(first + BLOCK, hidden_width)
        back_hidden = lax.dot_general(
            upstream,
            down_ref[first:last, :],
            (((1,), (1,)), ((), ())),
            preferred_element_type=F32,
        )
        gate_grad = (back_hidden * gate_ref[:, first:last]).astype(BF)
        up_grad = (back_hidden * up_ref[:, first:last]).astype(BF)
        out_ref[:, first:last] = dot(normed_ref[...], gate_grad).astype(BF)
        out_ref[:, hidden_width + first : hidden_width + last] = dot(
            normed_ref[...], up_grad
        ).astype(BF)


def backward(goal, output, weights, w_down, gate_factor, up_factor, normed_rows, top, rest):
    vmem = pl.BlockSpec(memory_space=pltpu.VMEM)
    columns = 2 * gate_factor.shape[1] + 2 * output.shape[1]
    return pl.pallas_call(
        backward_kernel,
        in_specs=[vmem] * 9,
        out_specs=vmem,
        out_shape=jax.ShapeDtypeStruct((normed_rows.shape[0], columns), BF),
        compiler_params=pltpu.CompilerParams(vmem_limit_bytes=24 * 1024 * 1024),
        cost_estimate=pl.CostEstimate(flops=3 * 10**9, bytes_accessed=12 * 10**6, transcendentals=1000),
        name="backward",
    )(goal, output, weights, w_down, gate_factor, up_factor, normed_rows, top, rest)


def shards(
    teacher_in,
    teacher_qkv,
    teacher_out,
    teacher_gain,
    final_gain,
    projection,
    bucket,
    slot_image,
    mask_list,
    student_in,
    student_gain,
    w_gate,
    w_up,
    w_down,
):
    section = lax.axis_index("segment")
    column = lax.axis_index("dp")
    members = lax.axis_size("dp")
    images = bucket.shape[0]
    patches = teacher_in.shape[1]
    features = teacher_out.shape[2] // 2
    width = student_in.shape[-1]
    hidden_width = w_gate.shape[1]

    swap = [(0, 1), (1, 0), (2, 3), (3, 2)]
    upper = section % 2
    packed_own = jnp.concatenate(
        [
            teacher_qkv[0],
            jnp.concatenate([teacher_out[0, :, :features], teacher_out[0, :, features:]], axis=0),
        ],
        axis=1,
    )
    packed_other = lax.ppermute(packed_own, "segment", swap)
    lower_rows = jnp.where(upper == 0, packed_own, packed_other)
    upper_rows = jnp.where(upper == 0, packed_other, packed_own)
    packed = jnp.concatenate([lower_rows, upper_rows], axis=1)
    packed = lax.all_gather(packed, "dp", axis=0, tiled=True)
    other_gain = lax.ppermute(teacher_gain, "segment", swap)
    gains = jnp.where(
        upper == 0,
        jnp.concatenate([teacher_gain, other_gain], axis=0),
        jnp.concatenate([other_gain, teacher_gain], axis=0),
    )

    core = column % 2
    other_core = [(device, device ^ 1) for device in range(members)]

    def of_chip(own):
        other = lax.ppermute(own, "dp", other_core)
        first = jnp.where(core == 0, own, other)
        second = jnp.where(core == 0, other, own)
        return jnp.concatenate([first, second], axis=0)

    image_ids = jnp.arange(images, dtype=jnp.int32)
    positions = jnp.arange(patches, dtype=jnp.int32)
    slot_of = jnp.sum(
        jnp.where(slot_image[None, :] == image_ids[:, None], image_ids[None, :], 0), axis=1
    )
    listed = jnp.pad(mask_list, ((0, 0), (0, SENT_ROWS - mask_list.shape[1])))
    own_slots = lax.dynamic_slice_in_dim(listed, 2 * column, 2)
    own_pick = (own_slots[:, :, None] == positions[None, None, :]).astype(BF)
    chosen = jnp.einsum("srp,spf->srf", own_pick, student_in, preferred_element_type=F32).astype(BF)
    chosen = lax.all_to_all(chosen, "dp", split_axis=1, concat_axis=0, tiled=True)
    chosen = jnp.take(chosen, slot_of, axis=0)
    chosen = lax.all_to_all(chosen, "dp", split_axis=0, concat_axis=1, tiled=True)
    chosen = of_chip(chosen[:, :ROWS])
    my_slots = lax.dynamic_slice_in_dim(slot_of, 2 * column, 2)
    my_lists = jnp.take(listed[:, :ROWS], my_slots, axis=0)
    my_valid = valid_counts(lax.dynamic_slice_in_dim(bucket, 2 * column, 2))
    chip_count = 2 * valid_counts(lax.dynamic_slice_in_dim(bucket, 4 * (column // 2), 4)) // 5
    weights = jnp.where(
        jnp.arange(ROWS, dtype=jnp.int32)[None, :] < chip_count[:, None],
        1.0 / chip_count.astype(F32)[:, None],
        0.0,
    ).reshape(-1)

    flat_rows = chosen.reshape(-1, width)
    normed = normalize(flat_rows.astype(F32), student_gain).astype(BF)
    gate_act = dot(normed, w_gate)
    up_act = dot(normed, w_up)
    gate_sig = jax.nn.sigmoid(gate_act)
    hidden = (gate_act * gate_sig * up_act).astype(BF)
    output = flat_rows.astype(F32) + dot(hidden, w_down)
    gate_factor = up_act * gate_sig * (1.0 + gate_act * (1.0 - gate_sig))
    up_factor = gate_act * gate_sig

    chips = members // 2

    def own_rows(columns, count):
        rows = lax.dynamic_slice_in_dim(columns, section * count, count, 1).T
        rows = rows.reshape(chips, 2, count // members, -1)
        return lax.dynamic_index_in_dim(rows, core, 1, keepdims=False)

    normed_rows = own_rows(normed, width // 4).reshape(8 * chips, -1)
    down_rows = own_rows(hidden, hidden_width // 4)
    down_each = hidden_width // 4 // members
    down_top = down_rows[:, :8].reshape(8 * chips, -1)
    down_rest = jnp.pad(down_rows[:, 8:], ((0, 0), (0, 16 - down_each), (0, 0)))
    down_rest = down_rest.reshape(8 * chips, -1)
    spread = spread_matrices()

    which = jnp.where((section == 0) | (section == 3), 0, 1)
    image = lax.dynamic_index_in_dim(teacher_in, which, 0, keepdims=False)
    valid = lax.dynamic_slice_in_dim(my_valid, which, 1)
    my_list = lax.dynamic_index_in_dim(my_lists, which, 0, keepdims=False)
    pick = (my_list[:, None] == positions[None, :]).astype(BF)

    (
        packed, gains, image, valid, pick, spread,
        output, gate_factor, up_factor, normed_rows, down_top, down_rest, weights,
    ) = lax.optimization_barrier(
        (
            packed, gains, image, valid, pick, spread,
            output, gate_factor, up_factor, normed_rows, down_top, down_rest, weights,
        )
    )
    middle = sublayers(False, valid, image, gains, pick, spread, packed)
    middle = lax.ppermute(middle, "segment", [(0, 3), (1, 2)])
    packed, projection = lax.optimization_barrier((packed, projection))
    proj_full = lax.all_gather(projection, "dp", axis=0, tiled=True)
    last = sublayers(True, valid, middle, gains, pick, spread, packed)
    normed_last = normalize(last.astype(F32), final_gain).astype(BF)
    target = dot(normed_last, proj_full).astype(BF)

    swapped = lax.ppermute(target, "segment", [(2, 3), (3, 2)])
    near = lax.ppermute(target, "segment", [(3, 0), (2, 1)])
    far = lax.ppermute(target, "segment", [(3, 1), (2, 0)])
    upper_half = section >= 2
    one = jnp.where(upper_half, target, near)
    two = jnp.where(upper_half, swapped, far)
    goal = of_chip(jnp.where(which == 0, jnp.stack([one, two]), jnp.stack([two, one])))

    terms = backward(
        goal.reshape(-1, width), output, weights[:, None], w_down,
        gate_factor, up_factor, normed_rows, down_top, down_rest,
    ).reshape(chips, 8, -1)
    same_core = [list(range(0, members, 2)), list(range(1, members, 2))]
    terms = lax.all_to_all(
        terms, "dp", split_axis=0, concat_axis=0, tiled=True, axis_index_groups=same_core
    )
    summed = jnp.sum(terms.astype(F32), axis=0)
    cut = 2 * hidden_width
    grad_down = jnp.concatenate(
        [summed[:, cut : cut + width], summed[: down_each - 8, cut + width :]], axis=0
    )
    return summed[:, :hidden_width], summed[:, hidden_width:cut], grad_down


def solution(mesh):
    in_specs = (
        P("dp", None, None),
        P("segment", "dp", None),
        P("segment", "dp", None),
        P("segment", None),
        P(),
        P("dp", None),
        P(),
        P(),
        P(),
        P("dp", None, None),
        P(),
        P(),
        P(),
        P(),
    )
    out_specs = (P(("segment", "dp"), None), P(("segment", "dp"), None), P(("segment", "dp"), None))
    return jax.shard_map(shards, mesh=mesh, in_specs=in_specs, out_specs=out_specs, check_vma=False)
```

```python
import functools

import jax
import jax.numpy as jnp
from jax import lax
from jax.experimental import pallas as pl
from jax.experimental.pallas import tpu as pltpu
from jax.sharding import PartitionSpec as P

HD = 112
SIDE = 16
EPS = 1e-06
LOSS_SCALE = 4096.0

ROWS = 112
SENT_ROWS = 128
BLOCK = 512
BLOCKS = 7
WINDOW = 256
QUARTER = 28
GROUP = 4
BF = jnp.bfloat16
F32 = jnp.float32


def normalize(values_in, gain):
    centred = values_in - jnp.mean(values_in, axis=-1, keepdims=True)
    return centred * lax.rsqrt(jnp.mean(centred * centred, axis=-1, keepdims=True) + EPS) * gain


def valid_counts(bucket_ids):
    side_len = SIDE - 2 * bucket_ids
    return side_len * side_len


def head_window(head):
    first = head * HD // 128 * 128
    first = min(first, 8 * HD - WINDOW)
    return first, head * HD - first


def spread_window(head):
    start = 2 * HD * (head % GROUP)
    first = start // 128 * 128
    return first, start - first, -(-(start + 2 * HD - first) // 128) * 128


def spread_matrices():
    feature = jnp.arange(WINDOW, dtype=jnp.int32)[:, None]
    lane = jnp.arange(384, dtype=jnp.int32)[None, :]
    sides = []
    for head in range(8):
        _, offset = head_window(head)
        _, lane_offset, _ = spread_window(head)
        place = feature - offset
        owner = sum((place >= QUARTER * i).astype(jnp.int32) for i in range(1, GROUP))
        target = lane_offset + place + QUARTER * owner
        inside = (place >= 0) & (place < HD)
        for side in range(2):
            sides.append((inside & (lane == target + QUARTER * side)).astype(BF))
    return jnp.stack(sides)


def dot(a, b):
    return jnp.dot(a, b, preferred_element_type=F32)


def sublayers_kernel(
    masked_last, valid_ref, x_ref, gain_ref, pick_ref, spread_ref, w_hbm,
    out_ref, x_scr, qkv_scr, att_scr, w_scr, sems,
):
    patches, width = x_ref.shape
    features = width // 2
    heads = features // HD
    copies = [
        pltpu.make_async_copy(
            w_hbm.at[:, pl.ds(BLOCK * i, BLOCK)], w_scr.at[i], sems.at[i]
        )
        for i in range(2 * BLOCKS)
    ]
    for copy in copies:
        copy.start()

    def attend(picked):
        rows = ROWS if picked else patches
        lane = lax.broadcasted_iota(jnp.int32, (1, WINDOW), 1)
        live = lax.broadcasted_iota(jnp.int32, (1, patches), 1) < valid_ref[0]
        for group in range(heads // GROUP):
            members = range(group * GROUP, (group + 1) * GROUP)
            scores = []
            for head in members:
                first, offset = head_window(head)
                q = qkv_scr[:, first : first + WINDOW]
                k = qkv_scr[:, features + first : features + first + WINDOW]
                if picked:
                    q = dot(pick_ref[...], q).astype(BF)
                q = jnp.where((lane >= offset) & (lane < offset + HD), q, jnp.zeros_like(q))
                scores.append(
                    lax.dot_general(q, k, (((1,), (1,)), ((), ())), preferred_element_type=F32)
                )
            attended = []
            for head, score in zip(members, scores):
                first, _ = head_window(head)
                v = qkv_scr[:, 2 * features + first : 2 * features + first + WINDOW]
                score = jnp.where(live, score * HD ** (-0.5), -jnp.inf)
                weights = jnp.exp(score - jnp.max(score, axis=-1, keepdims=True))
                probs = (weights * (1.0 / jnp.sum(weights, axis=-1, keepdims=True))).astype(BF)
                attended.append(dot(probs, v).astype(BF))
            for side in range(2):
                tiles = [[] for _ in range(GROUP * 2 * HD // 128)]
                for head, att in zip(members, attended):
                    first, _, wide = spread_window(head)
                    spread = dot(att, spread_ref[2 * head + side, :, :wide])
                    for tile in range(wide // 128):
                        tiles[first // 128 + tile].append(spread[:, tile * 128 : tile * 128 + 128])
                for tile, parts in enumerate(tiles):
                    start = GROUP * 2 * HD * group + 128 * tile
                    att_scr[rows * side : rows * (side + 1), start : start + 128] = sum(
                        parts[1:], parts[0]
                    ).astype(BF)

    for layer in range(2):
        base = layer * BLOCKS
        picked = masked_last and layer == 1
        rows = ROWS if picked else patches
        source = x_ref if layer == 0 else x_scr
        h = normalize(source[...].astype(F32), gain_ref[layer : layer + 1, :]).astype(BF)
        for block in range(BLOCKS - 2):
            copies[base + block].wait()
            qkv_scr[:, block * BLOCK : (block + 1) * BLOCK] = dot(h, w_scr[base + block]).astype(BF)
        rest = 3 * features - (BLOCKS - 2) * BLOCK
        copies[base + BLOCKS - 2].wait()
        qkv_scr[:, 3 * features - rest :] = dot(h, w_scr[base + BLOCKS - 2, :, :rest]).astype(BF)
        attend(picked)
        target = out_ref if picked or (layer == 1 and not masked_last) else x_scr

        def finish(start, columns, weights):
            update = dot(att_scr[: 2 * rows, :], weights)
            for side in range(2):
                place = slice(side * features + start, side * features + start + columns)
                before = source[:, place]
                before = dot(pick_ref[...], before) if picked else before.astype(F32)
                target[:, place] = (before + update[rows * side : rows * (side + 1)]).astype(BF)

        finish(0, BLOCK - rest, w_scr[base + BLOCKS - 2, :, rest:])
        copies[base + BLOCKS - 1].wait()
        finish(BLOCK - rest, BLOCK, w_scr[base + BLOCKS - 1])


def sublayers(masked_last, valid, x, gains, pick, spread, packed):
    patches, width = x.shape
    features = width // 2
    out_rows = ROWS if masked_last else patches
    vmem = pl.BlockSpec(memory_space=pltpu.VMEM)
    return pl.pallas_call(
        functools.partial(sublayers_kernel, masked_last),
        in_specs=[
            pl.BlockSpec(memory_space=pltpu.SMEM),
            vmem,
            vmem,
            vmem,
            vmem,
            pl.BlockSpec(memory_space=pl.ANY),
        ],
        out_specs=vmem,
        out_shape=jax.ShapeDtypeStruct((out_rows, width), BF),
        scratch_shapes=[
            pltpu.VMEM((patches, width), BF),
            pltpu.VMEM((patches, 3 * features), BF),
            pltpu.VMEM((2 * patches, width), BF),
            pltpu.VMEM((2 * BLOCKS, width, BLOCK), BF),
            pltpu.SemaphoreType.DMA((2 * BLOCKS,)),
        ],
        compiler_params=pltpu.CompilerParams(vmem_limit_bytes=36 * 1024 * 1024),
        cost_estimate=pl.CostEstimate(
            flops=14 * 10**9, bytes_accessed=27 * 10**6, transcendentals=10**6
        ),
        name="sublayers",
    )(valid, x, gains, pick, spread, packed)


def backward_kernel(
    goal_ref, output_ref, weight_ref, down_ref, gate_ref, up_ref, normed_ref, top_ref, rest_ref, out_ref
):
    width = output_ref.shape[1]
    hidden_width = gate_ref.shape[1]
    goal = goal_ref[...].astype(F32)
    output = output_ref[...]
    out_scale = lax.rsqrt(jnp.mean(output * output, axis=-1, keepdims=True) + EPS)
    goal_scale = lax.rsqrt(jnp.mean(goal * goal, axis=-1, keepdims=True) + EPS)
    inner_prod = jnp.sum(output * goal, axis=-1, keepdims=True)
    factor = -LOSS_SCALE * weight_ref[...] * goal_scale / width
    cubed = out_scale * out_scale * out_scale
    upstream = factor * (out_scale * goal - (inner_prod * cubed / width) * output)
    upstream = upstream.astype(BF)
    start = 2 * hidden_width
    out_ref[:, start : start + width] = dot(top_ref[...], upstream).astype(BF)
    out_ref[:, start + width :] = dot(rest_ref[...], upstream).astype(BF)
    for first in range(0, hidden_width, BLOCK):
        last = min(first + BLOCK, hidden_width)
        back_hidden = lax.dot_general(
            upstream,
            down_ref[first:last, :],
            (((1,), (1,)), ((), ())),
            preferred_element_type=F32,
        )
        gate_grad = (back_hidden * gate_ref[:, first:last].astype(F32)).astype(BF)
        up_grad = (back_hidden * up_ref[:, first:last].astype(F32)).astype(BF)
        out_ref[:, first:last] = dot(normed_ref[...], gate_grad).astype(BF)
        out_ref[:, hidden_width + first : hidden_width + last] = dot(
            normed_ref[...], up_grad
        ).astype(BF)


def backward(goal, output, weights, w_down, gate_factor, up_factor, normed_rows, top, rest):
    vmem = pl.BlockSpec(memory_space=pltpu.VMEM)
    columns = 2 * gate_factor.shape[1] + 2 * output.shape[1]
    return pl.pallas_call(
        backward_kernel,
        in_specs=[vmem] * 9,
        out_specs=vmem,
        out_shape=jax.ShapeDtypeStruct((normed_rows.shape[0], columns), BF),
        compiler_params=pltpu.CompilerParams(vmem_limit_bytes=24 * 1024 * 1024),
        cost_estimate=pl.CostEstimate(flops=3 * 10**9, bytes_accessed=12 * 10**6, transcendentals=1000),
        name="backward",
    )(goal, output, weights, w_down, gate_factor, up_factor, normed_rows, top, rest)


def shards(
    teacher_in,
    teacher_qkv,
    teacher_out,
    teacher_gain,
    final_gain,
    projection,
    bucket,
    slot_image,
    mask_list,
    student_in,
    student_gain,
    w_gate,
    w_up,
    w_down,
):
    section = lax.axis_index("segment")
    column = lax.axis_index("dp")
    members = lax.axis_size("dp")
    images = bucket.shape[0]
    patches = teacher_in.shape[1]
    features = teacher_out.shape[2] // 2
    width = student_in.shape[-1]
    hidden_width = w_gate.shape[1]

    def both_layers(own):
        near = lax.ppermute(own, "segment", [(1, 0), (2, 3)])
        next_to = lax.ppermute(own, "segment", [(1, 2), (2, 1)])
        cut = own.shape[1] // 2
        across = []
        for part in (own[:, :cut], own[:, cut:]):
            part = lax.ppermute(part, "segment", [(0, 3), (3, 0)])
            across.append(lax.ppermute(part, "segment", [(3, 2), (0, 1)]))
        across = jnp.concatenate(across, axis=1)
        planes = [section == plane for plane in range(3)]
        lower = jnp.select(planes, [own, next_to, across], near)
        upper = jnp.select(planes, [near, across, next_to], own)
        return lower, upper

    packed = jnp.concatenate(
        [
            teacher_qkv[0],
            jnp.concatenate([teacher_out[0, :, :features], teacher_out[0, :, features:]], axis=0),
        ],
        axis=1,
    )
    packed = jnp.concatenate(both_layers(packed), axis=1)
    packed = lax.all_gather(packed, "dp", axis=0, tiled=True)
    gains = jnp.concatenate(both_layers(teacher_gain), axis=0)

    core = column % 2
    other_core = [(device, device ^ 1) for device in range(members)]

    def of_chip(own):
        other = lax.ppermute(own, "dp", other_core)
        first = jnp.where(core == 0, own, other)
        second = jnp.where(core == 0, other, own)
        return jnp.concatenate([first, second], axis=0)

    image_ids = jnp.arange(images, dtype=jnp.int32)
    positions = jnp.arange(patches, dtype=jnp.int32)
    slot_of = jnp.sum(
        jnp.where(slot_image[None, :] == image_ids[:, None], image_ids[None, :], 0), axis=1
    )
    listed = jnp.pad(mask_list, ((0, 0), (0, SENT_ROWS - mask_list.shape[1])))
    own_slots = lax.dynamic_slice_in_dim(listed, 2 * column, 2)
    own_pick = (own_slots[:, :, None] == positions[None, None, :]).astype(BF)
    chosen = jnp.einsum("srp,spf->srf", own_pick, student_in, preferred_element_type=F32).astype(BF)
    chosen = lax.all_to_all(chosen, "dp", split_axis=1, concat_axis=0, tiled=True)
    chosen = jnp.take(chosen, slot_of, axis=0)
    chosen = lax.all_to_all(chosen, "dp", split_axis=0, concat_axis=1, tiled=True)
    chosen = of_chip(chosen[:, :ROWS])
    my_slots = lax.dynamic_slice_in_dim(slot_of, 2 * column, 2)
    my_lists = jnp.take(listed[:, :ROWS], my_slots, axis=0)
    my_valid = valid_counts(lax.dynamic_slice_in_dim(bucket, 2 * column, 2))
    chip_count = 2 * valid_counts(lax.dynamic_slice_in_dim(bucket, 4 * (column // 2), 4)) // 5
    weights = jnp.where(
        jnp.arange(ROWS, dtype=jnp.int32)[None, :] < chip_count[:, None],
        1.0 / chip_count.astype(F32)[:, None],
        0.0,
    ).reshape(-1)

    flat_rows = chosen.reshape(-1, width)
    normed = normalize(flat_rows.astype(F32), student_gain).astype(BF)
    gate_act = dot(normed, w_gate)
    up_act = dot(normed, w_up)
    gate_sig = jax.nn.sigmoid(gate_act)
    hidden = (gate_act * gate_sig * up_act).astype(BF)
    output = flat_rows.astype(F32) + dot(hidden, w_down)
    gate_factor = (up_act * gate_sig * (1.0 + gate_act * (1.0 - gate_sig))).astype(BF)
    up_factor = (gate_act * gate_sig).astype(BF)

    chips = members // 2

    def own_rows(columns, count):
        rows = lax.dynamic_slice_in_dim(columns, section * count, count, 1).T
        rows = rows.reshape(chips, 2, count // members, -1)
        return lax.dynamic_index_in_dim(rows, core, 1, keepdims=False)

    normed_rows = own_rows(normed, width // 4).reshape(8 * chips, -1)
    down_rows = own_rows(hidden, hidden_width // 4)
    down_each = hidden_width // 4 // members
    down_top = down_rows[:, :8].reshape(8 * chips, -1)
    down_rest = jnp.pad(down_rows[:, 8:], ((0, 0), (0, 16 - down_each), (0, 0)))
    down_rest = down_rest.reshape(8 * chips, -1)
    spread = spread_matrices()

    which = jnp.select([section == 0, section == 1, section == 2], [0, core, 1], 1 - core)
    hop = []
    for device in range(members):
        same, other = device, 2 * members + device
        hop += [(same, (1 + 2 * (device % 2)) * members + device)]
        hop += [(other, (3 - 2 * (device % 2)) * members + device)]
    image = lax.dynamic_index_in_dim(teacher_in, which, 0, keepdims=False)
    valid = lax.dynamic_slice_in_dim(my_valid, which, 1)
    my_list = lax.dynamic_index_in_dim(my_lists, which, 0, keepdims=False)
    pick = (my_list[:, None] == positions[None, :]).astype(BF)

    (
        packed, gains, image, valid, pick, spread,
        output, gate_factor, up_factor, normed_rows, down_top, down_rest, weights,
    ) = lax.optimization_barrier(
        (
            packed, gains, image, valid, pick, spread,
            output, gate_factor, up_factor, normed_rows, down_top, down_rest, weights,
        )
    )
    middle = sublayers(False, valid, image, gains, pick, spread, packed)
    middle = lax.ppermute(middle, ("segment", "dp"), hop)
    packed, projection = lax.optimization_barrier((packed, projection))
    proj_full = lax.all_gather(projection, "dp", axis=0, tiled=True)
    last = sublayers(True, valid, middle, gains, pick, spread, packed)
    normed_last = normalize(last.astype(F32), final_gain).astype(BF)
    target = dot(normed_last, proj_full).astype(BF)

    first_way = lax.ppermute(target, "segment", [(1, 0), (3, 2)])
    second_way = lax.ppermute(target, "segment", [(3, 0), (1, 2)])
    swapped = lax.ppermute(target, "segment", [(1, 3), (3, 1)])
    planes = [section == plane for plane in range(3)]
    of_one = jnp.select(planes, [first_way, target, second_way], swapped)
    of_three = jnp.select(planes, [second_way, swapped, first_way], target)
    goal = jnp.where(core == 0, jnp.stack([of_one, of_three]), jnp.stack([of_three, of_one]))
    goal = of_chip(goal)

    terms = backward(
        goal.reshape(-1, width), output, weights[:, None], w_down,
        gate_factor, up_factor, normed_rows, down_top, down_rest,
    ).reshape(chips, 8, -1)
    same_core = [list(range(0, members, 2)), list(range(1, members, 2))]
    terms = lax.all_to_all(
        terms, "dp", split_axis=0, concat_axis=0, tiled=True, axis_index_groups=same_core
    )
    summed = jnp.sum(terms.astype(F32), axis=0)
    cut = 2 * hidden_width
    grad_down = jnp.concatenate(
        [summed[:, cut : cut + width], summed[: down_each - 8, cut + width :]], axis=0
    )
    return summed[:, :hidden_width], summed[:, hidden_width:cut], grad_down


def solution(mesh):
    in_specs = (
        P("dp", None, None),
        P("segment", "dp", None),
        P("segment", "dp", None),
        P("segment", None),
        P(),
        P("dp", None),
        P(),
        P(),
        P(),
        P("dp", None, None),
        P(),
        P(),
        P(),
        P(),
    )
    out_specs = (P(("segment", "dp"), None), P(("segment", "dp"), None), P(("segment", "dp"), None))
    return jax.shard_map(shards, mesh=mesh, in_specs=in_specs, out_specs=out_specs, check_vma=False)
```

```python
import functools

import jax
import jax.numpy as jnp
from jax import lax
from jax.experimental import pallas as pl
from jax.experimental.pallas import tpu as pltpu
from jax.sharding import PartitionSpec as P

HD = 112
SIDE = 16
EPS = 1e-06
LOSS_SCALE = 4096.0

ROWS = 112
SENT_ROWS = 128
BLOCK = 512
BLOCKS = 7
WINDOW = 256
QUARTER = 28
GROUP = 4
BF = jnp.bfloat16
F32 = jnp.float32


def normalize(values_in, gain):
    centred = values_in - jnp.mean(values_in, axis=-1, keepdims=True)
    return centred * lax.rsqrt(jnp.mean(centred * centred, axis=-1, keepdims=True) + EPS) * gain


def valid_counts(bucket_ids):
    side_len = SIDE - 2 * bucket_ids
    return side_len * side_len


def head_window(head):
    first = head * HD // 128 * 128
    first = min(first, 8 * HD - WINDOW)
    return first, head * HD - first


def spread_window(head):
    start = 2 * HD * (head % GROUP)
    first = start // 128 * 128
    return first, start - first, -(-(start + 2 * HD - first) // 128) * 128


def spread_matrices():
    feature = jnp.arange(WINDOW, dtype=jnp.int32)[:, None]
    lane = jnp.arange(384, dtype=jnp.int32)[None, :]
    sides = []
    for head in range(8):
        _, offset = head_window(head)
        _, lane_offset, _ = spread_window(head)
        place = feature - offset
        owner = sum((place >= QUARTER * i).astype(jnp.int32) for i in range(1, GROUP))
        target = lane_offset + place + QUARTER * owner
        inside = (place >= 0) & (place < HD)
        for side in range(2):
            sides.append((inside & (lane == target + QUARTER * side)).astype(BF))
    return jnp.stack(sides)


def dot(a, b):
    return jnp.dot(a, b, preferred_element_type=F32)


def sublayers_kernel(
    masked_last, valid_ref, x_ref, gain_ref, final_ref, pick_ref, spread_ref, w_hbm,
    out_ref, x_scr, qkv_scr, att_scr, w_scr, sems,
):
    patches, width = x_ref.shape
    features = width // 2
    heads = features // HD
    copies = [
        pltpu.make_async_copy(
            w_hbm.at[:, pl.ds(BLOCK * i, BLOCK)], w_scr.at[i], sems.at[i]
        )
        for i in range(2 * BLOCKS)
    ]
    for copy in copies:
        copy.start()

    def attend(picked):
        rows = ROWS if picked else patches
        lane = lax.broadcasted_iota(jnp.int32, (1, WINDOW), 1)
        live = lax.broadcasted_iota(jnp.int32, (1, patches), 1) < valid_ref[0]
        for group in range(heads // GROUP):
            members = range(group * GROUP, (group + 1) * GROUP)
            scores = []
            for head in members:
                first, offset = head_window(head)
                q = qkv_scr[:, first : first + WINDOW]
                k = qkv_scr[:, features + first : features + first + WINDOW]
                if picked:
                    q = dot(pick_ref[...], q).astype(BF)
                q = jnp.where((lane >= offset) & (lane < offset + HD), q, jnp.zeros_like(q))
                scores.append(
                    lax.dot_general(q, k, (((1,), (1,)), ((), ())), preferred_element_type=F32)
                )
            attended = []
            for head, score in zip(members, scores):
                first, _ = head_window(head)
                v = qkv_scr[:, 2 * features + first : 2 * features + first + WINDOW]
                score = jnp.where(live, score * HD ** (-0.5), -jnp.inf)
                weights = jnp.exp(score - jnp.max(score, axis=-1, keepdims=True))
                probs = (weights * (1.0 / jnp.sum(weights, axis=-1, keepdims=True))).astype(BF)
                attended.append(dot(probs, v).astype(BF))
            for side in range(2):
                tiles = [[] for _ in range(GROUP * 2 * HD // 128)]
                for head, att in zip(members, attended):
                    first, _, wide = spread_window(head)
                    spread = dot(att, spread_ref[2 * head + side, :, :wide])
                    for tile in range(wide // 128):
                        tiles[first // 128 + tile].append(spread[:, tile * 128 : tile * 128 + 128])
                for tile, parts in enumerate(tiles):
                    start = GROUP * 2 * HD * group + 128 * tile
                    att_scr[rows * side : rows * (side + 1), start : start + 128] = sum(
                        parts[1:], parts[0]
                    ).astype(BF)

    for layer in range(2):
        base = layer * BLOCKS
        picked = masked_last and layer == 1
        rows = ROWS if picked else patches
        source = x_ref if layer == 0 else x_scr
        h = normalize(source[...].astype(F32), gain_ref[layer : layer + 1, :]).astype(BF)
        for block in range(BLOCKS - 2):
            copies[base + block].wait()
            qkv_scr[:, block * BLOCK : (block + 1) * BLOCK] = dot(h, w_scr[base + block]).astype(BF)
        rest = 3 * features - (BLOCKS - 2) * BLOCK
        copies[base + BLOCKS - 2].wait()
        qkv_scr[:, 3 * features - rest :] = dot(h, w_scr[base + BLOCKS - 2, :, :rest]).astype(BF)
        attend(picked)
        target = out_ref if picked or (layer == 1 and not masked_last) else x_scr

        def finish(start, columns, weights):
            update = dot(att_scr[: 2 * rows, :], weights)
            for side in range(2):
                place = slice(side * features + start, side * features + start + columns)
                before = source[:, place]
                before = dot(pick_ref[...], before) if picked else before.astype(F32)
                target[:, place] = (before + update[rows * side : rows * (side + 1)]).astype(BF)

        finish(0, BLOCK - rest, w_scr[base + BLOCKS - 2, :, rest:])
        copies[base + BLOCKS - 1].wait()
        finish(BLOCK - rest, BLOCK, w_scr[base + BLOCKS - 1])

    if masked_last:
        out_ref[...] = normalize(out_ref[...].astype(F32), final_ref[...]).astype(BF)


def sublayers(masked_last, valid, x, gains, final_gain, pick, spread, packed):
    patches, width = x.shape
    features = width // 2
    out_rows = ROWS if masked_last else patches
    vmem = pl.BlockSpec(memory_space=pltpu.VMEM)
    return pl.pallas_call(
        functools.partial(sublayers_kernel, masked_last),
        in_specs=[
            pl.BlockSpec(memory_space=pltpu.SMEM),
            vmem,
            vmem,
            vmem,
            vmem,
            vmem,
            pl.BlockSpec(memory_space=pl.ANY),
        ],
        out_specs=vmem,
        out_shape=jax.ShapeDtypeStruct((out_rows, width), BF),
        scratch_shapes=[
            pltpu.VMEM((patches, width), BF),
            pltpu.VMEM((patches, 3 * features), BF),
            pltpu.VMEM((2 * patches, width), BF),
            pltpu.VMEM((2 * BLOCKS, width, BLOCK), BF),
            pltpu.SemaphoreType.DMA((2 * BLOCKS,)),
        ],
        compiler_params=pltpu.CompilerParams(vmem_limit_bytes=36 * 1024 * 1024),
        cost_estimate=pl.CostEstimate(
            flops=14 * 10**9, bytes_accessed=27 * 10**6, transcendentals=10**6
        ),
        name="sublayers",
    )(valid, x, gains, final_gain[None, :], pick, spread, packed)


def backward_kernel(
    own_goal_ref, other_goal_ref, output_ref, weight_ref, down_ref, gate_ref, up_ref, normed_ref, top_ref, rest_ref, out_ref
):
    width = output_ref.shape[1]
    hidden_width = gate_ref.shape[1]
    goal = jnp.concatenate([own_goal_ref[...], other_goal_ref[...]], axis=0).astype(F32)
    output = output_ref[...]
    out_scale = lax.rsqrt(jnp.mean(output * output, axis=-1, keepdims=True) + EPS)
    goal_scale = lax.rsqrt(jnp.mean(goal * goal, axis=-1, keepdims=True) + EPS)
    inner_prod = jnp.sum(output * goal, axis=-1, keepdims=True)
    factor = -LOSS_SCALE * weight_ref[...] * goal_scale / width
    cubed = out_scale * out_scale * out_scale
    upstream = factor * (out_scale * goal - (inner_prod * cubed / width) * output)
    upstream = upstream.astype(BF)
    start = 2 * hidden_width
    out_ref[:, start : start + width] = dot(top_ref[...], upstream).astype(BF)
    out_ref[:, start + width :] = dot(rest_ref[...], upstream).astype(BF)
    for first in range(0, hidden_width, BLOCK):
        last = min(first + BLOCK, hidden_width)
        back_hidden = lax.dot_general(
            upstream,
            down_ref[first:last, :],
            (((1,), (1,)), ((), ())),
            preferred_element_type=F32,
        )
        gate_grad = (back_hidden * gate_ref[:, first:last].astype(F32)).astype(BF)
        up_grad = (back_hidden * up_ref[:, first:last].astype(F32)).astype(BF)
        out_ref[:, first:last] = dot(normed_ref[...], gate_grad).astype(BF)
        out_ref[:, hidden_width + first : hidden_width + last] = dot(
            normed_ref[...], up_grad
        ).astype(BF)


def backward(own_goal, other_goal, output, weights, w_down, gate_factor, up_factor, normed_rows, top, rest):
    vmem = pl.BlockSpec(memory_space=pltpu.VMEM)
    columns = 2 * gate_factor.shape[1] + 2 * output.shape[1]
    return pl.pallas_call(
        backward_kernel,
        in_specs=[vmem] * 10,
        out_specs=vmem,
        out_shape=jax.ShapeDtypeStruct((normed_rows.shape[0], columns), BF),
        compiler_params=pltpu.CompilerParams(vmem_limit_bytes=24 * 1024 * 1024),
        cost_estimate=pl.CostEstimate(flops=3 * 10**9, bytes_accessed=12 * 10**6, transcendentals=1000),
        name="backward",
    )(own_goal, other_goal, output, weights, w_down, gate_factor, up_factor, normed_rows, top, rest)


def shards(
    teacher_in,
    teacher_qkv,
    teacher_out,
    teacher_gain,
    final_gain,
    projection,
    bucket,
    slot_image,
    mask_list,
    student_in,
    student_gain,
    w_gate,
    w_up,
    w_down,
):
    section = lax.axis_index("segment")
    column = lax.axis_index("dp")
    members = lax.axis_size("dp")
    images = bucket.shape[0]
    patches = teacher_in.shape[1]
    features = teacher_out.shape[2] // 2
    width = student_in.shape[-1]
    hidden_width = w_gate.shape[1]

    swap = [(0, 1), (1, 0), (2, 3), (3, 2)]
    upper = section % 2
    other_qkv = lax.ppermute(teacher_qkv[0], "segment", swap)
    other_out = lax.ppermute(teacher_out[0], "segment", swap)

    def columns(qkv, out):
        return [qkv, jnp.concatenate([out[:, :features], out[:, features:]], axis=0)]

    lower_out = jnp.where(upper == 0, teacher_out[0], other_out)
    upper_out = jnp.where(upper == 0, other_out, teacher_out[0])
    packed = jnp.concatenate(
        columns(jnp.where(upper == 0, teacher_qkv[0], other_qkv), lower_out)
        + columns(jnp.where(upper == 0, other_qkv, teacher_qkv[0]), upper_out),
        axis=1,
    )
    packed = lax.all_gather(packed, "dp", axis=0, tiled=True)
    other_gain = lax.ppermute(teacher_gain, "segment", swap)
    gains = jnp.where(
        upper == 0,
        jnp.concatenate([teacher_gain, other_gain], axis=0),
        jnp.concatenate([other_gain, teacher_gain], axis=0),
    )

    core = column % 2
    other_core = [(device, device ^ 1) for device in range(members)]

    def from_other_core(own):
        return lax.ppermute(own, "dp", other_core)

    image_ids = jnp.arange(images, dtype=jnp.int32)
    positions = jnp.arange(patches, dtype=jnp.int32)
    slot_of = jnp.sum(
        jnp.where(slot_image[None, :] == image_ids[:, None], image_ids[None, :], 0), axis=1
    )
    listed = jnp.pad(mask_list, ((0, 0), (0, SENT_ROWS - mask_list.shape[1])))
    own_slots = lax.dynamic_slice_in_dim(listed, 2 * column, 2)
    own_pick = (own_slots[:, :, None] == positions[None, None, :]).astype(BF)
    chosen = jnp.einsum("srp,spf->srf", own_pick, student_in, preferred_element_type=F32).astype(BF)
    chosen = lax.all_to_all(chosen, "dp", split_axis=1, concat_axis=0, tiled=True)
    chosen = jnp.take(chosen, slot_of, axis=0)
    chosen = lax.all_to_all(chosen, "dp", split_axis=0, concat_axis=1, tiled=True)
    chosen = chosen[:, :ROWS]
    chosen = jnp.concatenate([chosen, from_other_core(chosen)], axis=0)
    my_slots = lax.dynamic_slice_in_dim(slot_of, 2 * column, 2)
    my_lists = jnp.take(listed[:, :ROWS], my_slots, axis=0)
    my_valid = valid_counts(lax.dynamic_slice_in_dim(bucket, 2 * column, 2))
    other_bucket = lax.dynamic_slice_in_dim(bucket, 2 * (column + 1 - 2 * core), 2)
    chip_count = 2 * jnp.concatenate([my_valid, valid_counts(other_bucket)]) // 5
    weights = jnp.where(
        jnp.arange(ROWS, dtype=jnp.int32)[None, :] < chip_count[:, None],
        1.0 / chip_count.astype(F32)[:, None],
        0.0,
    ).reshape(-1)

    flat_rows = chosen.reshape(-1, width)
    normed = normalize(flat_rows.astype(F32), student_gain).astype(BF)
    gate_act = dot(normed, w_gate)
    up_act = dot(normed, w_up)
    gate_sig = jax.nn.sigmoid(gate_act)
    hidden = (gate_act * gate_sig * up_act).astype(BF)
    output = flat_rows.astype(F32) + dot(hidden, w_down)
    gate_factor = (up_act * gate_sig * (1.0 + gate_act * (1.0 - gate_sig))).astype(BF)
    up_factor = (gate_act * gate_sig).astype(BF)

    chips = members // 2

    def own_rows(columns, count):
        rows = lax.dynamic_slice_in_dim(columns, section * count, count, 1).T
        rows = rows.reshape(chips, 2, count // members, -1)
        return lax.dynamic_index_in_dim(rows, core, 1, keepdims=False)

    normed_rows = own_rows(normed, width // 4).reshape(8 * chips, -1)
    down_rows = own_rows(hidden, hidden_width // 4)
    down_each = hidden_width // 4 // members
    down_top = down_rows[:, :8].reshape(8 * chips, -1)
    down_rest = jnp.pad(down_rows[:, 8:], ((0, 0), (0, 16 - down_each), (0, 0)))
    down_rest = down_rest.reshape(8 * chips, -1)
    spread = spread_matrices()

    which = jnp.where((section == 0) | (section == 3), 0, 1)
    image = lax.dynamic_index_in_dim(teacher_in, which, 0, keepdims=False)
    valid = lax.dynamic_slice_in_dim(my_valid, which, 1)
    my_list = lax.dynamic_index_in_dim(my_lists, which, 0, keepdims=False)
    pick = (my_list[:, None] == positions[None, :]).astype(BF)

    (
        packed, gains, image, valid, pick, spread,
        output, gate_factor, up_factor, normed_rows, down_top, down_rest, weights,
    ) = lax.optimization_barrier(
        (
            packed, gains, image, valid, pick, spread,
            output, gate_factor, up_factor, normed_rows, down_top, down_rest, weights,
        )
    )
    middle = sublayers(False, valid, image, gains, final_gain, pick, spread, packed)
    middle = lax.ppermute(middle, "segment", [(0, 3), (1, 2)])
    packed, projection = lax.optimization_barrier((packed, projection))
    proj_full = lax.all_gather(projection, "dp", axis=0, tiled=True)
    normed_last = sublayers(True, valid, middle, gains, final_gain, pick, spread, packed)
    target = dot(normed_last, proj_full).astype(BF)

    swapped = lax.ppermute(target, "segment", [(2, 3), (3, 2)])
    near = lax.ppermute(target, "segment", [(3, 0), (2, 1)])
    far = lax.ppermute(target, "segment", [(3, 1), (2, 0)])
    upper_half = section >= 2
    one = jnp.where(upper_half, target, near)
    two = jnp.where(upper_half, swapped, far)
    goal = jnp.where(which == 0, jnp.stack([one, two]), jnp.stack([two, one]))
    other_goal = from_other_core(goal)

    terms = backward(
        goal.reshape(-1, width), other_goal.reshape(-1, width), output, weights[:, None], w_down,
        gate_factor, up_factor, normed_rows, down_top, down_rest,
    ).reshape(chips, 8, -1)
    same_core = [list(range(0, members, 2)), list(range(1, members, 2))]
    terms = lax.all_to_all(
        terms, "dp", split_axis=0, concat_axis=0, tiled=True, axis_index_groups=same_core
    )
    summed = jnp.sum(terms.astype(F32), axis=0)
    cut = 2 * hidden_width
    grad_down = jnp.concatenate(
        [summed[:, cut : cut + width], summed[: down_each - 8, cut + width :]], axis=0
    )
    return summed[:, :hidden_width], summed[:, hidden_width:cut], grad_down


def solution(mesh):
    in_specs = (
        P("dp", None, None),
        P("segment", "dp", None),
        P("segment", "dp", None),
        P("segment", None),
        P(),
        P("dp", None),
        P(),
        P(),
        P(),
        P("dp", None, None),
        P(),
        P(),
        P(),
        P(),
    )
    out_specs = (P(("segment", "dp"), None), P(("segment", "dp"), None), P(("segment", "dp"), None))
    return jax.shard_map(shards, mesh=mesh, in_specs=in_specs, out_specs=out_specs, check_vma=False)
```

```python
import functools

import jax
import jax.numpy as jnp
from jax import lax
from jax.experimental import pallas as pl
from jax.experimental.pallas import tpu as pltpu
from jax.sharding import PartitionSpec as P

HD = 112
SIDE = 16
EPS = 1e-06
LOSS_SCALE = 4096.0

ROWS = 112
SENT_ROWS = 128
BLOCK = 512
BLOCKS = 7
WINDOW = 256
QUARTER = 28
GROUP = 4
BF = jnp.bfloat16
F32 = jnp.float32


def normalize(values_in, gain):
    centred = values_in - jnp.mean(values_in, axis=-1, keepdims=True)
    return centred * lax.rsqrt(jnp.mean(centred * centred, axis=-1, keepdims=True) + EPS) * gain


def valid_counts(bucket_ids):
    side_len = SIDE - 2 * bucket_ids
    return side_len * side_len


def head_window(head):
    first = head * HD // 128 * 128
    first = min(first, 8 * HD - WINDOW)
    return first, head * HD - first


def spread_window(head):
    start = 2 * HD * (head % GROUP)
    first = start // 128 * 128
    return first, start - first, -(-(start + 2 * HD - first) // 128) * 128


def spread_matrices():
    feature = jnp.arange(WINDOW, dtype=jnp.int32)[:, None]
    lane = jnp.arange(384, dtype=jnp.int32)[None, :]
    sides = []
    for head in range(8):
        _, offset = head_window(head)
        _, lane_offset, _ = spread_window(head)
        place = feature - offset
        owner = sum((place >= QUARTER * i).astype(jnp.int32) for i in range(1, GROUP))
        target = lane_offset + place + QUARTER * owner
        inside = (place >= 0) & (place < HD)
        for side in range(2):
            sides.append((inside & (lane == target + QUARTER * side)).astype(BF))
    return jnp.stack(sides)


def dot(a, b):
    return jnp.dot(a, b, preferred_element_type=F32)


def sublayers_kernel(
    masked_last, valid_ref, x_ref, gain_ref, final_ref, pick_ref, spread_ref, w_hbm,
    out_ref, x_scr, qkv_scr, att_scr, w_scr, sems,
):
    patches, width = x_ref.shape
    features = width // 2
    heads = features // HD
    copies = [
        pltpu.make_async_copy(
            w_hbm.at[:, pl.ds(BLOCK * i, BLOCK)], w_scr.at[i], sems.at[i]
        )
        for i in range(2 * BLOCKS)
    ]
    for copy in copies:
        copy.start()

    def attend(picked):
        rows = ROWS if picked else patches
        lane = lax.broadcasted_iota(jnp.int32, (1, WINDOW), 1)
        live = lax.broadcasted_iota(jnp.int32, (1, patches), 1) < valid_ref[0]
        for group in range(heads // GROUP):
            members = range(group * GROUP, (group + 1) * GROUP)
            scores = []
            for head in members:
                first, offset = head_window(head)
                q = qkv_scr[:, first : first + WINDOW]
                k = qkv_scr[:, features + first : features + first + WINDOW]
                if picked:
                    q = dot(pick_ref[...], q).astype(BF)
                q = jnp.where((lane >= offset) & (lane < offset + HD), q, jnp.zeros_like(q))
                scores.append(
                    lax.dot_general(q, k, (((1,), (1,)), ((), ())), preferred_element_type=F32)
                )
            attended = []
            for head, score in zip(members, scores):
                first, _ = head_window(head)
                v = qkv_scr[:, 2 * features + first : 2 * features + first + WINDOW]
                score = jnp.where(live, score * HD ** (-0.5), -jnp.inf)
                weights = jnp.exp(score - jnp.max(score, axis=-1, keepdims=True))
                probs = (weights * (1.0 / jnp.sum(weights, axis=-1, keepdims=True))).astype(BF)
                attended.append(dot(probs, v).astype(BF))
            for side in range(2):
                tiles = [[] for _ in range(GROUP * 2 * HD // 128)]
                for head, att in zip(members, attended):
                    first, _, wide = spread_window(head)
                    spread = dot(att, spread_ref[2 * head + side, :, :wide])
                    for tile in range(wide // 128):
                        tiles[first // 128 + tile].append(spread[:, tile * 128 : tile * 128 + 128])
                for tile, parts in enumerate(tiles):
                    start = GROUP * 2 * HD * group + 128 * tile
                    att_scr[rows * side : rows * (side + 1), start : start + 128] = sum(
                        parts[1:], parts[0]
                    ).astype(BF)

    for layer in range(2):
        base = layer * BLOCKS
        picked = masked_last and layer == 1
        rows = ROWS if picked else patches
        source = x_ref if layer == 0 else x_scr
        h = normalize(source[...].astype(F32), gain_ref[layer : layer + 1, :]).astype(BF)
        for block in range(BLOCKS - 2):
            copies[base + block].wait()
            qkv_scr[:, block * BLOCK : (block + 1) * BLOCK] = dot(h, w_scr[base + block]).astype(BF)
        rest = 3 * features - (BLOCKS - 2) * BLOCK
        copies[base + BLOCKS - 2].wait()
        qkv_scr[:, 3 * features - rest :] = dot(h, w_scr[base + BLOCKS - 2, :, :rest]).astype(BF)
        attend(picked)
        target = out_ref if picked or (layer == 1 and not masked_last) else x_scr

        def finish(start, columns, weights):
            update = dot(att_scr[: 2 * rows, :], weights)
            for side in range(2):
                place = slice(side * features + start, side * features + start + columns)
                before = source[:, place]
                before = dot(pick_ref[...], before) if picked else before.astype(F32)
                target[:, place] = (before + update[rows * side : rows * (side + 1)]).astype(BF)

        finish(0, BLOCK - rest, w_scr[base + BLOCKS - 2, :, rest:])
        copies[base + BLOCKS - 1].wait()
        finish(BLOCK - rest, BLOCK, w_scr[base + BLOCKS - 1])

    if masked_last:
        out_ref[...] = normalize(out_ref[...].astype(F32), final_ref[...]).astype(BF)


def sublayers(masked_last, valid, x, gains, final_gain, pick, spread, packed):
    patches, width = x.shape
    features = width // 2
    out_rows = ROWS if masked_last else patches
    vmem = pl.BlockSpec(memory_space=pltpu.VMEM)
    return pl.pallas_call(
        functools.partial(sublayers_kernel, masked_last),
        in_specs=[
            pl.BlockSpec(memory_space=pltpu.SMEM),
            vmem,
            vmem,
            vmem,
            vmem,
            vmem,
            pl.BlockSpec(memory_space=pl.ANY),
        ],
        out_specs=vmem,
        out_shape=jax.ShapeDtypeStruct((out_rows, width), BF),
        scratch_shapes=[
            pltpu.VMEM((patches, width), BF),
            pltpu.VMEM((patches, 3 * features), BF),
            pltpu.VMEM((2 * patches, width), BF),
            pltpu.VMEM((2 * BLOCKS, width, BLOCK), BF),
            pltpu.SemaphoreType.DMA((2 * BLOCKS,)),
        ],
        compiler_params=pltpu.CompilerParams(vmem_limit_bytes=36 * 1024 * 1024),
        cost_estimate=pl.CostEstimate(
            flops=14 * 10**9, bytes_accessed=27 * 10**6, transcendentals=10**6
        ),
        name="sublayers",
    )(valid, x, gains, final_gain[None, :], pick, spread, packed)


def backward_kernel(
    own_goal_ref, other_goal_ref, output_hbm, weight_ref, down_hbm, gate_hbm, up_hbm,
    normed_ref, top_ref, rest_ref, out_ref, output_ref, gate_ref, up_ref, down_ref, sems,
):
    copies = [
        pltpu.make_async_copy(source, target, sems.at[i])
        for i, (source, target) in enumerate(
            [(output_hbm, output_ref), (down_hbm, down_ref), (gate_hbm, gate_ref), (up_hbm, up_ref)]
        )
    ]
    for copy in copies:
        copy.start()
    width = output_ref.shape[1]
    hidden_width = gate_ref.shape[1]
    goal = jnp.concatenate([own_goal_ref[...], other_goal_ref[...]], axis=0).astype(F32)
    copies[0].wait()
    output = output_ref[...]
    out_scale = lax.rsqrt(jnp.mean(output * output, axis=-1, keepdims=True) + EPS)
    goal_scale = lax.rsqrt(jnp.mean(goal * goal, axis=-1, keepdims=True) + EPS)
    inner_prod = jnp.sum(output * goal, axis=-1, keepdims=True)
    factor = -LOSS_SCALE * weight_ref[...] * goal_scale / width
    cubed = out_scale * out_scale * out_scale
    upstream = factor * (out_scale * goal - (inner_prod * cubed / width) * output)
    upstream = upstream.astype(BF)
    start = 2 * hidden_width
    out_ref[:, start : start + width] = dot(top_ref[...], upstream).astype(BF)
    out_ref[:, start + width :] = dot(rest_ref[...], upstream).astype(BF)
    for copy in copies[1:]:
        copy.wait()
    for first in range(0, hidden_width, BLOCK):
        last = min(first + BLOCK, hidden_width)
        back_hidden = lax.dot_general(
            upstream,
            down_ref[first:last, :],
            (((1,), (1,)), ((), ())),
            preferred_element_type=F32,
        )
        gate_grad = (back_hidden * gate_ref[:, first:last].astype(F32)).astype(BF)
        up_grad = (back_hidden * up_ref[:, first:last].astype(F32)).astype(BF)
        out_ref[:, first:last] = dot(normed_ref[...], gate_grad).astype(BF)
        out_ref[:, hidden_width + first : hidden_width + last] = dot(
            normed_ref[...], up_grad
        ).astype(BF)


def backward(own_goal, other_goal, output, weights, w_down, gate_factor, up_factor, normed_rows, top, rest):
    hbm = pl.BlockSpec(memory_space=pl.ANY)
    vmem = pl.BlockSpec(memory_space=pltpu.VMEM)
    columns = 2 * gate_factor.shape[1] + 2 * output.shape[1]
    return pl.pallas_call(
        backward_kernel,
        in_specs=[vmem, vmem, hbm, vmem, hbm, hbm, hbm, vmem, vmem, vmem],
        out_specs=vmem,
        out_shape=jax.ShapeDtypeStruct((normed_rows.shape[0], columns), BF),
        scratch_shapes=[
            pltpu.VMEM(output.shape, F32),
            pltpu.VMEM(gate_factor.shape, BF),
            pltpu.VMEM(up_factor.shape, BF),
            pltpu.VMEM(w_down.shape, BF),
            pltpu.SemaphoreType.DMA((4,)),
        ],
        compiler_params=pltpu.CompilerParams(vmem_limit_bytes=24 * 1024 * 1024),
        cost_estimate=pl.CostEstimate(flops=3 * 10**9, bytes_accessed=12 * 10**6, transcendentals=1000),
        name="backward",
    )(own_goal, other_goal, output, weights, w_down, gate_factor, up_factor, normed_rows, top, rest)


def shards(
    teacher_in,
    teacher_qkv,
    teacher_out,
    teacher_gain,
    final_gain,
    projection,
    bucket,
    slot_image,
    mask_list,
    student_in,
    student_gain,
    w_gate,
    w_up,
    w_down,
):
    section = lax.axis_index("segment")
    column = lax.axis_index("dp")
    members = lax.axis_size("dp")
    images = bucket.shape[0]
    patches = teacher_in.shape[1]
    features = teacher_out.shape[2] // 2
    width = student_in.shape[-1]
    hidden_width = w_gate.shape[1]

    swap = [(0, 1), (1, 0), (2, 3), (3, 2)]
    upper = section % 2
    other_qkv = lax.ppermute(teacher_qkv[0], "segment", swap)
    other_out = lax.ppermute(teacher_out[0], "segment", swap)

    def columns(qkv, out):
        return [qkv, jnp.concatenate([out[:, :features], out[:, features:]], axis=0)]

    lower_out = jnp.where(upper == 0, teacher_out[0], other_out)
    upper_out = jnp.where(upper == 0, other_out, teacher_out[0])
    packed = jnp.concatenate(
        columns(jnp.where(upper == 0, teacher_qkv[0], other_qkv), lower_out)
        + columns(jnp.where(upper == 0, other_qkv, teacher_qkv[0]), upper_out),
        axis=1,
    )
    packed = lax.all_gather(packed, "dp", axis=0, tiled=True)
    other_gain = lax.ppermute(teacher_gain, "segment", swap)
    gains = jnp.where(
        upper == 0,
        jnp.concatenate([teacher_gain, other_gain], axis=0),
        jnp.concatenate([other_gain, teacher_gain], axis=0),
    )

    core = column % 2
    other_core = [(device, device ^ 1) for device in range(members)]

    def from_other_core(own):
        return lax.ppermute(own, "dp", other_core)

    image_ids = jnp.arange(images, dtype=jnp.int32)
    positions = jnp.arange(patches, dtype=jnp.int32)
    slot_of = jnp.sum(
        jnp.where(slot_image[None, :] == image_ids[:, None], image_ids[None, :], 0), axis=1
    )
    listed = jnp.pad(mask_list, ((0, 0), (0, SENT_ROWS - mask_list.shape[1])))
    own_slots = lax.dynamic_slice_in_dim(listed, 2 * column, 2)
    own_pick = (own_slots[:, :, None] == positions[None, None, :]).astype(BF)
    chosen = jnp.einsum("srp,spf->srf", own_pick, student_in, preferred_element_type=F32).astype(BF)
    chosen = lax.all_to_all(chosen, "dp", split_axis=1, concat_axis=0, tiled=True)
    chosen = jnp.take(chosen, slot_of, axis=0)
    chosen = lax.all_to_all(chosen, "dp", split_axis=0, concat_axis=1, tiled=True)
    chosen = chosen[:, :ROWS]
    chosen = jnp.concatenate([chosen, from_other_core(chosen)], axis=0)
    my_slots = lax.dynamic_slice_in_dim(slot_of, 2 * column, 2)
    my_lists = jnp.take(listed[:, :ROWS], my_slots, axis=0)
    my_valid = valid_counts(lax.dynamic_slice_in_dim(bucket, 2 * column, 2))
    other_bucket = lax.dynamic_slice_in_dim(bucket, 2 * (column + 1 - 2 * core), 2)
    chip_count = 2 * jnp.concatenate([my_valid, valid_counts(other_bucket)]) // 5
    weights = jnp.where(
        jnp.arange(ROWS, dtype=jnp.int32)[None, :] < chip_count[:, None],
        1.0 / chip_count.astype(F32)[:, None],
        0.0,
    ).reshape(-1)

    flat_rows = chosen.reshape(-1, width)
    normed = normalize(flat_rows.astype(F32), student_gain).astype(BF)
    gate_act = dot(normed, w_gate)
    up_act = dot(normed, w_up)
    gate_sig = jax.nn.sigmoid(gate_act)
    hidden = (gate_act * gate_sig * up_act).astype(BF)
    output = flat_rows.astype(F32) + dot(hidden, w_down)
    gate_factor = (up_act * gate_sig * (1.0 + gate_act * (1.0 - gate_sig))).astype(BF)
    up_factor = (gate_act * gate_sig).astype(BF)

    chips = members // 2

    def own_rows(columns, count):
        rows = lax.dynamic_slice_in_dim(columns, section * count, count, 1).T
        rows = rows.reshape(chips, 2, count // members, -1)
        return lax.dynamic_index_in_dim(rows, core, 1, keepdims=False)

    normed_rows = own_rows(normed, width // 4).reshape(8 * chips, -1)
    down_rows = own_rows(hidden, hidden_width // 4)
    down_each = hidden_width // 4 // members
    down_top = down_rows[:, :8].reshape(8 * chips, -1)
    down_rest = jnp.pad(down_rows[:, 8:], ((0, 0), (0, 16 - down_each), (0, 0)))
    down_rest = down_rest.reshape(8 * chips, -1)
    spread = spread_matrices()

    which = jnp.where((section == 0) | (section == 3), 0, 1)
    image = lax.dynamic_index_in_dim(teacher_in, which, 0, keepdims=False)
    valid = lax.dynamic_slice_in_dim(my_valid, which, 1)
    my_list = lax.dynamic_index_in_dim(my_lists, which, 0, keepdims=False)
    pick = (my_list[:, None] == positions[None, :]).astype(BF)

    (
        packed, gains, image, valid, pick, spread,
        output, gate_factor, up_factor, normed_rows, down_top, down_rest, weights,
    ) = lax.optimization_barrier(
        (
            packed, gains, image, valid, pick, spread,
            output, gate_factor, up_factor, normed_rows, down_top, down_rest, weights,
        )
    )
    middle = sublayers(False, valid, image, gains, final_gain, pick, spread, packed)
    middle = lax.ppermute(middle, "segment", [(0, 3), (1, 2)])
    packed, projection = lax.optimization_barrier((packed, projection))
    proj_full = lax.all_gather(projection, "dp", axis=0, tiled=True)
    normed_last = sublayers(True, valid, middle, gains, final_gain, pick, spread, packed)
    target = dot(normed_last, proj_full).astype(BF)

    swapped = lax.ppermute(target, "segment", [(2, 3), (3, 2)])
    near = lax.ppermute(target, "segment", [(3, 0), (2, 1)])
    far = lax.ppermute(target, "segment", [(3, 1), (2, 0)])
    upper_half = section >= 2
    one = jnp.where(upper_half, target, near)
    two = jnp.where(upper_half, swapped, far)
    goal = jnp.where(which == 0, jnp.stack([one, two]), jnp.stack([two, one]))
    other_goal = from_other_core(goal)

    terms = backward(
        goal.reshape(-1, width), other_goal.reshape(-1, width), output, weights[:, None], w_down,
        gate_factor, up_factor, normed_rows, down_top, down_rest,
    ).reshape(chips, 8, -1)
    same_core = [list(range(0, members, 2)), list(range(1, members, 2))]
    terms = lax.all_to_all(
        terms, "dp", split_axis=0, concat_axis=0, tiled=True, axis_index_groups=same_core
    )
    summed = jnp.sum(terms.astype(F32), axis=0)
    cut = 2 * hidden_width
    grad_down = jnp.concatenate(
        [summed[:, cut : cut + width], summed[: down_each - 8, cut + width :]], axis=0
    )
    return summed[:, :hidden_width], summed[:, hidden_width:cut], grad_down


def solution(mesh):
    in_specs = (
        P("dp", None, None),
        P("segment", "dp", None),
        P("segment", "dp", None),
        P("segment", None),
        P(),
        P("dp", None),
        P(),
        P(),
        P(),
        P("dp", None, None),
        P(),
        P(),
        P(),
        P(),
    )
    out_specs = (P(("segment", "dp"), None), P(("segment", "dp"), None), P(("segment", "dp"), None))
    return jax.shard_map(shards, mesh=mesh, in_specs=in_specs, out_specs=out_specs, check_vma=False)
```

```python
import functools

import jax
import jax.numpy as jnp
from jax import lax
from jax.experimental import pallas as pl
from jax.experimental.pallas import tpu as pltpu
from jax.sharding import PartitionSpec as P

HD = 112
SIDE = 16
EPS = 1e-06
LOSS_SCALE = 4096.0

ROWS = 112
SENT_ROWS = 128
BLOCK = 512
BLOCKS = 7
SLOTS = 10
WINDOW = 256
QUARTER = 28
GROUP = 4
BF = jnp.bfloat16
F32 = jnp.float32


def normalize(values_in, gain):
    centred = values_in - jnp.mean(values_in, axis=-1, keepdims=True)
    return centred * lax.rsqrt(jnp.mean(centred * centred, axis=-1, keepdims=True) + EPS) * gain


def valid_counts(bucket_ids):
    side_len = SIDE - 2 * bucket_ids
    return side_len * side_len


def head_window(head):
    first = head * HD // 128 * 128
    first = min(first, 8 * HD - WINDOW)
    return first, head * HD - first


def spread_window(head):
    start = 2 * HD * (head % GROUP)
    first = start // 128 * 128
    return first, start - first, -(-(start + 2 * HD - first) // 128) * 128


def spread_matrices():
    feature = jnp.arange(WINDOW, dtype=jnp.int32)[:, None]
    lane = jnp.arange(384, dtype=jnp.int32)[None, :]
    sides = []
    for head in range(8):
        _, offset = head_window(head)
        _, lane_offset, _ = spread_window(head)
        place = feature - offset
        owner = sum((place >= QUARTER * i).astype(jnp.int32) for i in range(1, GROUP))
        target = lane_offset + place + QUARTER * owner
        inside = (place >= 0) & (place < HD)
        for side in range(2):
            sides.append((inside & (lane == target + QUARTER * side)).astype(BF))
    return jnp.stack(sides)


def dot(a, b):
    return jnp.dot(a, b, preferred_element_type=F32)


def sublayers_kernel(
    masked_last, valid_ref, x_ref, gain_ref, final_ref, pick_ref, spread_ref, w_hbm,
    out_ref, x_scr, qkv_scr, att_scr, w_scr, sems,
):
    patches, width = x_ref.shape
    features = width // 2
    heads = features // HD
    copies = [
        pltpu.make_async_copy(
            w_hbm.at[:, pl.ds(BLOCK * i, BLOCK)], w_scr.at[i % SLOTS], sems.at[i]
        )
        for i in range(2 * BLOCKS)
    ]
    for copy in copies[:SLOTS]:
        copy.start()

    def attend(picked):
        rows = ROWS if picked else patches
        lane = lax.broadcasted_iota(jnp.int32, (1, WINDOW), 1)
        live = lax.broadcasted_iota(jnp.int32, (1, patches), 1) < valid_ref[0]
        for group in range(heads // GROUP):
            members = range(group * GROUP, (group + 1) * GROUP)
            scores = []
            for head in members:
                first, offset = head_window(head)
                q = qkv_scr[:, first : first + WINDOW]
                k = qkv_scr[:, features + first : features + first + WINDOW]
                if picked:
                    q = dot(pick_ref[...], q).astype(BF)
                q = jnp.where((lane >= offset) & (lane < offset + HD), q, jnp.zeros_like(q))
                scores.append(
                    lax.dot_general(q, k, (((1,), (1,)), ((), ())), preferred_element_type=F32)
                )
            attended = []
            for head, score in zip(members, scores):
                first, _ = head_window(head)
                v = qkv_scr[:, 2 * features + first : 2 * features + first + WINDOW]
                score = jnp.where(live, score * HD ** (-0.5), -jnp.inf)
                weights = jnp.exp(score - jnp.max(score, axis=-1, keepdims=True))
                probs = (weights * (1.0 / jnp.sum(weights, axis=-1, keepdims=True))).astype(BF)
                attended.append(dot(probs, v).astype(BF))
            for side in range(2):
                tiles = [[] for _ in range(GROUP * 2 * HD // 128)]
                for head, att in zip(members, attended):
                    first, _, wide = spread_window(head)
                    spread = dot(att, spread_ref[2 * head + side, :, :wide])
                    for tile in range(wide // 128):
                        tiles[first // 128 + tile].append(spread[:, tile * 128 : tile * 128 + 128])
                for tile, parts in enumerate(tiles):
                    start = GROUP * 2 * HD * group + 128 * tile
                    att_scr[rows * side : rows * (side + 1), start : start + 128] = sum(
                        parts[1:], parts[0]
                    ).astype(BF)

    for layer in range(2):
        base = layer * BLOCKS
        picked = masked_last and layer == 1
        rows = ROWS if picked else patches
        source = x_ref if layer == 0 else x_scr
        h = normalize(source[...].astype(F32), gain_ref[layer : layer + 1, :]).astype(BF)
        for block in range(BLOCKS - 2):
            copies[base + block].wait()
            qkv_scr[:, block * BLOCK : (block + 1) * BLOCK] = dot(h, w_scr[(base + block) % SLOTS]).astype(BF)
        rest = 3 * features - (BLOCKS - 2) * BLOCK
        copies[base + BLOCKS - 2].wait()
        qkv_scr[:, 3 * features - rest :] = dot(h, w_scr[(base + BLOCKS - 2) % SLOTS, :, :rest]).astype(BF)
        if layer == 0:
            for copy in copies[SLOTS:]:
                copy.start()
        attend(picked)
        target = out_ref if picked or (layer == 1 and not masked_last) else x_scr

        def finish(start, columns, weights):
            update = dot(att_scr[: 2 * rows, :], weights)
            for side in range(2):
                place = slice(side * features + start, side * features + start + columns)
                before = source[:, place]
                before = dot(pick_ref[...], before) if picked else before.astype(F32)
                target[:, place] = (before + update[rows * side : rows * (side + 1)]).astype(BF)

        finish(0, BLOCK - rest, w_scr[(base + BLOCKS - 2) % SLOTS, :, rest:])
        copies[base + BLOCKS - 1].wait()
        finish(BLOCK - rest, BLOCK, w_scr[(base + BLOCKS - 1) % SLOTS])

    if masked_last:
        out_ref[...] = normalize(out_ref[...].astype(F32), final_ref[...]).astype(BF)


def sublayers(masked_last, valid, x, gains, final_gain, pick, spread, packed):
    patches, width = x.shape
    features = width // 2
    out_rows = ROWS if masked_last else patches
    vmem = pl.BlockSpec(memory_space=pltpu.VMEM)
    return pl.pallas_call(
        functools.partial(sublayers_kernel, masked_last),
        in_specs=[
            pl.BlockSpec(memory_space=pltpu.SMEM),
            vmem,
            vmem,
            vmem,
            vmem,
            vmem,
            pl.BlockSpec(memory_space=pl.ANY),
        ],
        out_specs=vmem,
        out_shape=jax.ShapeDtypeStruct((out_rows, width), BF),
        scratch_shapes=[
            pltpu.VMEM((patches, width), BF),
            pltpu.VMEM((patches, 3 * features), BF),
            pltpu.VMEM((2 * patches, width), BF),
            pltpu.VMEM((SLOTS, width, BLOCK), BF),
            pltpu.SemaphoreType.DMA((2 * BLOCKS,)),
        ],
        compiler_params=pltpu.CompilerParams(vmem_limit_bytes=30 * 1024 * 1024),
        cost_estimate=pl.CostEstimate(
            flops=14 * 10**9, bytes_accessed=27 * 10**6, transcendentals=10**6
        ),
        name="sublayers",
    )(valid, x, gains, final_gain[None, :], pick, spread, packed)


def backward_kernel(
    own_goal_ref, other_goal_ref, output_ref, weight_ref, down_ref, gate_ref, up_ref, normed_ref, top_ref, rest_ref, out_ref
):
    width = output_ref.shape[1]
    hidden_width = gate_ref.shape[1]
    goal = jnp.concatenate([own_goal_ref[...], other_goal_ref[...]], axis=0).astype(F32)
    output = output_ref[...]
    out_scale = lax.rsqrt(jnp.mean(output * output, axis=-1, keepdims=True) + EPS)
    goal_scale = lax.rsqrt(jnp.mean(goal * goal, axis=-1, keepdims=True) + EPS)
    inner_prod = jnp.sum(output * goal, axis=-1, keepdims=True)
    factor = -LOSS_SCALE * weight_ref[...] * goal_scale / width
    cubed = out_scale * out_scale * out_scale
    upstream = factor * (out_scale * goal - (inner_prod * cubed / width) * output)
    upstream = upstream.astype(BF)
    start = 2 * hidden_width
    out_ref[:, start : start + width] = dot(top_ref[...], upstream).astype(BF)
    out_ref[:, start + width :] = dot(rest_ref[...], upstream).astype(BF)
    for first in range(0, hidden_width, BLOCK):
        last = min(first + BLOCK, hidden_width)
        back_hidden = lax.dot_general(
            upstream,
            down_ref[first:last, :],
            (((1,), (1,)), ((), ())),
            preferred_element_type=F32,
        )
        gate_grad = (back_hidden * gate_ref[:, first:last].astype(F32)).astype(BF)
        up_grad = (back_hidden * up_ref[:, first:last].astype(F32)).astype(BF)
        out_ref[:, first:last] = dot(normed_ref[...], gate_grad).astype(BF)
        out_ref[:, hidden_width + first : hidden_width + last] = dot(
            normed_ref[...], up_grad
        ).astype(BF)


def backward(own_goal, other_goal, output, weights, w_down, gate_factor, up_factor, normed_rows, top, rest):
    vmem = pl.BlockSpec(memory_space=pltpu.VMEM)
    columns = 2 * gate_factor.shape[1] + 2 * output.shape[1]
    return pl.pallas_call(
        backward_kernel,
        in_specs=[vmem] * 10,
        out_specs=vmem,
        out_shape=jax.ShapeDtypeStruct((normed_rows.shape[0], columns), BF),
        compiler_params=pltpu.CompilerParams(vmem_limit_bytes=24 * 1024 * 1024),
        cost_estimate=pl.CostEstimate(flops=3 * 10**9, bytes_accessed=12 * 10**6, transcendentals=1000),
        name="backward",
    )(own_goal, other_goal, output, weights, w_down, gate_factor, up_factor, normed_rows, top, rest)


def shards(
    teacher_in,
    teacher_qkv,
    teacher_out,
    teacher_gain,
    final_gain,
    projection,
    bucket,
    slot_image,
    mask_list,
    student_in,
    student_gain,
    w_gate,
    w_up,
    w_down,
):
    section = lax.axis_index("segment")
    column = lax.axis_index("dp")
    members = lax.axis_size("dp")
    images = bucket.shape[0]
    patches = teacher_in.shape[1]
    features = teacher_out.shape[2] // 2
    width = student_in.shape[-1]
    hidden_width = w_gate.shape[1]

    swap = [(0, 1), (1, 0), (2, 3), (3, 2)]
    upper = section % 2
    other_qkv = lax.ppermute(teacher_qkv[0], "segment", swap)
    other_out = lax.ppermute(teacher_out[0], "segment", swap)

    def columns(qkv, out):
        return [qkv, jnp.concatenate([out[:, :features], out[:, features:]], axis=0)]

    lower_out = jnp.where(upper == 0, teacher_out[0], other_out)
    upper_out = jnp.where(upper == 0, other_out, teacher_out[0])
    packed = jnp.concatenate(
        columns(jnp.where(upper == 0, teacher_qkv[0], other_qkv), lower_out)
        + columns(jnp.where(upper == 0, other_qkv, teacher_qkv[0]), upper_out),
        axis=1,
    )
    packed = lax.all_gather(packed, "dp", axis=0, tiled=True)
    other_gain = lax.ppermute(teacher_gain, "segment", swap)
    gains = jnp.where(
        upper == 0,
        jnp.concatenate([teacher_gain, other_gain], axis=0),
        jnp.concatenate([other_gain, teacher_gain], axis=0),
    )

    core = column % 2
    other_core = [(device, device ^ 1) for device in range(members)]

    def from_other_core(own):
        return lax.ppermute(own, "dp", other_core)

    image_ids = jnp.arange(images, dtype=jnp.int32)
    positions = jnp.arange(patches, dtype=jnp.int32)
    slot_of = jnp.sum(
        jnp.where(slot_image[None, :] == image_ids[:, None], image_ids[None, :], 0), axis=1
    )
    listed = jnp.pad(mask_list, ((0, 0), (0, SENT_ROWS - mask_list.shape[1])))
    own_slots = lax.dynamic_slice_in_dim(listed, 2 * column, 2)
    own_pick = (own_slots[:, :, None] == positions[None, None, :]).astype(BF)
    chosen = jnp.einsum("srp,spf->srf", own_pick, student_in, preferred_element_type=F32).astype(BF)
    chosen = lax.all_to_all(chosen, "dp", split_axis=1, concat_axis=0, tiled=True)
    chosen = jnp.take(chosen, slot_of, axis=0)
    chosen = lax.all_to_all(chosen, "dp", split_axis=0, concat_axis=1, tiled=True)
    chosen = chosen[:, :ROWS]
    chosen = jnp.concatenate([chosen, from_other_core(chosen)], axis=0)
    my_slots = lax.dynamic_slice_in_dim(slot_of, 2 * column, 2)
    my_lists = jnp.take(listed[:, :ROWS], my_slots, axis=0)
    my_valid = valid_counts(lax.dynamic_slice_in_dim(bucket, 2 * column, 2))
    other_bucket = lax.dynamic_slice_in_dim(bucket, 2 * (column + 1 - 2 * core), 2)
    chip_count = 2 * jnp.concatenate([my_valid, valid_counts(other_bucket)]) // 5
    weights = jnp.where(
        jnp.arange(ROWS, dtype=jnp.int32)[None, :] < chip_count[:, None],
        1.0 / chip_count.astype(F32)[:, None],
        0.0,
    ).reshape(-1)

    flat_rows = chosen.reshape(-1, width)
    normed = normalize(flat_rows.astype(F32), student_gain).astype(BF)
    gate_act = dot(normed, w_gate)
    up_act = dot(normed, w_up)
    gate_sig = jax.nn.sigmoid(gate_act)
    hidden = (gate_act * gate_sig * up_act).astype(BF)
    output = flat_rows.astype(F32) + dot(hidden, w_down)
    gate_factor = (up_act * gate_sig * (1.0 + gate_act * (1.0 - gate_sig))).astype(BF)
    up_factor = (gate_act * gate_sig).astype(BF)

    chips = members // 2

    def own_rows(columns, count):
        rows = lax.dynamic_slice_in_dim(columns, section * count, count, 1).T
        rows = rows.reshape(chips, 2, count // members, -1)
        return lax.dynamic_index_in_dim(rows, core, 1, keepdims=False)

    normed_rows = own_rows(normed, width // 4).reshape(8 * chips, -1)
    down_rows = own_rows(hidden, hidden_width // 4)
    down_each = hidden_width // 4 // members
    down_top = down_rows[:, :8].reshape(8 * chips, -1)
    down_rest = jnp.pad(down_rows[:, 8:], ((0, 0), (0, 16 - down_each), (0, 0)))
    down_rest = down_rest.reshape(8 * chips, -1)
    spread = spread_matrices()

    which = jnp.where((section == 0) | (section == 3), 0, 1)
    image = lax.dynamic_index_in_dim(teacher_in, which, 0, keepdims=False)
    valid = lax.dynamic_slice_in_dim(my_valid, which, 1)
    my_list = lax.dynamic_index_in_dim(my_lists, which, 0, keepdims=False)
    pick = (my_list[:, None] == positions[None, :]).astype(BF)

    (
        packed, gains, image, valid, pick, spread,
        output, gate_factor, up_factor, normed_rows, down_top, down_rest, weights,
    ) = lax.optimization_barrier(
        (
            packed, gains, image, valid, pick, spread,
            output, gate_factor, up_factor, normed_rows, down_top, down_rest, weights,
        )
    )
    middle = sublayers(False, valid, image, gains, final_gain, pick, spread, packed)
    middle = lax.ppermute(middle, "segment", [(0, 3), (1, 2)])
    packed, projection = lax.optimization_barrier((packed, projection))
    proj_full = lax.all_gather(projection, "dp", axis=0, tiled=True)
    normed_last = sublayers(True, valid, middle, gains, final_gain, pick, spread, packed)
    target = dot(normed_last, proj_full).astype(BF)

    swapped = lax.ppermute(target, "segment", [(2, 3), (3, 2)])
    near = lax.ppermute(target, "segment", [(3, 0), (2, 1)])
    far = lax.ppermute(target, "segment", [(3, 1), (2, 0)])
    upper_half = section >= 2
    one = jnp.where(upper_half, target, near)
    two = jnp.where(upper_half, swapped, far)
    goal = jnp.where(which == 0, jnp.stack([one, two]), jnp.stack([two, one]))
    other_goal = from_other_core(goal)

    terms = backward(
        goal.reshape(-1, width), other_goal.reshape(-1, width), output, weights[:, None], w_down,
        gate_factor, up_factor, normed_rows, down_top, down_rest,
    ).reshape(chips, 8, -1)
    same_core = [list(range(0, members, 2)), list(range(1, members, 2))]
    terms = lax.all_to_all(
        terms, "dp", split_axis=0, concat_axis=0, tiled=True, axis_index_groups=same_core
    )
    summed = jnp.sum(terms.astype(F32), axis=0)
    cut = 2 * hidden_width
    grad_down = jnp.concatenate(
        [summed[:, cut : cut + width], summed[: down_each - 8, cut + width :]], axis=0
    )
    return summed[:, :hidden_width], summed[:, hidden_width:cut], grad_down


def solution(mesh):
    in_specs = (
        P("dp", None, None),
        P("segment", "dp", None),
        P("segment", "dp", None),
        P("segment", None),
        P(),
        P("dp", None),
        P(),
        P(),
        P(),
        P("dp", None, None),
        P(),
        P(),
        P(),
        P(),
    )
    out_specs = (P(("segment", "dp"), None), P(("segment", "dp"), None), P(("segment", "dp"), None))
    return jax.shard_map(shards, mesh=mesh, in_specs=in_specs, out_specs=out_specs, check_vma=False)
```

```python
import functools

import jax
import jax.numpy as jnp
from jax import lax
from jax.experimental import pallas as pl
from jax.experimental.pallas import tpu as pltpu
from jax.sharding import PartitionSpec as P

HD = 112
SIDE = 16
EPS = 1e-06
LOSS_SCALE = 4096.0

ROWS = 112
SENT_ROWS = 128
BLOCK = 512
BLOCKS = 7
SLOTS = 10
WINDOW = 256
QUARTER = 28
GROUP = 4
BF = jnp.bfloat16
F32 = jnp.float32


def normalize(values_in, gain):
    centred = values_in - jnp.mean(values_in, axis=-1, keepdims=True)
    return centred * lax.rsqrt(jnp.mean(centred * centred, axis=-1, keepdims=True) + EPS) * gain


def valid_counts(bucket_ids):
    side_len = SIDE - 2 * bucket_ids
    return side_len * side_len


def head_window(head):
    first = head * HD // 128 * 128
    first = min(first, 8 * HD - WINDOW)
    return first, head * HD - first


def spread_window(head):
    start = 2 * HD * (head % GROUP)
    first = start // 128 * 128
    return first, start - first, -(-(start + 2 * HD - first) // 128) * 128


def spread_matrices():
    feature = jnp.arange(WINDOW, dtype=jnp.int32)[:, None]
    lane = jnp.arange(384, dtype=jnp.int32)[None, :]
    sides = []
    for head in range(8):
        _, offset = head_window(head)
        _, lane_offset, _ = spread_window(head)
        place = feature - offset
        owner = sum((place >= QUARTER * i).astype(jnp.int32) for i in range(1, GROUP))
        target = lane_offset + place + QUARTER * owner
        inside = (place >= 0) & (place < HD)
        for side in range(2):
            sides.append((inside & (lane == target + QUARTER * side)).astype(BF))
    return jnp.stack(sides)


def dot(a, b):
    return jnp.dot(a, b, preferred_element_type=F32)


def sublayers_kernel(
    masked_last, valid_ref, x_ref, gain_ref, final_ref, pick_ref, spread_ref, w_hbm,
    out_ref, x_scr, qkv_scr, att_scr, w_scr, sems,
):
    patches, width = x_ref.shape
    features = width // 2
    heads = features // HD
    copies = [
        pltpu.make_async_copy(
            w_hbm.at[:, pl.ds(BLOCK * i, BLOCK)], w_scr.at[i % SLOTS], sems.at[i]
        )
        for i in range(2 * BLOCKS)
    ]
    for copy in copies[:SLOTS]:
        copy.start()

    def attend(picked):
        rows = ROWS if picked else patches
        lane = lax.broadcasted_iota(jnp.int32, (1, WINDOW), 1)
        live = lax.broadcasted_iota(jnp.int32, (1, patches), 1) < valid_ref[0]
        for group in range(heads // GROUP):
            members = range(group * GROUP, (group + 1) * GROUP)
            scores = []
            for head in members:
                first, offset = head_window(head)
                q = qkv_scr[:, first : first + WINDOW]
                k = qkv_scr[:, features + first : features + first + WINDOW]
                if picked:
                    q = dot(pick_ref[...], q).astype(BF)
                q = jnp.where((lane >= offset) & (lane < offset + HD), q, jnp.zeros_like(q))
                scores.append(
                    lax.dot_general(q, k, (((1,), (1,)), ((), ())), preferred_element_type=F32)
                )
            attended = []
            for head, score in zip(members, scores):
                first, _ = head_window(head)
                v = qkv_scr[:, 2 * features + first : 2 * features + first + WINDOW]
                score = jnp.where(live, score * HD ** (-0.5), -jnp.inf)
                weights = jnp.exp(score - jnp.max(score, axis=-1, keepdims=True))
                probs = (weights * (1.0 / jnp.sum(weights, axis=-1, keepdims=True))).astype(BF)
                attended.append(dot(probs, v).astype(BF))
            for side in range(2):
                tiles = [[] for _ in range(GROUP * 2 * HD // 128)]
                for head, att in zip(members, attended):
                    first, _, wide = spread_window(head)
                    spread = dot(att, spread_ref[2 * head + side, :, :wide])
                    for tile in range(wide // 128):
                        tiles[first // 128 + tile].append(spread[:, tile * 128 : tile * 128 + 128])
                for tile, parts in enumerate(tiles):
                    start = GROUP * 2 * HD * group + 128 * tile
                    att_scr[rows * side : rows * (side + 1), start : start + 128] = sum(
                        parts[1:], parts[0]
                    ).astype(BF)

    for layer in range(2):
        base = layer * BLOCKS
        picked = masked_last and layer == 1
        rows = ROWS if picked else patches
        source = x_ref if layer == 0 else x_scr
        h = normalize(source[...].astype(F32), gain_ref[layer : layer + 1, :]).astype(BF)
        for block in range(BLOCKS - 2):
            copies[base + block].wait()
            qkv_scr[:, block * BLOCK : (block + 1) * BLOCK] = dot(h, w_scr[(base + block) % SLOTS]).astype(BF)
        rest = 3 * features - (BLOCKS - 2) * BLOCK
        copies[base + BLOCKS - 2].wait()
        qkv_scr[:, 3 * features - rest :] = dot(h, w_scr[(base + BLOCKS - 2) % SLOTS, :, :rest]).astype(BF)
        if layer == 0:
            for copy in copies[SLOTS:]:
                copy.start()
        attend(picked)
        target = out_ref if picked or (layer == 1 and not masked_last) else x_scr

        def finish(start, columns, weights):
            update = dot(att_scr[: 2 * rows, :], weights)
            for side in range(2):
                place = slice(side * features + start, side * features + start + columns)
                before = source[:, place]
                before = dot(pick_ref[...], before) if picked else before.astype(F32)
                target[:, place] = (before + update[rows * side : rows * (side + 1)]).astype(BF)

        finish(0, BLOCK - rest, w_scr[(base + BLOCKS - 2) % SLOTS, :, rest:])
        copies[base + BLOCKS - 1].wait()
        finish(BLOCK - rest, BLOCK, w_scr[(base + BLOCKS - 1) % SLOTS])

    if masked_last:
        out_ref[...] = normalize(out_ref[...].astype(F32), final_ref[...]).astype(BF)


def sublayers(masked_last, valid, x, gains, final_gain, pick, spread, packed):
    patches, width = x.shape
    features = width // 2
    out_rows = ROWS if masked_last else patches
    vmem = pl.BlockSpec(memory_space=pltpu.VMEM)
    return pl.pallas_call(
        functools.partial(sublayers_kernel, masked_last),
        in_specs=[
            pl.BlockSpec(memory_space=pltpu.SMEM),
            vmem,
            vmem,
            vmem,
            vmem,
            vmem,
            pl.BlockSpec(memory_space=pl.ANY),
        ],
        out_specs=vmem,
        out_shape=jax.ShapeDtypeStruct((out_rows, width), BF),
        scratch_shapes=[
            pltpu.VMEM((patches, width), BF),
            pltpu.VMEM((patches, 3 * features), BF),
            pltpu.VMEM((2 * patches, width), BF),
            pltpu.VMEM((SLOTS, width, BLOCK), BF),
            pltpu.SemaphoreType.DMA((2 * BLOCKS,)),
        ],
        compiler_params=pltpu.CompilerParams(vmem_limit_bytes=30 * 1024 * 1024),
        cost_estimate=pl.CostEstimate(
            flops=14 * 10**9, bytes_accessed=27 * 10**6, transcendentals=10**6
        ),
        name="sublayers",
    )(valid, x, gains, final_gain[None, :], pick, spread, packed)


def backward_kernel(
    own_goal_ref, other_goal_ref, output_ref, weight_ref, down_ref, gate_ref, up_ref, normed_ref, top_ref, rest_ref, out_ref
):
    width = output_ref.shape[1]
    hidden_width = gate_ref.shape[1]
    goal = jnp.concatenate([own_goal_ref[...], other_goal_ref[...]], axis=0).astype(F32)
    output = output_ref[...]
    out_scale = lax.rsqrt(jnp.mean(output * output, axis=-1, keepdims=True) + EPS)
    goal_scale = lax.rsqrt(jnp.mean(goal * goal, axis=-1, keepdims=True) + EPS)
    inner_prod = jnp.sum(output * goal, axis=-1, keepdims=True)
    factor = -LOSS_SCALE * weight_ref[...] * goal_scale / width
    cubed = out_scale * out_scale * out_scale
    upstream = factor * (out_scale * goal - (inner_prod * cubed / width) * output)
    upstream = upstream.astype(BF)
    start = 2 * hidden_width
    out_ref[:, start : start + width] = dot(top_ref[...], upstream).astype(BF)
    out_ref[:, start + width :] = dot(rest_ref[...], upstream).astype(BF)
    for first in range(0, hidden_width, BLOCK):
        last = min(first + BLOCK, hidden_width)
        back_hidden = lax.dot_general(
            upstream,
            down_ref[first:last, :],
            (((1,), (1,)), ((), ())),
            preferred_element_type=F32,
        )
        gate_grad = (back_hidden * gate_ref[:, first:last]).astype(BF)
        up_grad = (back_hidden * up_ref[:, first:last]).astype(BF)
        out_ref[:, first:last] = dot(normed_ref[...], gate_grad).astype(BF)
        out_ref[:, hidden_width + first : hidden_width + last] = dot(
            normed_ref[...], up_grad
        ).astype(BF)


def backward(own_goal, other_goal, output, weights, w_down, gate_factor, up_factor, normed_rows, top, rest):
    vmem = pl.BlockSpec(memory_space=pltpu.VMEM)
    columns = 2 * gate_factor.shape[1] + 2 * output.shape[1]
    return pl.pallas_call(
        backward_kernel,
        in_specs=[vmem] * 10,
        out_specs=vmem,
        out_shape=jax.ShapeDtypeStruct((normed_rows.shape[0], columns), BF),
        compiler_params=pltpu.CompilerParams(vmem_limit_bytes=24 * 1024 * 1024),
        cost_estimate=pl.CostEstimate(flops=3 * 10**9, bytes_accessed=12 * 10**6, transcendentals=1000),
        name="backward",
    )(own_goal, other_goal, output, weights, w_down, gate_factor, up_factor, normed_rows, top, rest)


def shards(
    teacher_in,
    teacher_qkv,
    teacher_out,
    teacher_gain,
    final_gain,
    projection,
    bucket,
    slot_image,
    mask_list,
    student_in,
    student_gain,
    w_gate,
    w_up,
    w_down,
):
    section = lax.axis_index("segment")
    column = lax.axis_index("dp")
    members = lax.axis_size("dp")
    images = bucket.shape[0]
    patches = teacher_in.shape[1]
    features = teacher_out.shape[2] // 2
    width = student_in.shape[-1]
    hidden_width = w_gate.shape[1]

    swap = [(0, 1), (1, 0), (2, 3), (3, 2)]
    upper = section % 2
    other_qkv = lax.ppermute(teacher_qkv[0], "segment", swap)
    other_out = lax.ppermute(teacher_out[0], "segment", swap)

    def columns(qkv, out):
        return [qkv, jnp.concatenate([out[:, :features], out[:, features:]], axis=0)]

    lower_out = jnp.where(upper == 0, teacher_out[0], other_out)
    upper_out = jnp.where(upper == 0, other_out, teacher_out[0])
    packed = jnp.concatenate(
        columns(jnp.where(upper == 0, teacher_qkv[0], other_qkv), lower_out)
        + columns(jnp.where(upper == 0, other_qkv, teacher_qkv[0]), upper_out),
        axis=1,
    )
    packed = lax.all_gather(packed, "dp", axis=0, tiled=True)
    other_gain = lax.ppermute(teacher_gain, "segment", swap)
    gains = jnp.where(
        upper == 0,
        jnp.concatenate([teacher_gain, other_gain], axis=0),
        jnp.concatenate([other_gain, teacher_gain], axis=0),
    )

    core = column % 2
    other_core = [(device, device ^ 1) for device in range(members)]

    def from_other_core(own):
        return lax.ppermute(own, "dp", other_core)

    image_ids = jnp.arange(images, dtype=jnp.int32)
    positions = jnp.arange(patches, dtype=jnp.int32)
    slot_of = jnp.sum(
        jnp.where(slot_image[None, :] == image_ids[:, None], image_ids[None, :], 0), axis=1
    )
    listed = jnp.pad(mask_list, ((0, 0), (0, SENT_ROWS - mask_list.shape[1])))
    own_slots = lax.dynamic_slice_in_dim(listed, 2 * column, 2)
    own_pick = (own_slots[:, :, None] == positions[None, None, :]).astype(BF)
    chosen = jnp.einsum("srp,spf->srf", own_pick, student_in, preferred_element_type=F32).astype(BF)
    chosen = lax.all_to_all(chosen, "dp", split_axis=1, concat_axis=0, tiled=True)
    chosen = jnp.take(chosen, slot_of, axis=0)
    chosen = lax.all_to_all(chosen, "dp", split_axis=0, concat_axis=1, tiled=True)
    chosen = chosen[:, :ROWS]
    chosen = jnp.concatenate([chosen, from_other_core(chosen)], axis=0)
    my_slots = lax.dynamic_slice_in_dim(slot_of, 2 * column, 2)
    my_lists = jnp.take(listed[:, :ROWS], my_slots, axis=0)
    my_valid = valid_counts(lax.dynamic_slice_in_dim(bucket, 2 * column, 2))
    other_bucket = lax.dynamic_slice_in_dim(bucket, 2 * (column + 1 - 2 * core), 2)
    chip_count = 2 * jnp.concatenate([my_valid, valid_counts(other_bucket)]) // 5
    weights = jnp.where(
        jnp.arange(ROWS, dtype=jnp.int32)[None, :] < chip_count[:, None],
        1.0 / chip_count.astype(F32)[:, None],
        0.0,
    ).reshape(-1)

    flat_rows = chosen.reshape(-1, width)
    normed = normalize(flat_rows.astype(F32), student_gain).astype(BF)
    gate_act = dot(normed, w_gate)
    up_act = dot(normed, w_up)
    gate_sig = jax.nn.sigmoid(gate_act)
    hidden = (gate_act * gate_sig * up_act).astype(BF)
    added = dot(hidden, w_down)
    gate_factor = (up_act * gate_sig * (1.0 + gate_act * (1.0 - gate_sig))).astype(BF)
    up_factor = (gate_act * gate_sig).astype(BF)

    chips = members // 2

    def own_rows(columns, count):
        rows = lax.dynamic_slice_in_dim(columns, section * count, count, 1).T
        rows = rows.reshape(chips, 2, count // members, -1)
        return lax.dynamic_index_in_dim(rows, core, 1, keepdims=False)

    normed_rows = own_rows(normed, width // 4).reshape(8 * chips, -1)
    down_rows = own_rows(hidden, hidden_width // 4)
    down_each = hidden_width // 4 // members
    down_top = down_rows[:, :8].reshape(8 * chips, -1)
    down_rest = jnp.pad(down_rows[:, 8:], ((0, 0), (0, 16 - down_each), (0, 0)))
    down_rest = down_rest.reshape(8 * chips, -1)
    spread = spread_matrices()

    which = jnp.where((section == 0) | (section == 3), 0, 1)
    image = lax.dynamic_index_in_dim(teacher_in, which, 0, keepdims=False)
    valid = lax.dynamic_slice_in_dim(my_valid, which, 1)
    my_list = lax.dynamic_index_in_dim(my_lists, which, 0, keepdims=False)
    pick = (my_list[:, None] == positions[None, :]).astype(BF)

    (
        packed, gains, image, valid, pick, spread,
        added, flat_rows, gate_factor, up_factor, normed_rows, down_top, down_rest, weights,
    ) = lax.optimization_barrier(
        (
            packed, gains, image, valid, pick, spread,
            added, flat_rows, gate_factor, up_factor, normed_rows, down_top, down_rest, weights,
        )
    )
    middle = sublayers(False, valid, image, gains, final_gain, pick, spread, packed)
    middle = lax.ppermute(middle, "segment", [(0, 3), (1, 2)])
    packed, projection = lax.optimization_barrier((packed, projection))
    proj_full = lax.all_gather(projection, "dp", axis=0, tiled=True)
    normed_last = sublayers(True, valid, middle, gains, final_gain, pick, spread, packed)
    target = dot(normed_last, proj_full).astype(BF)

    target, added, flat_rows, gate_factor, up_factor = lax.optimization_barrier(
        (target, added, flat_rows, gate_factor, up_factor)
    )
    output = flat_rows.astype(F32) + added
    gate_factor, up_factor = gate_factor.astype(F32), up_factor.astype(F32)

    swapped = lax.ppermute(target, "segment", [(2, 3), (3, 2)])
    near = lax.ppermute(target, "segment", [(3, 0), (2, 1)])
    far = lax.ppermute(target, "segment", [(3, 1), (2, 0)])
    upper_half = section >= 2
    one = jnp.where(upper_half, target, near)
    two = jnp.where(upper_half, swapped, far)
    goal = jnp.where(which == 0, jnp.stack([one, two]), jnp.stack([two, one]))
    other_goal = from_other_core(goal)

    terms = backward(
        goal.reshape(-1, width), other_goal.reshape(-1, width), output, weights[:, None], w_down,
        gate_factor, up_factor, normed_rows, down_top, down_rest,
    ).reshape(chips, 8, -1)
    same_core = [list(range(0, members, 2)), list(range(1, members, 2))]
    terms = lax.all_to_all(
        terms, "dp", split_axis=0, concat_axis=0, tiled=True, axis_index_groups=same_core
    )
    summed = jnp.sum(terms.astype(F32), axis=0)
    cut = 2 * hidden_width
    grad_down = jnp.concatenate(
        [summed[:, cut : cut + width], summed[: down_each - 8, cut + width :]], axis=0
    )
    return summed[:, :hidden_width], summed[:, hidden_width:cut], grad_down


def solution(mesh):
    in_specs = (
        P("dp", None, None),
        P("segment", "dp", None),
        P("segment", "dp", None),
        P("segment", None),
        P(),
        P("dp", None),
        P(),
        P(),
        P(),
        P("dp", None, None),
        P(),
        P(),
        P(),
        P(),
    )
    out_specs = (P(("segment", "dp"), None), P(("segment", "dp"), None), P(("segment", "dp"), None))
    return jax.shard_map(shards, mesh=mesh, in_specs=in_specs, out_specs=out_specs, check_vma=False)
```
